512 devices in a mesh: grp: 16 (over y, core), seq: 32 (over z, x).
Axes of the slice: x: 4, y: 8, z: 8, core: 2. Of those that a mesh axis runs over, the one named last changes fastest.
Arguments:
- queries: bfloat16 [16, 4096, 4096], P('grp', 'seq'), may hold values from -6 to 6
- keys_values: bfloat16 [16, 4096, 1024], P('grp', 'seq'), may hold values from -6 to 6
- route_group: int32 [16, 4096], P('grp', 'seq'), may hold values from 0 to 15, as said below
- route_slot: int32 [16, 4096], P('grp', 'seq'), may hold values from 0 to 127, as said below
- doc_lengths: int32 [16, 2, 3], P('grp'), may hold values from 1 to 1024, 2048 in all within a row
Outputs:
- attn_out: bfloat16 [16, 4096, 4096], P('grp', 'seq')
The draws below stay inside these ranges and needn't reach their ends.
Inputs may be any that keep to these rules, and one draw needn't show every extreme that they name: `route_group`: A row keeps its position index s along seq. For each s, every packed row receives exactly 128 rows in all; from one generator device at most 16 rows go to one packed row, and for every s and every packed row exactly one generator device sends exactly 16. `route_slot`: the rows that reach one device (same packed row, same s) have distinct places.
All inputs are finite; a program needn't handle non-finite values.
Results may differ from the reference program's by a relative error of at most 0.004.
Values may be sent and summed in bfloat16 or wider, within the bound.
A program may use at most 128 MiB of HBM per device.

```python
import math
import jax
import jax.numpy as jnp
import numpy as np
from jax import lax

HQ = 32
HK = 4
HD = 128
NDOC = 3
TOK_DEV = 128
GROUPS = 16
SEQ_TOK = 4096
HALF = 2048
CAP = 16
N_SEQ = 32


def route_tables(key):
    key = jax.random.fold_in(key, 101)
    column_keys = jax.random.split(key, N_SEQ)
    sources = jnp.arange(GROUPS, dtype=jnp.int32)

    def one_column(column_key):
        weight_key, order_key = jax.random.split(column_key)
        ranking = jax.random.permutation(weight_key, GROUPS)
        weights = jnp.where(ranking == 0, CAP, jnp.where(ranking == 1, 0, CAP // 2)).astype(jnp.int32)
        counts = weights[(sources[None, :] - sources[:, None]) % GROUPS]

        def one_source(counts_row, source_key):
            listing = jnp.repeat(sources, counts_row, total_repeat_length=TOK_DEV)
            return listing[jax.random.permutation(source_key, TOK_DEV)]
        targets = jax.vmap(one_source)(counts, jax.random.split(order_key, GROUPS))
        hits = (targets[:, :, None] == sources[None, None, :]).astype(jnp.int32)
        ranks = jnp.sum((jnp.cumsum(hits, axis=1) - hits) * hits, axis=2)
        offsets = jnp.cumsum(counts, axis=0) - counts
        slots = jnp.take_along_axis(offsets, targets, axis=1) + ranks
        return (targets, slots)
    targets, slots = jax.vmap(one_column)(column_keys)
    targets = jnp.transpose(targets, (1, 0, 2)).reshape(GROUPS, SEQ_TOK)
    slots = jnp.transpose(slots, (1, 0, 2)).reshape(GROUPS, SEQ_TOK)
    return (targets.astype(jnp.int32), slots.astype(jnp.int32))


def draw_route_group(key, part):
    targets, slots = route_tables(key)
    return targets


def draw_route_slot(key, part):
    targets, slots = route_tables(key)
    return slots


def draw_queries(key, part):
    key = jax.random.fold_in(key, 1)
    base = jnp.clip(jax.random.normal(key, (GROUPS, SEQ_TOK, HQ * HD), jnp.float32), -6.0, 6.0)
    return base.astype(jnp.bfloat16)


def draw_keys_values(key, part):
    key = jax.random.fold_in(key, 2)
    base = jnp.clip(jax.random.normal(key, (GROUPS, SEQ_TOK, 2 * HK * HD), jnp.float32), -6.0, 6.0)
    return base.astype(jnp.bfloat16)


def profile(amount, total, reach, slope):
    loads = [(1 << 20) // math.isqrt(standing ** slope) + 1 for standing in range(2, amount + 1)]
    surplus, given = total - reach - (amount - 1), [1] * (amount - 1)
    while surplus > 0:
        movable = [i for i in range(amount - 1) if given[i] < reach]
        whole, budget = sum([loads[i] for i in movable]), surplus
        for i in movable:
            more = min(reach - given[i], max(1, budget * loads[i] // whole), surplus)
            given[i] = given[i] + more
            surplus = surplus - more
    return np.array([reach] + given)


def ragged_sizes(own_key, number_of, total, reach, slope):
    if number_of == 2:
        one = jax.random.randint(own_key, (), max(1, total - reach), min(reach, total - 1) + 1)
        return jnp.stack([one, total - one])
    sizes = jnp.asarray(profile(number_of, total, reach, slope), jnp.int32)
    twos = (number_of - 1) // 2
    source_of, receiver = sizes[1:1 + 2 * twos:2], sizes[2:2 + 2 * twos:2]
    slack = jnp.minimum(source_of - 1, reach - receiver)
    shifted = jax.random.randint(jax.random.fold_in(own_key, 1), (twos,), 0, 1 << 20) % (slack + 1)
    sizes = sizes.at[1:1 + 2 * twos:2].set(source_of - shifted).at[2:2 + 2 * twos:2].set(receiver + shifted)
    return sizes[jax.random.permutation(jax.random.fold_in(own_key, 2), number_of)]


def setup_inputs(seed: int = 0) -> dict:
    key_of = jax.random.split(jax.random.key(seed), 6)
    return {
        "queries": draw_queries(jax.random.fold_in(key_of[5], 71), 0),
        "keys_values": draw_keys_values(jax.random.fold_in(key_of[5], 71), 0),
        "route_group": draw_route_group(jax.random.fold_in(key_of[5], 71), 0),
        "route_slot": draw_route_slot(jax.random.fold_in(key_of[5], 71), 0),
        "doc_lengths": jax.vmap(lambda own: ragged_sizes(own, NDOC, HALF, HALF // 2, 2))(jax.random.split(key_of[4], GROUPS * 2)).reshape((GROUPS, 2, NDOC)).astype(jnp.int32),
    }


NEGATIVE = -1.0e30


def document_index(lengths, positions):
    bounds = jnp.cumsum(lengths)
    return jnp.sum((positions[:, None] >= bounds[None, :]).astype(jnp.int32), axis=1)


def to_trainers(matrix, route_group, route_slot):
    columns = jnp.arange(SEQ_TOK, dtype=jnp.int32)
    target = route_group * SEQ_TOK + (columns // TOK_DEV * TOK_DEV)[None, :] + route_slot
    width = matrix.shape[-1]
    flat = matrix.reshape(GROUPS * SEQ_TOK, width)
    placed = jnp.zeros_like(flat).at[target.reshape(-1).astype(jnp.int32)].set(flat)
    return placed.reshape(GROUPS, SEQ_TOK, width)


def attend_group(operands):
    queries, keys_values, lengths = operands
    block = min(512, SEQ_TOK)
    grouping = HQ // HK
    scale = HD ** -0.5
    heads_query = queries.reshape(SEQ_TOK, HQ, HD).astype(jnp.float32)
    keys = jnp.repeat(keys_values[:, :HK * HD].reshape(SEQ_TOK, HK, HD), grouping, axis=1).astype(jnp.float32)
    values = jnp.repeat(keys_values[:, HK * HD:].reshape(SEQ_TOK, HK, HD), grouping, axis=1).astype(jnp.float32)
    positions = jnp.arange(SEQ_TOK, dtype=jnp.int32)
    documents = document_index(lengths.reshape(-1), positions)

    def one_block(index):
        first = (index * block).astype(jnp.int32)
        query_block = lax.dynamic_slice_in_dim(heads_query, first, block, 0)
        query_places = first + jnp.arange(block, dtype=jnp.int32)
        query_documents = lax.dynamic_slice_in_dim(documents, first, block, 0)
        scores = jnp.einsum("qhd,khd->hqk", query_block, keys) * scale
        allowed = (positions[None, :] <= query_places[:, None]) & (documents[None, :] == query_documents[:, None])
        masked = jnp.where(allowed[None], scores, NEGATIVE)
        highest = jnp.max(masked, axis=2, keepdims=True)
        raised = jnp.where(allowed[None], jnp.exp(masked - highest), 0.0)
        totals = jnp.sum(raised, axis=2)
        weights = lax.optimization_barrier(raised.astype(jnp.bfloat16)).astype(jnp.float32)
        summed = jnp.einsum("hqk,khd->qhd", weights, values)
        return (summed / totals.T[:, :, None]).astype(jnp.bfloat16)

    blocks = lax.map(one_block, jnp.arange(SEQ_TOK // block, dtype=jnp.int32))
    return blocks.reshape(SEQ_TOK, HQ * HD)


def reference(queries, keys_values, route_group, route_slot, doc_lengths):
    placed_queries = to_trainers(queries, route_group, route_slot)
    placed_keys_values = to_trainers(keys_values, route_group, route_slot)
    return lax.map(attend_group, (placed_queries, placed_keys_values, doc_lengths))
```

```python
import functools
import math

import jax
import jax.numpy as jnp
from jax import lax
from jax.experimental import pallas as pl
from jax.experimental.pallas import tpu as pltpu
from jax.sharding import PartitionSpec as P

HQ = 32
HK = 4
HD = 128
TOK = 128
GROUPS = 16
CAP = 16
SLOTS = GROUPS * CAP
WIDE = HQ // HK * HD
PAIR = 2 * HK * HD
BACK = 8
SPAN = (BACK + 1) * TOK
NX = 4
HALF_ROWS = 4
NEGATIVE = -1e30
MESH = pl.DeviceIdType.MESH
FACTOR = HD ** (-0.5) * math.log2(math.e)


def remote(src, dst, send, recv, device):
    return pltpu.make_async_remote_copy(
        src_ref=src,
        dst_ref=dst,
        send_sem=send,
        recv_sem=recv,
        device_id=device,
        device_id_type=MESH,
    )


def contract(a, b, dims):
    return lax.dot_general(a, b, (dims, ((), ())), preferred_element_type=jnp.float32)


def kernel(
    q_hbm,
    kv_ref,
    group_ref,
    slot_ref,
    length_ref,
    out_hbm,
    q_in,
    q_send,
    q_recv,
    kv_send,
    kv_recv,
    window,
    mask,
    placed,
    out_buf,
    in_sem,
    out_sem,
    q_ss,
    q_rs,
    kv_ss,
    kv_rs,
    z_ss,
    z_rs,
    x_ss,
    x_rs,
):
    me = lax.axis_index("grp")
    seq = lax.axis_index("seq")
    z = seq // NX
    x = seq % NX
    zz = z % HALF_ROWS
    has_next = zz < HALF_ROWS - 1
    has_last = zz > 0

    def load(j):
        cols = pl.ds(j * WIDE, WIDE)
        return pltpu.make_async_copy(q_hbm.at[0, :, cols], q_in.at[:, cols], in_sem.at[j])

    for j in range(HK):
        load(j).start()

    barrier = pltpu.get_barrier_semaphore()

    def greet(group, place):
        pl.semaphore_signal(barrier, inc=1, device_id=(group, place), device_id_type=MESH)

    for d in range(1, GROUPS):
        greet((me + d) % GROUPS, seq)
    for d in range(1, NX):
        greet(me, z * NX + (x + d) % NX)

    @pl.when(has_next)
    def _():
        greet(me, seq + NX)

    @pl.when(has_last)
    def _():
        greet(me, seq - NX)

    targets = group_ref[...]
    lane = lax.broadcasted_iota(jnp.int32, (TOK, TOK), 1)
    sub = lax.broadcasted_iota(jnp.int32, (TOK, TOK), 0)
    hits = lax.broadcasted_iota(jnp.int32, (GROUPS, TOK), 0) == targets
    before = (sub < lane).astype(jnp.float32).astype(jnp.bfloat16)
    hits_f = hits.astype(jnp.float32)
    ranks = contract(hits_f.astype(jnp.bfloat16), before, ((1,), (0,)))
    ranks = jnp.where(hits, ranks, -1.0)
    level = lax.broadcasted_iota(jnp.int32, (GROUPS, CAP, TOK), 1).astype(jnp.float32)
    pick_f = (ranks[:, None, :] == level).astype(jnp.float32).reshape(SLOTS, TOK)
    pick = pick_f.astype(jnp.bfloat16)
    marks = (pick_f * (slot_ref[...] + 1).astype(jnp.float32)).astype(jnp.bfloat16)
    slots = contract(marks, jnp.ones((TOK, TOK), jnp.bfloat16), ((1,), (0,)))
    kv_send[:, :, PAIR:] = slots.astype(jnp.bfloat16).reshape(GROUPS, CAP, TOK)
    kv_send[:, :, :PAIR] = (
        contract(pick, kv_ref[0], ((1,), (0,))).astype(jnp.bfloat16).reshape(GROUPS, CAP, PAIR)
    )

    pl.semaphore_wait(
        barrier, GROUPS - 1 + NX - 1 + has_next.astype(jnp.int32) + has_last.astype(jnp.int32)
    )

    def kv_copy(d):
        target = (me + d) % GROUPS
        return remote(
            kv_send.at[target], kv_recv.at[me], kv_ss.at[d], kv_rs.at[d], (target, seq)
        )

    @pl.loop(1, GROUPS)
    def _(d):
        kv_copy(d).start()

    kv_recv[me] = kv_send[me]

    def q_copy(j, d):
        target = (me + d) % GROUPS
        return remote(
            q_send.at[j, target], q_recv.at[j, me], q_ss.at[j, d], q_rs.at[j, d], (target, seq)
        )

    for j in range(HK):
        load(j).wait()
        q_send[j] = (
            contract(pick, q_in[:, j * WIDE : (j + 1) * WIDE], ((1,), (0,)))
            .astype(jnp.bfloat16)
            .reshape(GROUPS, CAP, WIDE)
        )

        @pl.loop(1, GROUPS)
        def _(d, j=j):
            q_copy(j, d).start()

        q_recv[j, me] = q_send[j, me]

    query = seq * TOK + lax.broadcasted_iota(jnp.int32, (TOK, SPAN), 0)
    key = (seq - BACK) * TOK + lax.broadcasted_iota(jnp.int32, (TOK, SPAN), 1)
    begin = jnp.zeros((TOK, SPAN), jnp.int32)
    bound = jnp.int32(0)
    for half in range(2):
        for n in range(3):
            bound = bound + length_ref[0, half, n]
            begin = jnp.where(query >= bound, bound, begin)
    mask[...] = jnp.where((key >= begin) & (key <= query), 0.0, NEGATIVE)

    @pl.when(zz == 0)
    def _():
        window[pl.ds(0, 2 * NX)] = jnp.zeros((2 * NX, TOK, PAIR), jnp.bfloat16)

    @pl.when(zz == 1)
    def _():
        window[pl.ds(0, NX)] = jnp.zeros((NX, TOK, PAIR), jnp.bfloat16)

    @pl.loop(1, GROUPS)
    def _(d):
        kv_copy(d).wait_recv()

    marks_in = kv_recv[:, :, PAIR:].reshape(SLOTS, TOK).astype(jnp.float32)
    column = lax.broadcasted_iota(jnp.int32, (SLOTS, TOK), 1).astype(jnp.float32) + 1.0
    put = (marks_in == column).astype(jnp.float32).T.astype(jnp.bfloat16)
    window[2 * NX + x] = contract(
        put, kv_recv[:, :, :PAIR].reshape(SLOTS, PAIR), ((1,), (0,))
    ).astype(jnp.bfloat16)

    def z_copy(plane):
        return remote(
            window.at[plane * NX + x],
            window.at[(plane - 1) * NX + x],
            z_ss.at[plane],
            z_rs.at[plane],
            (me, (seq + NX) % (NX * 8)),
        )

    def x_copy(plane, d):
        return remote(
            window.at[plane * NX + x],
            window.at[plane * NX + x],
            x_ss.at[plane, d],
            x_rs.at[plane, d],
            (me, z * NX + (x + d) % NX),
        )

    def x_wait(plane, d):
        source = (x + NX - d) % NX
        return remote(
            window.at[plane * NX + source],
            window.at[plane * NX + source],
            x_ss.at[plane, d],
            x_rs.at[plane, d],
            (me, z * NX + (x + d) % NX),
        )

    def each_x(plane, act, sending):
        for d in range(1, NX):
            wraps = x + d >= NX if sending else x - d < 0
            if plane == 1:
                act(plane, d)
            else:
                pl.when(wraps if plane == 0 else jnp.logical_not(wraps))(
                    functools.partial(act, plane, d)
                )

    def start_x(plane, d):
        x_copy(plane, d).start()

    def sent_x(plane, d):
        x_copy(plane, d).wait_send()

    def came_x(plane, d):
        x_wait(plane, d).wait_recv()

    @pl.when(has_next)
    def _():
        z_copy(2).start()

    each_x(2, start_x, True)

    @pl.when(has_last)
    def _():
        z_copy(2).wait_recv()

        @pl.when(has_next)
        def _():
            z_copy(1).start()

        each_x(1, start_x, True)

    @pl.when(zz >= 2)
    def _():
        z_copy(1).wait_recv()
        each_x(0, start_x, True)

    each_x(2, came_x, False)

    @pl.when(has_last)
    def _():
        each_x(1, came_x, False)

    @pl.when(zz >= 2)
    def _():
        each_x(0, came_x, False)

    def store(j):
        cols = pl.ds(pl.multiple_of(j * WIDE, WIDE), WIDE)
        return pltpu.make_async_copy(out_buf.at[:, cols], out_hbm.at[0, :, cols], out_sem.at[j])

    @pl.loop(0, HK)
    def _(j):
        @pl.loop(1, GROUPS)
        def _(d):
            q_copy(j, d).wait_recv()

        rows = contract(put, q_recv[j].reshape(SLOTS, WIDE), ((1,), (0,))).astype(jnp.bfloat16)
        for h in range(HQ // HK):
            placed[h] = rows[:, h * HD : (h + 1) * HD]
        key_cols = pl.ds(pl.multiple_of(j * HD, HD), HD)
        value_cols = pl.ds(pl.multiple_of((HK + j) * HD, HD), HD)

        @pl.loop(0, HQ // HK)
        def _(h):
            keys = window[pl.ds(x, BACK + 1), :, key_cols].reshape(SPAN, HD)
            values = window[pl.ds(x, BACK + 1), :, value_cols].reshape(SPAN, HD)
            scores = contract(placed[h], keys, ((1,), (1,))) + mask[...]
            top = jnp.max(scores, axis=1, keepdims=True)
            raised = jnp.exp2((scores - top) * FACTOR)
            total = jnp.sum(raised, axis=1, keepdims=True)
            summed = contract(raised.astype(jnp.bfloat16), values, ((1,), (0,)))
            cols = pl.ds(pl.multiple_of((j * (HQ // HK) + h) * HD, HD), HD)
            out_buf[:, cols] = (summed / total).astype(jnp.bfloat16)

        store(j).start()

    for j in range(HK):
        store(j).wait()

    @pl.loop(1, GROUPS)
    def _(d):
        kv_copy(d).wait_send()
        for j in range(HK):
            q_copy(j, d).wait_send()

    each_x(2, sent_x, True)

    @pl.when(has_next)
    def _():
        z_copy(2).wait_send()

    @pl.when(has_last)
    def _():
        each_x(1, sent_x, True)

        @pl.when(has_next)
        def _():
            z_copy(1).wait_send()

    @pl.when(zz >= 2)
    def _():
        each_x(0, sent_x, True)


def local(queries, keys_values, route_group, route_slot, doc_lengths):
    bf16 = jnp.bfloat16
    dma = pltpu.SemaphoreType.DMA
    return pl.pallas_call(
        kernel,
        out_shape=jax.ShapeDtypeStruct((1, TOK, HQ * HD), bf16),
        in_specs=[
            pl.BlockSpec(memory_space=pl.ANY),
            pl.BlockSpec(memory_space=pltpu.VMEM),
            pl.BlockSpec(memory_space=pltpu.VMEM),
            pl.BlockSpec(memory_space=pltpu.VMEM),
            pl.BlockSpec(memory_space=pltpu.SMEM),
        ],
        out_specs=pl.BlockSpec(memory_space=pl.ANY),
        scratch_shapes=[
            pltpu.VMEM((TOK, HQ * HD), bf16),
            pltpu.VMEM((HK, GROUPS, CAP, WIDE), bf16),
            pltpu.VMEM((HK, GROUPS, CAP, WIDE), bf16),
            pltpu.VMEM((GROUPS, CAP, PAIR + TOK), bf16),
            pltpu.VMEM((GROUPS, CAP, PAIR + TOK), bf16),
            pltpu.VMEM((3 * NX, TOK, PAIR), bf16),
            pltpu.VMEM((TOK, SPAN), jnp.float32),
            pltpu.VMEM((HQ // HK, TOK, HD), bf16),
            pltpu.VMEM((TOK, HQ * HD), bf16),
            dma((HK,)),
            dma((HK,)),
            dma((HK, GROUPS)),
            dma((HK, GROUPS)),
            dma((GROUPS,)),
            dma((GROUPS,)),
            dma((3,)),
            dma((3,)),
            dma((3, NX)),
            dma((3, NX)),
        ],
        compiler_params=pltpu.CompilerParams(
            collective_id=0, has_side_effects=True, vmem_limit_bytes=48 << 20
        ),
    )(queries, keys_values, route_group, route_slot, doc_lengths)


def solution(mesh):
    return jax.shard_map(
        local,
        mesh=mesh,
        in_specs=(
            P("grp", "seq", None),
            P("grp", "seq", None),
            P("grp", "seq"),
            P("grp", "seq"),
            P("grp", None, None),
        ),
        out_specs=P("grp", "seq", None),
        check_vma=False,
    )
```

```python
import functools
import math

import jax
import jax.numpy as jnp
from jax import lax
from jax.experimental import pallas as pl
from jax.experimental.pallas import tpu as pltpu
from jax.sharding import PartitionSpec as P

HQ = 32
HK = 4
HD = 128
TOK = 128
GROUPS = 16
CAP = 16
SLOTS = GROUPS * CAP
WIDE = HQ // HK * HD
PAIR = 2 * HK * HD
BACK = 8
SPAN = (BACK + 1) * TOK
NX = 4
HALF_ROWS = 4
NEGATIVE = -1e30
MESH = pl.DeviceIdType.MESH
FACTOR = HD ** (-0.5) * math.log2(math.e)


def remote(src, dst, send, recv, device):
    return pltpu.make_async_remote_copy(
        src_ref=src,
        dst_ref=dst,
        send_sem=send,
        recv_sem=recv,
        device_id=device,
        device_id_type=MESH,
    )


def contract(a, b, dims):
    return lax.dot_general(a, b, (dims, ((), ())), preferred_element_type=jnp.float32)


def kernel(
    q_hbm,
    kv_hbm,
    group_hbm,
    slot_hbm,
    length_hbm,
    out_hbm,
    q_in,
    kv_ref,
    group_ref,
    slot_ref,
    length_ref,
    q_send,
    q_recv,
    kv_send,
    kv_recv,
    window,
    mask,
    placed,
    out_buf,
    in_sem,
    out_sem,
    q_ss,
    q_rs,
    kv_ss,
    kv_rs,
    z_ss,
    z_rs,
    x_ss,
    x_rs,
):
    me = lax.axis_index("grp")
    seq = lax.axis_index("seq")
    z = seq // NX
    x = seq % NX
    zz = z % HALF_ROWS
    has_next = zz < HALF_ROWS - 1
    has_last = zz > 0

    def load(j):
        cols = pl.ds(j * WIDE, WIDE)
        return pltpu.make_async_copy(q_hbm.at[0, :, cols], q_in.at[:, cols], in_sem.at[j])

    small = [
        pltpu.make_async_copy(source, target, in_sem.at[HK + n])
        for n, (source, target) in enumerate(
            [
                (group_hbm, group_ref),
                (slot_hbm, slot_ref),
                (kv_hbm, kv_ref),
                (length_hbm, length_ref),
            ]
        )
    ]
    for copy in small:
        copy.start()
    for j in range(HK):
        load(j).start()

    barrier = pltpu.get_barrier_semaphore()

    def greet(group, place):
        pl.semaphore_signal(barrier, inc=1, device_id=(group, place), device_id_type=MESH)

    for d in range(1, GROUPS):
        greet((me + d) % GROUPS, seq)
    for d in range(1, NX):
        greet(me, z * NX + (x + d) % NX)

    @pl.when(has_next)
    def _():
        greet(me, seq + NX)

    @pl.when(has_last)
    def _():
        greet(me, seq - NX)

    for copy in small:
        copy.wait()
    targets = group_ref[...]
    lane = lax.broadcasted_iota(jnp.int32, (TOK, TOK), 1)
    sub = lax.broadcasted_iota(jnp.int32, (TOK, TOK), 0)
    hits = lax.broadcasted_iota(jnp.int32, (GROUPS, TOK), 0) == targets
    before = (sub < lane).astype(jnp.float32).astype(jnp.bfloat16)
    hits_f = hits.astype(jnp.float32)
    ranks = contract(hits_f.astype(jnp.bfloat16), before, ((1,), (0,)))
    ranks = jnp.where(hits, ranks, -1.0)
    level = lax.broadcasted_iota(jnp.int32, (GROUPS, CAP, TOK), 1).astype(jnp.float32)
    pick_f = (ranks[:, None, :] == level).astype(jnp.float32).reshape(SLOTS, TOK)
    pick = pick_f.astype(jnp.bfloat16)
    marks = (pick_f * (slot_ref[...] + 1).astype(jnp.float32)).astype(jnp.bfloat16)
    slots = contract(marks, jnp.ones((TOK, TOK), jnp.bfloat16), ((1,), (0,)))
    kv_send[:, :, PAIR:] = slots.astype(jnp.bfloat16).reshape(GROUPS, CAP, TOK)
    kv_send[:, :, :PAIR] = (
        contract(pick, kv_ref[0], ((1,), (0,))).astype(jnp.bfloat16).reshape(GROUPS, CAP, PAIR)
    )

    pl.semaphore_wait(
        barrier, GROUPS - 1 + NX - 1 + has_next.astype(jnp.int32) + has_last.astype(jnp.int32)
    )

    def kv_copy(d):
        target = (me + d) % GROUPS
        return remote(
            kv_send.at[target], kv_recv.at[me], kv_ss.at[d], kv_rs.at[d], (target, seq)
        )

    @pl.loop(1, GROUPS)
    def _(d):
        kv_copy(d).start()

    kv_recv[me] = kv_send[me]

    def q_copy(j, d):
        target = (me + d) % GROUPS
        return remote(
            q_send.at[j, target], q_recv.at[j, me], q_ss.at[j, d], q_rs.at[j, d], (target, seq)
        )

    for j in range(HK):
        load(j).wait()
        q_send[j] = (
            contract(pick, q_in[:, j * WIDE : (j + 1) * WIDE], ((1,), (0,)))
            .astype(jnp.bfloat16)
            .reshape(GROUPS, CAP, WIDE)
        )

        @pl.loop(1, GROUPS)
        def _(d, j=j):
            q_copy(j, d).start()

        q_recv[j, me] = q_send[j, me]

    query = seq * TOK + lax.broadcasted_iota(jnp.int32, (TOK, SPAN), 0)
    key = (seq - BACK) * TOK + lax.broadcasted_iota(jnp.int32, (TOK, SPAN), 1)
    begin = jnp.zeros((TOK, SPAN), jnp.int32)
    bound = jnp.int32(0)
    for half in range(2):
        for n in range(3):
            bound = bound + length_ref[0, half, n]
            begin = jnp.where(query >= bound, bound, begin)
    mask[...] = jnp.where((key >= begin) & (key <= query), 0.0, NEGATIVE)

    @pl.when(zz == 0)
    def _():
        window[pl.ds(0, 2 * NX)] = jnp.zeros((2 * NX, TOK, PAIR), jnp.bfloat16)

    @pl.when(zz == 1)
    def _():
        window[pl.ds(0, NX)] = jnp.zeros((NX, TOK, PAIR), jnp.bfloat16)

    @pl.loop(1, GROUPS)
    def _(d):
        kv_copy(d).wait_recv()

    marks_in = kv_recv[:, :, PAIR:].reshape(SLOTS, TOK).astype(jnp.float32)
    column = lax.broadcasted_iota(jnp.int32, (SLOTS, TOK), 1).astype(jnp.float32) + 1.0
    put = (marks_in == column).astype(jnp.float32).T.astype(jnp.bfloat16)
    window[2 * NX + x] = contract(
        put, kv_recv[:, :, :PAIR].reshape(SLOTS, PAIR), ((1,), (0,))
    ).astype(jnp.bfloat16)

    def z_copy(plane):
        return remote(
            window.at[plane * NX + x],
            window.at[(plane - 1) * NX + x],
            z_ss.at[plane],
            z_rs.at[plane],
            (me, (seq + NX) % (NX * 8)),
        )

    def x_copy(plane, d):
        return remote(
            window.at[plane * NX + x],
            window.at[plane * NX + x],
            x_ss.at[plane, d],
            x_rs.at[plane, d],
            (me, z * NX + (x + d) % NX),
        )

    def x_wait(plane, d):
        source = (x + NX - d) % NX
        return remote(
            window.at[plane * NX + source],
            window.at[plane * NX + source],
            x_ss.at[plane, d],
            x_rs.at[plane, d],
            (me, z * NX + (x + d) % NX),
        )

    def each_x(plane, act, sending):
        for d in range(1, NX):
            wraps = x + d >= NX if sending else x - d < 0
            if plane == 1:
                act(plane, d)
            else:
                pl.when(wraps if plane == 0 else jnp.logical_not(wraps))(
                    functools.partial(act, plane, d)
                )

    def start_x(plane, d):
        x_copy(plane, d).start()

    def sent_x(plane, d):
        x_copy(plane, d).wait_send()

    def came_x(plane, d):
        x_wait(plane, d).wait_recv()

    @pl.when(has_next)
    def _():
        z_copy(2).start()

    each_x(2, start_x, True)

    @pl.when(has_last)
    def _():
        z_copy(2).wait_recv()

        @pl.when(has_next)
        def _():
            z_copy(1).start()

        each_x(1, start_x, True)

    @pl.when(zz >= 2)
    def _():
        z_copy(1).wait_recv()
        each_x(0, start_x, True)

    each_x(2, came_x, False)

    @pl.when(has_last)
    def _():
        each_x(1, came_x, False)

    @pl.when(zz >= 2)
    def _():
        each_x(0, came_x, False)

    def store(j):
        cols = pl.ds(pl.multiple_of(j * WIDE, WIDE), WIDE)
        return pltpu.make_async_copy(out_buf.at[:, cols], out_hbm.at[0, :, cols], out_sem.at[j])

    ones = jnp.ones((SPAN, HD), jnp.bfloat16)

    @pl.loop(0, HK)
    def _(j):
        @pl.loop(1, GROUPS)
        def _(d):
            q_copy(j, d).wait_recv()

        rows = contract(put, q_recv[j].reshape(SLOTS, WIDE), ((1,), (0,))).astype(jnp.bfloat16)
        for h in range(HQ // HK):
            placed[h] = rows[:, h * HD : (h + 1) * HD]
        key_cols = pl.ds(pl.multiple_of(j * HD, HD), HD)
        value_cols = pl.ds(pl.multiple_of((HK + j) * HD, HD), HD)

        for h in range(HQ // HK):
            keys = window[pl.ds(x, BACK + 1), :, key_cols].reshape(SPAN, HD)
            values = window[pl.ds(x, BACK + 1), :, value_cols].reshape(SPAN, HD)
            scores = contract(placed[h], keys, ((1,), (1,))) + mask[...]
            top = jnp.max(scores, axis=1, keepdims=True)
            weights = jnp.exp2((scores - top) * FACTOR).astype(jnp.bfloat16)
            summed = contract(weights, jnp.concatenate([values, ones], axis=1), ((1,), (0,)))
            cols = pl.ds(pl.multiple_of((j * (HQ // HK) + h) * HD, HD), HD)
            out_buf[:, cols] = (summed[:, :HD] / summed[:, HD:]).astype(jnp.bfloat16)

        store(j).start()

    for j in range(HK):
        store(j).wait()

    @pl.loop(1, GROUPS)
    def _(d):
        kv_copy(d).wait_send()
        for j in range(HK):
            q_copy(j, d).wait_send()

    each_x(2, sent_x, True)

    @pl.when(has_next)
    def _():
        z_copy(2).wait_send()

    @pl.when(has_last)
    def _():
        each_x(1, sent_x, True)

        @pl.when(has_next)
        def _():
            z_copy(1).wait_send()

    @pl.when(zz >= 2)
    def _():
        each_x(0, sent_x, True)


def local(queries, keys_values, route_group, route_slot, doc_lengths):
    bf16 = jnp.bfloat16
    dma = pltpu.SemaphoreType.DMA
    return pl.pallas_call(
        kernel,
        out_shape=jax.ShapeDtypeStruct((1, TOK, HQ * HD), bf16),
        in_specs=[
            pl.BlockSpec(memory_space=pltpu.HBM),
            pl.BlockSpec(memory_space=pltpu.HBM),
            pl.BlockSpec(memory_space=pltpu.HBM),
            pl.BlockSpec(memory_space=pltpu.HBM),
            pl.BlockSpec(memory_space=pltpu.HBM),
        ],
        out_specs=pl.BlockSpec(memory_space=pl.ANY),
        scratch_shapes=[
            pltpu.VMEM((TOK, HQ * HD), bf16),
            pltpu.VMEM((1, TOK, PAIR), bf16),
            pltpu.VMEM((1, TOK), jnp.int32),
            pltpu.VMEM((1, TOK), jnp.int32),
            pltpu.SMEM((1, 2, 3), jnp.int32),
            pltpu.VMEM((HK, GROUPS, CAP, WIDE), bf16),
            pltpu.VMEM((HK, GROUPS, CAP, WIDE), bf16),
            pltpu.VMEM((GROUPS, CAP, PAIR + TOK), bf16),
            pltpu.VMEM((GROUPS, CAP, PAIR + TOK), bf16),
            pltpu.VMEM((3 * NX, TOK, PAIR), bf16),
            pltpu.VMEM((TOK, SPAN), jnp.float32),
            pltpu.VMEM((HQ // HK, TOK, HD), bf16),
            pltpu.VMEM((TOK, HQ * HD), bf16),
            dma((HK + 4,)),
            dma((HK,)),
            dma((HK, GROUPS)),
            dma((HK, GROUPS)),
            dma((GROUPS,)),
            dma((GROUPS,)),
            dma((3,)),
            dma((3,)),
            dma((3, NX)),
            dma((3, NX)),
        ],
        compiler_params=pltpu.CompilerParams(
            collective_id=0, has_side_effects=True, vmem_limit_bytes=63 << 20
        ),
    )(queries, keys_values, route_group, route_slot, doc_lengths)


def solution(mesh):
    return jax.shard_map(
        local,
        mesh=mesh,
        in_specs=(
            P("grp", "seq", None),
            P("grp", "seq", None),
            P("grp", "seq"),
            P("grp", "seq"),
            P("grp", None, None),
        ),
        out_specs=P("grp", "seq", None),
        check_vma=False,
    )
```

```python
import functools
import math

import jax
import jax.numpy as jnp
from jax import lax
from jax.experimental import pallas as pl
from jax.experimental.pallas import tpu as pltpu
from jax.sharding import PartitionSpec as P

HQ = 32
HK = 4
HD = 128
TOK = 128
GROUPS = 16
CAP = 16
SLOTS = GROUPS * CAP
WIDE = HQ // HK * HD
PAIR = 2 * HK * HD
BACK = 8
SPAN = (BACK + 1) * TOK
NX = 4
HALF_ROWS = 4
NEGATIVE = -1e30
MESH = pl.DeviceIdType.MESH
FACTOR = HD ** (-0.5) * math.log2(math.e)


def remote(src, dst, send, recv, device):
    return pltpu.make_async_remote_copy(
        src_ref=src,
        dst_ref=dst,
        send_sem=send,
        recv_sem=recv,
        device_id=device,
        device_id_type=MESH,
    )


def contract(a, b, dims):
    return lax.dot_general(a, b, (dims, ((), ())), preferred_element_type=jnp.float32)


def padded_kernel(
    q_hbm,
    kv_hbm,
    group_hbm,
    slot_hbm,
    length_hbm,
    out_hbm,
    q_in,
    kv_ref,
    group_ref,
    slot_ref,
    length_ref,
    q_send,
    q_recv,
    kv_send,
    kv_recv,
    window,
    mask,
    placed,
    out_buf,
    in_sem,
    out_sem,
    q_ss,
    q_rs,
    kv_ss,
    kv_rs,
    z_ss,
    z_rs,
    x_ss,
    x_rs,
):
    me = lax.axis_index("grp")
    seq = lax.axis_index("seq")
    z = seq // NX
    x = seq % NX
    zz = z % HALF_ROWS
    has_next = zz < HALF_ROWS - 1
    has_last = zz > 0

    def load(j):
        cols = pl.ds(j * WIDE, WIDE)
        return pltpu.make_async_copy(q_hbm.at[0, :, cols], q_in.at[:, cols], in_sem.at[j])

    small = [
        pltpu.make_async_copy(source, target, in_sem.at[HK + n])
        for n, (source, target) in enumerate(
            [
                (group_hbm, group_ref),
                (slot_hbm, slot_ref),
                (kv_hbm, kv_ref),
                (length_hbm, length_ref),
            ]
        )
    ]
    for copy in small:
        copy.start()
    for j in range(HK):
        load(j).start()

    barrier = pltpu.get_barrier_semaphore()

    def greet(group, place):
        pl.semaphore_signal(barrier, inc=1, device_id=(group, place), device_id_type=MESH)

    for d in range(1, GROUPS):
        greet((me + d) % GROUPS, seq)
    for d in range(1, NX):
        greet(me, z * NX + (x + d) % NX)

    @pl.when(has_next)
    def _():
        greet(me, seq + NX)

    @pl.when(has_last)
    def _():
        greet(me, seq - NX)

    for copy in small:
        copy.wait()
    targets = group_ref[...]
    lane = lax.broadcasted_iota(jnp.int32, (TOK, TOK), 1)
    sub = lax.broadcasted_iota(jnp.int32, (TOK, TOK), 0)
    hits = lax.broadcasted_iota(jnp.int32, (GROUPS, TOK), 0) == targets
    before = (sub < lane).astype(jnp.float32).astype(jnp.bfloat16)
    hits_f = hits.astype(jnp.float32)
    ranks = contract(hits_f.astype(jnp.bfloat16), before, ((1,), (0,)))
    ranks = jnp.where(hits, ranks, -1.0)
    level = lax.broadcasted_iota(jnp.int32, (GROUPS, CAP, TOK), 1).astype(jnp.float32)
    pick_f = (ranks[:, None, :] == level).astype(jnp.float32).reshape(SLOTS, TOK)
    pick = pick_f.astype(jnp.bfloat16)
    marks = (pick_f * (slot_ref[...] + 1).astype(jnp.float32)).astype(jnp.bfloat16)
    slots = contract(marks, jnp.ones((TOK, TOK), jnp.bfloat16), ((1,), (0,)))
    kv_send[:, :, PAIR:] = slots.astype(jnp.bfloat16).reshape(GROUPS, CAP, TOK)
    kv_send[:, :, :PAIR] = (
        contract(pick, kv_ref[0], ((1,), (0,))).astype(jnp.bfloat16).reshape(GROUPS, CAP, PAIR)
    )

    pl.semaphore_wait(
        barrier, GROUPS - 1 + NX - 1 + has_next.astype(jnp.int32) + has_last.astype(jnp.int32)
    )

    def kv_copy(d):
        target = (me + d) % GROUPS
        return remote(
            kv_send.at[target], kv_recv.at[me], kv_ss.at[d], kv_rs.at[d], (target, seq)
        )

    @pl.loop(1, GROUPS)
    def _(d):
        kv_copy(d).start()

    kv_recv[me] = kv_send[me]

    def q_copy(j, d):
        target = (me + d) % GROUPS
        return remote(
            q_send.at[j, target], q_recv.at[j, me], q_ss.at[j, d], q_rs.at[j, d], (target, seq)
        )

    for j in range(HK):
        load(j).wait()
        q_send[j] = (
            contract(pick, q_in[:, j * WIDE : (j + 1) * WIDE], ((1,), (0,)))
            .astype(jnp.bfloat16)
            .reshape(GROUPS, CAP, WIDE)
        )

        @pl.loop(1, GROUPS)
        def _(d, j=j):
            q_copy(j, d).start()

        q_recv[j, me] = q_send[j, me]

    query = seq * TOK + lax.broadcasted_iota(jnp.int32, (TOK, SPAN), 0)
    key = (seq - BACK) * TOK + lax.broadcasted_iota(jnp.int32, (TOK, SPAN), 1)
    begin = jnp.zeros((TOK, SPAN), jnp.int32)
    bound = jnp.int32(0)
    for half in range(2):
        for n in range(3):
            bound = bound + length_ref[0, half, n]
            begin = jnp.where(query >= bound, bound, begin)
    mask[...] = jnp.where((key >= begin) & (key <= query), 0.0, NEGATIVE)

    @pl.when(zz == 0)
    def _():
        window[pl.ds(0, 2 * NX)] = jnp.zeros((2 * NX, TOK, PAIR), jnp.bfloat16)

    @pl.when(zz == 1)
    def _():
        window[pl.ds(0, NX)] = jnp.zeros((NX, TOK, PAIR), jnp.bfloat16)

    @pl.loop(1, GROUPS)
    def _(d):
        kv_copy(d).wait_recv()

    marks_in = kv_recv[:, :, PAIR:].reshape(SLOTS, TOK).astype(jnp.float32)
    column = lax.broadcasted_iota(jnp.int32, (SLOTS, TOK), 1).astype(jnp.float32) + 1.0
    put = (marks_in == column).astype(jnp.float32).T.astype(jnp.bfloat16)
    window[2 * NX + x] = contract(
        put, kv_recv[:, :, :PAIR].reshape(SLOTS, PAIR), ((1,), (0,))
    ).astype(jnp.bfloat16)

    def z_copy(plane):
        return remote(
            window.at[plane * NX + x],
            window.at[(plane - 1) * NX + x],
            z_ss.at[plane],
            z_rs.at[plane],
            (me, (seq + NX) % (NX * 8)),
        )

    def x_copy(plane, d):
        return remote(
            window.at[plane * NX + x],
            window.at[plane * NX + x],
            x_ss.at[plane, d],
            x_rs.at[plane, d],
            (me, z * NX + (x + d) % NX),
        )

    def x_wait(plane, d):
        source = (x + NX - d) % NX
        return remote(
            window.at[plane * NX + source],
            window.at[plane * NX + source],
            x_ss.at[plane, d],
            x_rs.at[plane, d],
            (me, z * NX + (x + d) % NX),
        )

    def each_x(plane, act, sending):
        for d in range(1, NX):
            wraps = x + d >= NX if sending else x - d < 0
            if plane == 1:
                act(plane, d)
            else:
                pl.when(wraps if plane == 0 else jnp.logical_not(wraps))(
                    functools.partial(act, plane, d)
                )

    def start_x(plane, d):
        x_copy(plane, d).start()

    def sent_x(plane, d):
        x_copy(plane, d).wait_send()

    def came_x(plane, d):
        x_wait(plane, d).wait_recv()

    @pl.when(has_next)
    def _():
        z_copy(2).start()

    each_x(2, start_x, True)

    @pl.when(has_last)
    def _():
        z_copy(2).wait_recv()

        @pl.when(has_next)
        def _():
            z_copy(1).start()

        each_x(1, start_x, True)

    @pl.when(zz >= 2)
    def _():
        z_copy(1).wait_recv()
        each_x(0, start_x, True)

    each_x(2, came_x, False)

    @pl.when(has_last)
    def _():
        each_x(1, came_x, False)

    @pl.when(zz >= 2)
    def _():
        each_x(0, came_x, False)

    def store(j):
        cols = pl.ds(pl.multiple_of(j * WIDE, WIDE), WIDE)
        return pltpu.make_async_copy(out_buf.at[:, cols], out_hbm.at[0, :, cols], out_sem.at[j])

    ones = jnp.ones((SPAN, HD), jnp.bfloat16)

    @pl.loop(0, HK)
    def _(j):
        @pl.loop(1, GROUPS)
        def _(d):
            q_copy(j, d).wait_recv()

        rows = contract(put, q_recv[j].reshape(SLOTS, WIDE), ((1,), (0,))).astype(jnp.bfloat16)
        for h in range(HQ // HK):
            placed[h] = rows[:, h * HD : (h + 1) * HD]
        key_cols = pl.ds(pl.multiple_of(j * HD, HD), HD)
        value_cols = pl.ds(pl.multiple_of((HK + j) * HD, HD), HD)

        for h in range(HQ // HK):
            keys = window[pl.ds(x, BACK + 1), :, key_cols].reshape(SPAN, HD)
            values = window[pl.ds(x, BACK + 1), :, value_cols].reshape(SPAN, HD)
            scores = contract(placed[h], keys, ((1,), (1,))) + mask[...]
            top = jnp.max(scores, axis=1, keepdims=True)
            weights = jnp.exp2((scores - top) * FACTOR).astype(jnp.bfloat16)
            summed = contract(weights, jnp.concatenate([values, ones], axis=1), ((1,), (0,)))
            cols = pl.ds(pl.multiple_of((j * (HQ // HK) + h) * HD, HD), HD)
            out_buf[:, cols] = (summed[:, :HD] / summed[:, HD:]).astype(jnp.bfloat16)

        store(j).start()

    for j in range(HK):
        store(j).wait()

    @pl.loop(1, GROUPS)
    def _(d):
        kv_copy(d).wait_send()
        for j in range(HK):
            q_copy(j, d).wait_send()

    each_x(2, sent_x, True)

    @pl.when(has_next)
    def _():
        z_copy(2).wait_send()

    @pl.when(has_last)
    def _():
        each_x(1, sent_x, True)

        @pl.when(has_next)
        def _():
            z_copy(1).wait_send()

    @pl.when(zz >= 2)
    def _():
        each_x(0, sent_x, True)


def padded(queries, keys_values, route_group, route_slot, doc_lengths):
    bf16 = jnp.bfloat16
    dma = pltpu.SemaphoreType.DMA
    return pl.pallas_call(
        padded_kernel,
        out_shape=jax.ShapeDtypeStruct((1, TOK, HQ * HD), bf16),
        in_specs=[
            pl.BlockSpec(memory_space=pltpu.HBM),
            pl.BlockSpec(memory_space=pltpu.HBM),
            pl.BlockSpec(memory_space=pltpu.HBM),
            pl.BlockSpec(memory_space=pltpu.HBM),
            pl.BlockSpec(memory_space=pltpu.HBM),
        ],
        out_specs=pl.BlockSpec(memory_space=pl.ANY),
        scratch_shapes=[
            pltpu.VMEM((TOK, HQ * HD), bf16),
            pltpu.VMEM((1, TOK, PAIR), bf16),
            pltpu.VMEM((1, TOK), jnp.int32),
            pltpu.VMEM((1, TOK), jnp.int32),
            pltpu.SMEM((1, 2, 3), jnp.int32),
            pltpu.VMEM((HK, GROUPS, CAP, WIDE), bf16),
            pltpu.VMEM((HK, GROUPS, CAP, WIDE), bf16),
            pltpu.VMEM((GROUPS, CAP, PAIR + TOK), bf16),
            pltpu.VMEM((GROUPS, CAP, PAIR + TOK), bf16),
            pltpu.VMEM((3 * NX, TOK, PAIR), bf16),
            pltpu.VMEM((TOK, SPAN), jnp.float32),
            pltpu.VMEM((HQ // HK, TOK, HD), bf16),
            pltpu.VMEM((TOK, HQ * HD), bf16),
            dma((HK + 4,)),
            dma((HK,)),
            dma((HK, GROUPS)),
            dma((HK, GROUPS)),
            dma((GROUPS,)),
            dma((GROUPS,)),
            dma((3,)),
            dma((3,)),
            dma((3, NX)),
            dma((3, NX)),
        ],
        compiler_params=pltpu.CompilerParams(
            collective_id=0, has_side_effects=True, vmem_limit_bytes=64 << 20
        ),
    )(queries, keys_values, route_group, route_slot, doc_lengths)


LOW = 8
OVER = 8
HALF_WIDE = WIDE // 2
PIECE = PAIR // 2
NY = GROUPS // 2
NZ = 2 * HALF_ROWS


def both_halves(one):
    none = jnp.zeros_like(one)
    left = jnp.concatenate([one, none], axis=1)
    right = jnp.concatenate([none, one], axis=1)
    lanes = one.shape[2]
    return jnp.concatenate([left.reshape(-1, lanes), right.reshape(-1, lanes)], axis=1)


def compact_kernel(
    q_hbm,
    kv_hbm,
    group_hbm,
    slot_hbm,
    length_hbm,
    out_hbm,
    flag_ref,
    q_in,
    kv_ref,
    group_ref,
    slot_ref,
    length_ref,
    q_send,
    q_recv,
    kva_send,
    kva_recv,
    kvb_send,
    kvb_recv,
    over,
    window,
    mask,
    placed,
    out_buf,
    flag_x,
    flag_z,
    in_sem,
    out_sem,
    q_ss,
    q_rs,
    kv_ss,
    kv_rs,
    ring_ss,
    ring_rs,
    sib_ss,
    sib_rs,
    z_ss,
    z_rs,
    x_ss,
    x_rs,
    fx_ss,
    fx_rs,
    fz_ss,
    fz_rs,
):
    bf16 = jnp.bfloat16
    f32 = jnp.float32
    me = lax.axis_index("grp")
    seq = lax.axis_index("seq")
    z = seq // NX
    x = seq % NX
    zz = z % HALF_ROWS
    y = me // 2
    core = me % 2
    has_next = zz < HALF_ROWS - 1
    has_last = zz > 0

    small = [
        pltpu.make_async_copy(source, target, in_sem.at[2 * HK + n])
        for n, (source, target) in enumerate(
            [
                (group_hbm, group_ref),
                (slot_hbm, slot_ref),
                (kv_hbm, kv_ref),
                (length_hbm, length_ref),
            ]
        )
    ]
    loads = [
        pltpu.make_async_copy(
            q_hbm.at[0, :, pl.ds(n * HALF_WIDE, HALF_WIDE)], q_in.at[n], in_sem.at[n]
        )
        for n in range(2 * HK)
    ]
    for copy in small + loads:
        copy.start()

    barrier = pltpu.get_barrier_semaphore()

    def greet(group, place):
        pl.semaphore_signal(barrier, inc=1, device_id=(group, place), device_id_type=MESH)

    for d in range(1, GROUPS):
        greet((me + d) % GROUPS, seq)
    for d in range(1, NX):
        greet(me, z * NX + (x + d) % NX)
    for d in range(1, NZ):
        greet(me, (z + d) % NZ * NX + x)

    for copy in small:
        copy.wait()
    targets = group_ref[...]
    lane = lax.broadcasted_iota(jnp.int32, (TOK, TOK), 1)
    sub = lax.broadcasted_iota(jnp.int32, (TOK, TOK), 0)
    hits = lax.broadcasted_iota(jnp.int32, (GROUPS, TOK), 0) == targets
    before = (sub < lane).astype(f32).astype(bf16)
    all_ones = jnp.ones((TOK, TOK), bf16)
    ranks = contract(hits.astype(f32).astype(bf16), before, ((1,), (0,)))
    ranks = jnp.where(hits, ranks, -1.0)
    level = lax.broadcasted_iota(jnp.int32, (GROUPS, CAP, TOK), 1).astype(f32)
    pick_three = (ranks[:, None, :] == level).astype(f32)
    pick_f = pick_three.reshape(SLOTS, TOK)
    pick = pick_f.astype(bf16)
    places = (slot_ref[...] + 1).astype(f32)
    beyond = jnp.sum((ranks >= LOW).astype(f32), axis=0, keepdims=True)
    order = contract(jnp.broadcast_to(beyond, (OVER, TOK)).astype(bf16), before, ((1,), (0,)))
    row = lax.broadcasted_iota(jnp.int32, (OVER, TOK), 0).astype(f32)
    extra = jnp.where((order == row) & (beyond > 0.0), 1.0, 0.0)
    crowded = jnp.sum(beyond, axis=1, keepdims=True) > OVER
    marks = contract((pick_f * places).astype(bf16), all_ones, ((1,), (0,)))
    marks = jnp.where(crowded, -1.0, marks)
    kva_send[:, :, PIECE:] = marks.astype(bf16).reshape(GROUPS, CAP, TOK)

    sends = [kva_send, kvb_send]
    recvs = [kva_recv, kvb_recv]

    def pack_pairs(n):
        for part in range(2):
            cols = kv_ref[0, :, part * PIECE + n * PIECE // 2 : part * PIECE + (n + 1) * PIECE // 2]
            sends[n][:, :, part * PIECE // 2 : (part + 1) * PIECE // 2] = (
                contract(pick, cols, ((1,), (0,))).astype(bf16).reshape(GROUPS, CAP, PIECE // 2)
            )

    def kv_copy(n, d):
        target = (me + d) % GROUPS
        return remote(
            sends[n].at[target], recvs[n].at[me], kv_ss.at[n, d], kv_rs.at[n, d], (target, seq)
        )

    def start_pairs(n):
        @pl.loop(1, GROUPS)
        def _(d):
            kv_copy(n, d).start()

        recvs[n][me] = sends[n][me]

    high = both_halves(extra[None]).astype(bf16)
    for j in range(HK):
        loads[2 * j].wait()
        loads[2 * j + 1].wait()
        halves = q_in[2 * j : 2 * j + 2].reshape(2 * TOK, HALF_WIDE)
        over[me, :, j * HALF_WIDE : (j + 1) * HALF_WIDE] = contract(
            high, halves, ((1,), (0,))
        ).astype(bf16)
    tags = jnp.concatenate([extra * places, extra * (targets + 1).astype(f32)], axis=0)
    over[me, :, HK * HALF_WIDE :] = contract(tags.astype(bf16), all_ones, ((1,), (0,))).astype(bf16)
    pack_pairs(0)

    turn = 1 - 2 * core

    def on_ring(at):
        return (at + 2 * NY) % NY * 2 + core

    def on_sibling(at):
        return (at + 2 * NY) % NY * 2 + 1 - core

    def ring(step, way):
        sign = turn if way == 0 else -turn
        block = on_ring(y - sign * (step - 1))
        return remote(
            over.at[block],
            over.at[block],
            ring_ss.at[way, step],
            ring_rs.at[way, step],
            (on_ring(y + sign), seq),
        )

    def ring_came(step, way):
        sign = turn if way == 0 else -turn
        block = on_ring(y - sign * step)
        remote(
            over.at[block],
            over.at[block],
            ring_ss.at[way, step],
            ring_rs.at[way, step],
            (on_ring(y + sign), seq),
        ).wait_recv()

    def sibling(n):
        block = on_ring(y - turn * n if n <= NY // 2 else y + turn * (n - NY // 2))
        return remote(
            over.at[block], over.at[block], sib_ss.at[n], sib_rs.at[n], (on_sibling(y), seq)
        )

    def sibling_came(n):
        block = on_sibling(y + turn * n if n <= NY // 2 else y - turn * (n - NY // 2))
        remote(
            over.at[block], over.at[block], sib_ss.at[n], sib_rs.at[n], (on_sibling(y), seq)
        ).wait_recv()

    def ring_turn(step):
        ring_came(step, 0)
        if step < NY // 2:
            ring(step + 1, 0).start()
            ring_came(step, 1)
            if step + 1 < NY // 2:
                ring(step + 1, 1).start()
            sibling(NY // 2 + step).start()
        sibling(step).start()

    pl.semaphore_wait(barrier, GROUPS - 1 + NX - 1 + NZ - 1)
    ring(1, 0).start()
    ring(1, 1).start()
    start_pairs(0)
    sibling(0).start()
    pack_pairs(1)
    start_pairs(1)

    low = both_halves(pick_three[:, :LOW]).astype(bf16)
    for j in range(HK):
        halves = q_in[2 * j : 2 * j + 2].reshape(2 * TOK, HALF_WIDE)
        q_send[j] = (
            contract(low, halves, ((1,), (0,))).astype(bf16).reshape(GROUPS, CAP, HALF_WIDE)
        )

    def q_copy(j, d):
        target = (me + d) % GROUPS
        return remote(
            q_send.at[j, target], q_recv.at[j, me], q_ss.at[j, d], q_rs.at[j, d], (target, seq)
        )

    def start_queries(j):
        @pl.loop(1, GROUPS)
        def _(d):
            q_copy(j, d).start()

        q_recv[j, me] = q_send[j, me]

    start_queries(0)

    query = seq * TOK + lax.broadcasted_iota(jnp.int32, (TOK, SPAN), 0)
    key = (seq - BACK) * TOK + lax.broadcasted_iota(jnp.int32, (TOK, SPAN), 1)
    begin = jnp.zeros((TOK, SPAN), jnp.int32)
    bound = jnp.int32(0)
    for half in range(2):
        for n in range(3):
            bound = bound + length_ref[0, half, n]
            begin = jnp.where(query >= bound, bound, begin)
    mask[...] = jnp.where((key >= begin) & (key <= query), 0.0, NEGATIVE)

    @pl.when(zz == 0)
    def _():
        window[:, pl.ds(0, 2 * NX)] = jnp.zeros((2, 2 * NX, TOK, PIECE), bf16)

    @pl.when(zz == 1)
    def _():
        window[:, pl.ds(0, NX)] = jnp.zeros((2, NX, TOK, PIECE), bf16)

    def z_copy(n, plane):
        return remote(
            window.at[n, plane * NX + x],
            window.at[n, (plane - 1) * NX + x],
            z_ss.at[n, plane],
            z_rs.at[n, plane],
            (me, (seq + NX) % (NX * NZ)),
        )

    def x_copy(n, plane, d, came=False):
        at = plane * NX + ((x + NX - d) % NX if came else x)
        return remote(
            window.at[n, at],
            window.at[n, at],
            x_ss.at[n, plane, d],
            x_rs.at[n, plane, d],
            (me, z * NX + (x + d) % NX),
        )

    def start_x(n, plane, d):
        x_copy(n, plane, d).start()

    def sent_x(n, plane, d):
        x_copy(n, plane, d).wait_send()

    def came_x(n, plane, d):
        x_copy(n, plane, d, True).wait_recv()

    def each_x(n, plane, act):
        for d in range(1, NX):
            wraps = x - d < 0 if act is came_x else x + d >= NX
            if plane == 1:
                act(n, plane, d)
            else:
                pl.when(wraps if plane == 0 else jnp.logical_not(wraps))(
                    functools.partial(act, n, plane, d)
                )

    def place_pairs(n):
        window[n, 2 * NX + x] = contract(
            put, recvs[n][:, :, :PIECE].reshape(SLOTS, PIECE), ((1,), (0,))
        ).astype(bf16)

        @pl.when(has_next)
        def _():
            z_copy(n, 2).start()

        each_x(n, 2, start_x)

    def one_back(n):
        @pl.when(has_last)
        def _():
            z_copy(n, 2).wait_recv()

            @pl.when(has_next)
            def _():
                z_copy(n, 1).start()

            each_x(n, 1, start_x)

    def two_back(n):
        @pl.when(zz >= 2)
        def _():
            z_copy(n, 1).wait_recv()
            each_x(n, 0, start_x)

    def flag_x_copy(d, came=False):
        at = (x + NX - d) % NX if came else x
        return remote(
            flag_x.at[at],
            flag_x.at[at],
            fx_ss.at[d],
            fx_rs.at[d],
            (me, z * NX + (x + d) % NX),
        )

    def flag_z_copy(d, came=False):
        at = (z + NZ - d) % NZ if came else z
        return remote(
            flag_z.at[at],
            flag_z.at[at],
            fz_ss.at[d],
            fz_rs.at[d],
            (me, (z + d) % NZ * NX + x),
        )

    def pairs_came(n):
        @pl.loop(1, GROUPS)
        def _(d):
            kv_copy(n, d).wait_recv()

    ring_turn(1)
    pairs_came(0)
    marks_in = kva_recv[:, :, PIECE:].astype(f32)
    column = lax.broadcasted_iota(jnp.int32, (GROUPS, CAP, TOK), 2).astype(f32) + 1.0
    match = (marks_in == column).astype(f32)
    put = match.reshape(SLOTS, TOK).T.astype(bf16)
    place_pairs(0)
    worst = jnp.max((marks_in < 0.0).astype(f32).reshape(SLOTS, TOK), axis=0, keepdims=True)
    flag_x[x] = jnp.broadcast_to(worst, (CAP, TOK)).astype(bf16)
    for d in range(1, NX):
        flag_x_copy(d).start()
    put_low = both_halves(match[:, :LOW]).T.astype(bf16)

    ring_turn(2)
    pairs_came(1)
    place_pairs(1)
    start_queries(1)
    for d in range(1, NX):
        flag_x_copy(d, True).wait_recv()
    flag_z[z] = jnp.max(flag_x[...].astype(f32), axis=0).astype(bf16)
    for d in range(1, NZ):
        flag_z_copy(d).start()
    ring_turn(3)
    one_back(0)
    one_back(1)
    start_queries(2)
    ring_turn(4)
    two_back(0)
    start_queries(3)
    two_back(1)
    for d in range(1, NZ):
        flag_z_copy(d, True).wait_recv()
    flag_ref[0, 0] = jnp.max(flag_z[...].astype(f32)).astype(jnp.int32)
    for n in range(NY):
        sibling_came(n)

    tags_in = over[:, :, HK * HALF_WIDE :].astype(f32)
    mine = (me + 1).astype(f32)
    match_over = ((tags_in[:, :OVER] == column[:, :OVER]) & (tags_in[:, OVER:] == mine)).astype(f32)
    put_over = both_halves(match_over).T.astype(bf16)

    def store(j):
        cols = pl.ds(pl.multiple_of(j * WIDE, WIDE), WIDE)
        return pltpu.make_async_copy(out_buf.at[:, cols], out_hbm.at[0, :, cols], out_sem.at[j])

    ones = jnp.ones((SPAN, HD), bf16)

    def window_came(n):
        each_x(n, 2, came_x)

        @pl.when(has_last)
        def _():
            each_x(n, 1, came_x)

        @pl.when(zz >= 2)
        def _():
            each_x(n, 0, came_x)

    @pl.loop(0, HK)
    def _(j):
        pl.when(j == 0)(functools.partial(window_came, 0))
        pl.when(j == HK // 2)(functools.partial(window_came, 1))

        @pl.loop(1, GROUPS)
        def _(d):
            q_copy(j, d).wait_recv()

        cols = pl.ds(pl.multiple_of(j * HALF_WIDE, HALF_WIDE), HALF_WIDE)
        rows = contract(put_low, q_recv[j].reshape(SLOTS, HALF_WIDE), ((1,), (0,)))
        rows = rows + contract(put_over, over[:, :, cols].reshape(SLOTS, HALF_WIDE), ((1,), (0,)))
        rows = rows.astype(bf16)
        for h in range(HQ // HK):
            half, at = h // (HQ // HK // 2), h % (HQ // HK // 2)
            placed[h] = rows[half * TOK : (half + 1) * TOK, at * HD : (at + 1) * HD]
        key_cols = pl.ds(pl.multiple_of(j % 2 * HD, HD), HD)
        value_cols = pl.ds(pl.multiple_of(PIECE // 2 + j % 2 * HD, HD), HD)
        for h in range(HQ // HK):
            keys = window[j // 2, pl.ds(x, BACK + 1), :, key_cols].reshape(SPAN, HD)
            values = window[j // 2, pl.ds(x, BACK + 1), :, value_cols].reshape(SPAN, HD)
            scores = contract(placed[h], keys, ((1,), (1,))) + mask[...]
            top = jnp.max(scores, axis=1, keepdims=True)
            weights = jnp.exp2((scores - top) * FACTOR).astype(bf16)
            summed = contract(weights, jnp.concatenate([values, ones], axis=1), ((1,), (0,)))
            head_cols = pl.ds(pl.multiple_of((j * (HQ // HK) + h) * HD, HD), HD)
            out_buf[:, head_cols] = (summed[:, :HD] / summed[:, HD:]).astype(bf16)

        store(j).start()

    for j in range(HK):
        store(j).wait()

    @pl.loop(1, GROUPS)
    def _(d):
        for n in range(2):
            kv_copy(n, d).wait_send()
        for j in range(HK):
            q_copy(j, d).wait_send()

    for n in range(2):
        each_x(n, 2, sent_x)

        @pl.when(has_next)
        def _(n=n):
            z_copy(n, 2).wait_send()

        @pl.when(has_last)
        def _(n=n):
            each_x(n, 1, sent_x)

            @pl.when(has_next)
            def _():
                z_copy(n, 1).wait_send()

        @pl.when(zz >= 2)
        def _(n=n):
            each_x(n, 0, sent_x)

    for step in range(1, NY // 2 + 1):
        ring(step, 0).wait_send()
        if step < NY // 2:
            ring(step, 1).wait_send()
    for n in range(NY):
        sibling(n).wait_send()
    for d in range(1, NX):
        flag_x_copy(d).wait_send()
    for d in range(1, NZ):
        flag_z_copy(d).wait_send()


def compact(*operands):
    bf16 = jnp.bfloat16
    dma = pltpu.SemaphoreType.DMA
    vmem = pltpu.VMEM
    return pl.pallas_call(
        compact_kernel,
        out_shape=(
            jax.ShapeDtypeStruct((1, TOK, HQ * HD), bf16),
            jax.ShapeDtypeStruct((1, 1), jnp.int32),
        ),
        in_specs=[pl.BlockSpec(memory_space=pltpu.HBM)] * 5,
        out_specs=(pl.BlockSpec(memory_space=pl.ANY), pl.BlockSpec(memory_space=pltpu.SMEM)),
        scratch_shapes=[
            vmem((2 * HK, TOK, HALF_WIDE), bf16),
            vmem((1, TOK, PAIR), bf16),
            vmem((1, TOK), jnp.int32),
            vmem((1, TOK), jnp.int32),
            pltpu.SMEM((1, 2, 3), jnp.int32),
            vmem((HK, GROUPS, CAP, HALF_WIDE), bf16),
            vmem((HK, GROUPS, CAP, HALF_WIDE), bf16),
            vmem((GROUPS, CAP, PIECE + TOK), bf16),
            vmem((GROUPS, CAP, PIECE + TOK), bf16),
            vmem((GROUPS, CAP, PIECE), bf16),
            vmem((GROUPS, CAP, PIECE), bf16),
            vmem((GROUPS, CAP, HK * HALF_WIDE + TOK), bf16),
            vmem((2, 3 * NX, TOK, PIECE), bf16),
            vmem((TOK, SPAN), jnp.float32),
            vmem((HQ // HK, TOK, HD), bf16),
            vmem((TOK, HQ * HD), bf16),
            vmem((NX, CAP, TOK), bf16),
            vmem((NZ, CAP, TOK), bf16),
            dma((2 * HK + 4,)),
            dma((HK,)),
            dma((HK, GROUPS)),
            dma((HK, GROUPS)),
            dma((2, GROUPS)),
            dma((2, GROUPS)),
            dma((2, NY // 2 + 1)),
            dma((2, NY // 2 + 1)),
            dma((NY,)),
            dma((NY,)),
            dma((2, 3)),
            dma((2, 3)),
            dma((2, 3, NX)),
            dma((2, 3, NX)),
            dma((NX,)),
            dma((NX,)),
            dma((NZ,)),
            dma((NZ,)),
        ],
        compiler_params=pltpu.CompilerParams(
            collective_id=1, has_side_effects=True, vmem_limit_bytes=64 << 20
        ),
    )(*operands)


def local(*operands):
    result, crowded = compact(*operands)
    return lax.switch(crowded[0, 0], [lambda: result, lambda: padded(*operands)])


def solution(mesh):
    return jax.shard_map(
        local,
        mesh=mesh,
        in_specs=(
            P("grp", "seq", None),
            P("grp", "seq", None),
            P("grp", "seq"),
            P("grp", "seq"),
            P("grp", None, None),
        ),
        out_specs=P("grp", "seq", None),
        check_vma=False,
    )
```

```python
import functools
import math

import jax
import jax.numpy as jnp
from jax import lax
from jax.experimental import pallas as pl
from jax.experimental.pallas import tpu as pltpu
from jax.sharding import PartitionSpec as P

HQ = 32
HK = 4
HD = 128
TOK = 128
GROUPS = 16
CAP = 16
SLOTS = GROUPS * CAP
WIDE = HQ // HK * HD
PAIR = 2 * HK * HD
BACK = 8
SPAN = (BACK + 1) * TOK
NX = 4
HALF_ROWS = 4
NEGATIVE = -1e30
MESH = pl.DeviceIdType.MESH
FACTOR = HD ** (-0.5) * math.log2(math.e)


def remote(src, dst, send, recv, device):
    return pltpu.make_async_remote_copy(
        src_ref=src,
        dst_ref=dst,
        send_sem=send,
        recv_sem=recv,
        device_id=device,
        device_id_type=MESH,
    )


def contract(a, b, dims):
    return lax.dot_general(a, b, (dims, ((), ())), preferred_element_type=jnp.float32)


def padded_kernel(
    q_hbm,
    kv_hbm,
    group_hbm,
    slot_hbm,
    length_hbm,
    out_hbm,
    q_in,
    kv_ref,
    group_ref,
    slot_ref,
    length_ref,
    q_send,
    q_recv,
    kv_send,
    kv_recv,
    window,
    mask,
    placed,
    out_buf,
    in_sem,
    out_sem,
    q_ss,
    q_rs,
    kv_ss,
    kv_rs,
    z_ss,
    z_rs,
    x_ss,
    x_rs,
):
    me = lax.axis_index("grp")
    seq = lax.axis_index("seq")
    z = seq // NX
    x = seq % NX
    zz = z % HALF_ROWS
    has_next = zz < HALF_ROWS - 1
    has_last = zz > 0

    def load(j):
        cols = pl.ds(j * WIDE, WIDE)
        return pltpu.make_async_copy(q_hbm.at[0, :, cols], q_in.at[:, cols], in_sem.at[j])

    small = [
        pltpu.make_async_copy(source, target, in_sem.at[HK + n])
        for n, (source, target) in enumerate(
            [
                (group_hbm, group_ref),
                (slot_hbm, slot_ref),
                (kv_hbm, kv_ref),
                (length_hbm, length_ref),
            ]
        )
    ]
    for copy in small:
        copy.start()
    for j in range(HK):
        load(j).start()

    barrier = pltpu.get_barrier_semaphore()

    def greet(group, place):
        pl.semaphore_signal(barrier, inc=1, device_id=(group, place), device_id_type=MESH)

    for d in range(1, GROUPS):
        greet((me + d) % GROUPS, seq)
    for d in range(1, NX):
        greet(me, z * NX + (x + d) % NX)

    @pl.when(has_next)
    def _():
        greet(me, seq + NX)

    @pl.when(has_last)
    def _():
        greet(me, seq - NX)

    for copy in small:
        copy.wait()
    targets = group_ref[...]
    lane = lax.broadcasted_iota(jnp.int32, (TOK, TOK), 1)
    sub = lax.broadcasted_iota(jnp.int32, (TOK, TOK), 0)
    hits = lax.broadcasted_iota(jnp.int32, (GROUPS, TOK), 0) == targets
    before = (sub < lane).astype(jnp.float32).astype(jnp.bfloat16)
    hits_f = hits.astype(jnp.float32)
    ranks = contract(hits_f.astype(jnp.bfloat16), before, ((1,), (0,)))
    ranks = jnp.where(hits, ranks, -1.0)
    level = lax.broadcasted_iota(jnp.int32, (GROUPS, CAP, TOK), 1).astype(jnp.float32)
    pick_f = (ranks[:, None, :] == level).astype(jnp.float32).reshape(SLOTS, TOK)
    pick = pick_f.astype(jnp.bfloat16)
    marks = (pick_f * (slot_ref[...] + 1).astype(jnp.float32)).astype(jnp.bfloat16)
    slots = contract(marks, jnp.ones((TOK, TOK), jnp.bfloat16), ((1,), (0,)))
    kv_send[:, :, PAIR:] = slots.astype(jnp.bfloat16).reshape(GROUPS, CAP, TOK)
    kv_send[:, :, :PAIR] = (
        contract(pick, kv_ref[0], ((1,), (0,))).astype(jnp.bfloat16).reshape(GROUPS, CAP, PAIR)
    )

    pl.semaphore_wait(
        barrier, GROUPS - 1 + NX - 1 + has_next.astype(jnp.int32) + has_last.astype(jnp.int32)
    )

    def kv_copy(d):
        target = (me + d) % GROUPS
        return remote(
            kv_send.at[target], kv_recv.at[me], kv_ss.at[d], kv_rs.at[d], (target, seq)
        )

    @pl.loop(1, GROUPS)
    def _(d):
        kv_copy(d).start()

    kv_recv[me] = kv_send[me]

    def q_copy(j, d):
        target = (me + d) % GROUPS
        return remote(
            q_send.at[j, target], q_recv.at[j, me], q_ss.at[j, d], q_rs.at[j, d], (target, seq)
        )

    for j in range(HK):
        load(j).wait()
        q_send[j] = (
            contract(pick, q_in[:, j * WIDE : (j + 1) * WIDE], ((1,), (0,)))
            .astype(jnp.bfloat16)
            .reshape(GROUPS, CAP, WIDE)
        )

        @pl.loop(1, GROUPS)
        def _(d, j=j):
            q_copy(j, d).start()

        q_recv[j, me] = q_send[j, me]

    query = seq * TOK + lax.broadcasted_iota(jnp.int32, (TOK, SPAN), 0)
    key = (seq - BACK) * TOK + lax.broadcasted_iota(jnp.int32, (TOK, SPAN), 1)
    begin = jnp.zeros((TOK, SPAN), jnp.int32)
    bound = jnp.int32(0)
    for half in range(2):
        for n in range(3):
            bound = bound + length_ref[0, half, n]
            begin = jnp.where(query >= bound, bound, begin)
    mask[...] = jnp.where((key >= begin) & (key <= query), 0.0, NEGATIVE)

    @pl.when(zz == 0)
    def _():
        window[pl.ds(0, 2 * NX)] = jnp.zeros((2 * NX, TOK, PAIR), jnp.bfloat16)

    @pl.when(zz == 1)
    def _():
        window[pl.ds(0, NX)] = jnp.zeros((NX, TOK, PAIR), jnp.bfloat16)

    @pl.loop(1, GROUPS)
    def _(d):
        kv_copy(d).wait_recv()

    marks_in = kv_recv[:, :, PAIR:].reshape(SLOTS, TOK).astype(jnp.float32)
    column = lax.broadcasted_iota(jnp.int32, (SLOTS, TOK), 1).astype(jnp.float32) + 1.0
    put = (marks_in == column).astype(jnp.float32).T.astype(jnp.bfloat16)
    window[2 * NX + x] = contract(
        put, kv_recv[:, :, :PAIR].reshape(SLOTS, PAIR), ((1,), (0,))
    ).astype(jnp.bfloat16)

    def z_copy(plane):
        return remote(
            window.at[plane * NX + x],
            window.at[(plane - 1) * NX + x],
            z_ss.at[plane],
            z_rs.at[plane],
            (me, (seq + NX) % (NX * 8)),
        )

    def x_copy(plane, d):
        return remote(
            window.at[plane * NX + x],
            window.at[plane * NX + x],
            x_ss.at[plane, d],
            x_rs.at[plane, d],
            (me, z * NX + (x + d) % NX),
        )

    def x_wait(plane, d):
        source = (x + NX - d) % NX
        return remote(
            window.at[plane * NX + source],
            window.at[plane * NX + source],
            x_ss.at[plane, d],
            x_rs.at[plane, d],
            (me, z * NX + (x + d) % NX),
        )

    def each_x(plane, act, sending):
        for d in range(1, NX):
            wraps = x + d >= NX if sending else x - d < 0
            if plane == 1:
                act(plane, d)
            else:
                pl.when(wraps if plane == 0 else jnp.logical_not(wraps))(
                    functools.partial(act, plane, d)
                )

    def start_x(plane, d):
        x_copy(plane, d).start()

    def sent_x(plane, d):
        x_copy(plane, d).wait_send()

    def came_x(plane, d):
        x_wait(plane, d).wait_recv()

    @pl.when(has_next)
    def _():
        z_copy(2).start()

    each_x(2, start_x, True)

    @pl.when(has_last)
    def _():
        z_copy(2).wait_recv()

        @pl.when(has_next)
        def _():
            z_copy(1).start()

        each_x(1, start_x, True)

    @pl.when(zz >= 2)
    def _():
        z_copy(1).wait_recv()
        each_x(0, start_x, True)

    each_x(2, came_x, False)

    @pl.when(has_last)
    def _():
        each_x(1, came_x, False)

    @pl.when(zz >= 2)
    def _():
        each_x(0, came_x, False)

    def store(j):
        cols = pl.ds(pl.multiple_of(j * WIDE, WIDE), WIDE)
        return pltpu.make_async_copy(out_buf.at[:, cols], out_hbm.at[0, :, cols], out_sem.at[j])

    ones = jnp.ones((SPAN, HD), jnp.bfloat16)

    @pl.loop(0, HK)
    def _(j):
        @pl.loop(1, GROUPS)
        def _(d):
            q_copy(j, d).wait_recv()

        rows = contract(put, q_recv[j].reshape(SLOTS, WIDE), ((1,), (0,))).astype(jnp.bfloat16)
        for h in range(HQ // HK):
            placed[h] = rows[:, h * HD : (h + 1) * HD]
        key_cols = pl.ds(pl.multiple_of(j * HD, HD), HD)
        value_cols = pl.ds(pl.multiple_of((HK + j) * HD, HD), HD)

        for h in range(HQ // HK):
            keys = window[pl.ds(x, BACK + 1), :, key_cols].reshape(SPAN, HD)
            values = window[pl.ds(x, BACK + 1), :, value_cols].reshape(SPAN, HD)
            scores = contract(placed[h], keys, ((1,), (1,))) + mask[...]
            top = jnp.max(scores, axis=1, keepdims=True)
            weights = jnp.exp2((scores - top) * FACTOR).astype(jnp.bfloat16)
            summed = contract(weights, jnp.concatenate([values, ones], axis=1), ((1,), (0,)))
            cols = pl.ds(pl.multiple_of((j * (HQ // HK) + h) * HD, HD), HD)
            out_buf[:, cols] = (summed[:, :HD] / summed[:, HD:]).astype(jnp.bfloat16)

        store(j).start()

    for j in range(HK):
        store(j).wait()

    @pl.loop(1, GROUPS)
    def _(d):
        kv_copy(d).wait_send()
        for j in range(HK):
            q_copy(j, d).wait_send()

    each_x(2, sent_x, True)

    @pl.when(has_next)
    def _():
        z_copy(2).wait_send()

    @pl.when(has_last)
    def _():
        each_x(1, sent_x, True)

        @pl.when(has_next)
        def _():
            z_copy(1).wait_send()

    @pl.when(zz >= 2)
    def _():
        each_x(0, sent_x, True)


def padded(queries, keys_values, route_group, route_slot, doc_lengths):
    bf16 = jnp.bfloat16
    dma = pltpu.SemaphoreType.DMA
    return pl.pallas_call(
        padded_kernel,
        out_shape=jax.ShapeDtypeStruct((1, TOK, HQ * HD), bf16),
        in_specs=[
            pl.BlockSpec(memory_space=pltpu.HBM),
            pl.BlockSpec(memory_space=pltpu.HBM),
            pl.BlockSpec(memory_space=pltpu.HBM),
            pl.BlockSpec(memory_space=pltpu.HBM),
            pl.BlockSpec(memory_space=pltpu.HBM),
        ],
        out_specs=pl.BlockSpec(memory_space=pl.ANY),
        scratch_shapes=[
            pltpu.VMEM((TOK, HQ * HD), bf16),
            pltpu.VMEM((1, TOK, PAIR), bf16),
            pltpu.VMEM((1, TOK), jnp.int32),
            pltpu.VMEM((1, TOK), jnp.int32),
            pltpu.SMEM((1, 2, 3), jnp.int32),
            pltpu.VMEM((HK, GROUPS, CAP, WIDE), bf16),
            pltpu.VMEM((HK, GROUPS, CAP, WIDE), bf16),
            pltpu.VMEM((GROUPS, CAP, PAIR + TOK), bf16),
            pltpu.VMEM((GROUPS, CAP, PAIR + TOK), bf16),
            pltpu.VMEM((3 * NX, TOK, PAIR), bf16),
            pltpu.VMEM((TOK, SPAN), jnp.float32),
            pltpu.VMEM((HQ // HK, TOK, HD), bf16),
            pltpu.VMEM((TOK, HQ * HD), bf16),
            dma((HK + 4,)),
            dma((HK,)),
            dma((HK, GROUPS)),
            dma((HK, GROUPS)),
            dma((GROUPS,)),
            dma((GROUPS,)),
            dma((3,)),
            dma((3,)),
            dma((3, NX)),
            dma((3, NX)),
        ],
        compiler_params=pltpu.CompilerParams(
            collective_id=0, has_side_effects=True, vmem_limit_bytes=64 << 20
        ),
    )(queries, keys_values, route_group, route_slot, doc_lengths)


LOW = 8
OVER = 8
HALF_WIDE = WIDE // 2
PIECE = PAIR // 2
NY = GROUPS // 2
NZ = 2 * HALF_ROWS


def both_halves(one):
    none = jnp.zeros_like(one)
    left = jnp.concatenate([one, none], axis=1)
    right = jnp.concatenate([none, one], axis=1)
    lanes = one.shape[2]
    return jnp.concatenate([left.reshape(-1, lanes), right.reshape(-1, lanes)], axis=1)


def compact_kernel(
    q_hbm,
    kv_hbm,
    group_hbm,
    slot_hbm,
    length_hbm,
    out_hbm,
    flag_ref,
    q_in,
    kv_ref,
    group_ref,
    slot_ref,
    length_ref,
    q_send,
    q_recv,
    kva_send,
    kva_recv,
    kvb_send,
    kvb_recv,
    over,
    window,
    mask,
    placed,
    out_buf,
    flag_x,
    flag_z,
    in_sem,
    out_sem,
    q_ss,
    q_rs,
    kv_ss,
    kv_rs,
    ring_ss,
    ring_rs,
    sib_ss,
    sib_rs,
    z_ss,
    z_rs,
    x_ss,
    x_rs,
    fx_ss,
    fx_rs,
    fz_ss,
    fz_rs,
):
    bf16 = jnp.bfloat16
    f32 = jnp.float32
    me = lax.axis_index("grp")
    seq = lax.axis_index("seq")
    z = seq // NX
    x = seq % NX
    zz = z % HALF_ROWS
    y = me // 2
    core = me % 2
    has_next = zz < HALF_ROWS - 1
    has_last = zz > 0

    small = [
        pltpu.make_async_copy(source, target, in_sem.at[2 * HK + n])
        for n, (source, target) in enumerate(
            [
                (group_hbm, group_ref),
                (slot_hbm, slot_ref),
                (kv_hbm, kv_ref),
                (length_hbm, length_ref),
            ]
        )
    ]
    loads = [
        pltpu.make_async_copy(
            q_hbm.at[0, :, pl.ds(n * HALF_WIDE, HALF_WIDE)], q_in.at[n], in_sem.at[n]
        )
        for n in range(2 * HK)
    ]
    for copy in small + loads:
        copy.start()

    barrier = pltpu.get_barrier_semaphore()

    def greet(group, place):
        pl.semaphore_signal(barrier, inc=1, device_id=(group, place), device_id_type=MESH)

    for d in range(1, GROUPS):
        greet((me + d) % GROUPS, seq)
    for d in range(1, NX):
        greet(me, z * NX + (x + d) % NX)
    for d in range(1, NZ):
        greet(me, (z + d) % NZ * NX + x)

    for copy in small:
        copy.wait()
    targets = group_ref[...]
    lane = lax.broadcasted_iota(jnp.int32, (TOK, TOK), 1)
    sub = lax.broadcasted_iota(jnp.int32, (TOK, TOK), 0)
    hits = lax.broadcasted_iota(jnp.int32, (GROUPS, TOK), 0) == targets
    before = (sub < lane).astype(f32).astype(bf16)
    all_ones = jnp.ones((TOK, TOK), bf16)
    ranks = contract(hits.astype(f32).astype(bf16), before, ((1,), (0,)))
    ranks = jnp.where(hits, ranks, -1.0)
    level = lax.broadcasted_iota(jnp.int32, (GROUPS, CAP, TOK), 1).astype(f32)
    pick_three = (ranks[:, None, :] == level).astype(f32)
    pick_f = pick_three.reshape(SLOTS, TOK)
    pick = pick_f.astype(bf16)
    places = (slot_ref[...] + 1).astype(f32)
    beyond = jnp.sum((ranks >= LOW).astype(f32), axis=0, keepdims=True)
    order = contract(jnp.broadcast_to(beyond, (OVER, TOK)).astype(bf16), before, ((1,), (0,)))
    row = lax.broadcasted_iota(jnp.int32, (OVER, TOK), 0).astype(f32)
    extra = jnp.where((order == row) & (beyond > 0.0), 1.0, 0.0)
    crowded = jnp.sum(beyond, axis=1, keepdims=True) > OVER
    marks = contract((pick_f * places).astype(bf16), all_ones, ((1,), (0,)))
    marks = jnp.where(crowded, -1.0, marks)
    kva_send[:, :, PIECE:] = marks.astype(bf16).reshape(GROUPS, CAP, TOK)

    sends = [kva_send, kvb_send]
    recvs = [kva_recv, kvb_recv]

    def pack_pairs(n):
        for part in range(2):
            cols = kv_ref[0, :, part * PIECE + n * PIECE // 2 : part * PIECE + (n + 1) * PIECE // 2]
            sends[n][:, :, part * PIECE // 2 : (part + 1) * PIECE // 2] = (
                contract(pick, cols, ((1,), (0,))).astype(bf16).reshape(GROUPS, CAP, PIECE // 2)
            )

    def partner(d):
        return (y + d // 2) % NY * 2 + (core + d % 2) % 2

    def far_first(act):
        @pl.loop(0, NY - 1)
        def _(i):
            away = NY // 2 + i // 2 * (1 - i % 2) - (i + 1) // 2 * (i % 2)
            act(2 * away)
            act(2 * away + 1)

        act(1)

    def kv_copy(n, d):
        target = partner(d)
        return remote(
            sends[n].at[target], recvs[n].at[me], kv_ss.at[n, d], kv_rs.at[n, d], (target, seq)
        )

    def start_pairs(n):
        far_first(lambda d: kv_copy(n, d).start())
        recvs[n][me] = sends[n][me]

    high = both_halves(extra[None]).astype(bf16)
    for j in range(HK):
        loads[2 * j].wait()
        loads[2 * j + 1].wait()
        halves = q_in[2 * j : 2 * j + 2].reshape(2 * TOK, HALF_WIDE)
        over[me, :, j * HALF_WIDE : (j + 1) * HALF_WIDE] = contract(
            high, halves, ((1,), (0,))
        ).astype(bf16)
    tags = jnp.concatenate([extra * places, extra * (targets + 1).astype(f32)], axis=0)
    over[me, :, HK * HALF_WIDE :] = contract(tags.astype(bf16), all_ones, ((1,), (0,))).astype(bf16)
    pack_pairs(0)

    turn = 1 - 2 * core

    def on_ring(at):
        return (at + 2 * NY) % NY * 2 + core

    def on_sibling(at):
        return (at + 2 * NY) % NY * 2 + 1 - core

    def ring(step, way):
        sign = turn if way == 0 else -turn
        block = on_ring(y - sign * (step - 1))
        return remote(
            over.at[block],
            over.at[block],
            ring_ss.at[way, step],
            ring_rs.at[way, step],
            (on_ring(y + sign), seq),
        )

    def ring_came(step, way):
        sign = turn if way == 0 else -turn
        block = on_ring(y - sign * step)
        remote(
            over.at[block],
            over.at[block],
            ring_ss.at[way, step],
            ring_rs.at[way, step],
            (on_ring(y + sign), seq),
        ).wait_recv()

    def sibling(n):
        block = on_ring(y - turn * n if n <= NY // 2 else y + turn * (n - NY // 2))
        return remote(
            over.at[block], over.at[block], sib_ss.at[n], sib_rs.at[n], (on_sibling(y), seq)
        )

    def sibling_came(n):
        block = on_sibling(y + turn * n if n <= NY // 2 else y - turn * (n - NY // 2))
        remote(
            over.at[block], over.at[block], sib_ss.at[n], sib_rs.at[n], (on_sibling(y), seq)
        ).wait_recv()

    def ring_turn(step):
        ring_came(step, 0)
        if step < NY // 2:
            ring(step + 1, 0).start()
            ring_came(step, 1)
            if step + 1 < NY // 2:
                ring(step + 1, 1).start()
            sibling(NY // 2 + step).start()
        sibling(step).start()

    pl.semaphore_wait(barrier, GROUPS - 1 + NX - 1 + NZ - 1)
    ring(1, 0).start()
    ring(1, 1).start()
    start_pairs(0)
    sibling(0).start()
    pack_pairs(1)
    start_pairs(1)

    low = both_halves(pick_three[:, :LOW]).astype(bf16)
    for j in range(HK):
        halves = q_in[2 * j : 2 * j + 2].reshape(2 * TOK, HALF_WIDE)
        q_send[j] = (
            contract(low, halves, ((1,), (0,))).astype(bf16).reshape(GROUPS, CAP, HALF_WIDE)
        )

    def q_copy(j, d):
        target = partner(d)
        return remote(
            q_send.at[j, target], q_recv.at[j, me], q_ss.at[j, d], q_rs.at[j, d], (target, seq)
        )

    def start_queries(j):
        far_first(lambda d: q_copy(j, d).start())
        q_recv[j, me] = q_send[j, me]

    query = seq * TOK + lax.broadcasted_iota(jnp.int32, (TOK, SPAN), 0)
    key = (seq - BACK) * TOK + lax.broadcasted_iota(jnp.int32, (TOK, SPAN), 1)
    begin = jnp.zeros((TOK, SPAN), jnp.int32)
    bound = jnp.int32(0)
    for half in range(2):
        for n in range(3):
            bound = bound + length_ref[0, half, n]
            begin = jnp.where(query >= bound, bound, begin)
    mask[...] = jnp.where((key >= begin) & (key <= query), 0.0, NEGATIVE)

    @pl.when(zz == 0)
    def _():
        window[:, pl.ds(0, 2 * NX)] = jnp.zeros((2, 2 * NX, TOK, PIECE), bf16)

    @pl.when(zz == 1)
    def _():
        window[:, pl.ds(0, NX)] = jnp.zeros((2, NX, TOK, PIECE), bf16)

    def z_copy(n, plane):
        return remote(
            window.at[n, plane * NX + x],
            window.at[n, (plane - 1) * NX + x],
            z_ss.at[n, plane],
            z_rs.at[n, plane],
            (me, (seq + NX) % (NX * NZ)),
        )

    def x_copy(n, plane, d, came=False):
        at = plane * NX + ((x + NX - d) % NX if came else x)
        return remote(
            window.at[n, at],
            window.at[n, at],
            x_ss.at[n, plane, d],
            x_rs.at[n, plane, d],
            (me, z * NX + (x + d) % NX),
        )

    def start_x(n, plane, d):
        x_copy(n, plane, d).start()

    def sent_x(n, plane, d):
        x_copy(n, plane, d).wait_send()

    def came_x(n, plane, d):
        x_copy(n, plane, d, True).wait_recv()

    def each_x(n, plane, act, steps):
        for d in steps:
            wraps = x - d < 0 if act is came_x else x + d >= NX
            if plane == 1:
                act(n, plane, d)
            else:
                pl.when(wraps if plane == 0 else jnp.logical_not(wraps))(
                    functools.partial(act, n, plane, d)
                )

    beside = (1, NX - 1)
    inner = (x == 1) | (x == 2)

    def pass_on(n, plane, way, slot):
        at = plane * NX + (x + NX - way) % NX
        return remote(
            window.at[n, at],
            window.at[n, at],
            x_ss.at[n, plane, slot],
            x_rs.at[n, plane, 2],
            (me, z * NX + (x + NX + way) % NX),
        )

    def each_pass(n, plane, act):
        if plane == 1:

            @pl.when(jnp.logical_not(inner))
            def _():
                act(pass_on(n, plane, 1, 0))
                act(pass_on(n, plane, -1, 2))

        else:

            @pl.when(inner)
            def _():
                act(pass_on(n, plane, 1 if plane == 2 else -1, 2))

    def forward(n, plane):
        def go():
            each_x(n, plane, came_x, beside)
            each_pass(n, plane, lambda copy: copy.start())

        if plane == 2:
            go()
        else:
            pl.when(has_last if plane == 1 else zz >= 2)(go)

    def place_pairs(n):
        window[n, 2 * NX + x] = contract(
            put, recvs[n][:, :, :PIECE].reshape(SLOTS, PIECE), ((1,), (0,))
        ).astype(bf16)

        @pl.when(has_next)
        def _():
            z_copy(n, 2).start()

        each_x(n, 2, start_x, beside)

    def one_back(n):
        @pl.when(has_last)
        def _():
            z_copy(n, 2).wait_recv()

            @pl.when(has_next)
            def _():
                z_copy(n, 1).start()

            each_x(n, 1, start_x, beside)

    def two_back(n):
        @pl.when(zz >= 2)
        def _():
            z_copy(n, 1).wait_recv()
            each_x(n, 0, start_x, beside)

    def flag_x_copy(d, came=False):
        at = (x + NX - d) % NX if came else x
        return remote(
            flag_x.at[at],
            flag_x.at[at],
            fx_ss.at[d],
            fx_rs.at[d],
            (me, z * NX + (x + d) % NX),
        )

    def flag_z_copy(d, came=False):
        at = (z + NZ - d) % NZ if came else z
        return remote(
            flag_z.at[at],
            flag_z.at[at],
            fz_ss.at[d],
            fz_rs.at[d],
            (me, (z + d) % NZ * NX + x),
        )

    def pairs_came(n):
        @pl.loop(1, GROUPS)
        def _(d):
            kv_copy(n, d).wait_recv()

    ring_turn(1)
    start_queries(0)
    pairs_came(0)
    marks_in = kva_recv[:, :, PIECE:].astype(f32)
    column = lax.broadcasted_iota(jnp.int32, (GROUPS, CAP, TOK), 2).astype(f32) + 1.0
    match = (marks_in == column).astype(f32)
    put = match.reshape(SLOTS, TOK).T.astype(bf16)
    place_pairs(0)
    worst = jnp.max((marks_in < 0.0).astype(f32).reshape(SLOTS, TOK), axis=0, keepdims=True)
    flag_x[x] = jnp.broadcast_to(worst, (CAP, TOK)).astype(bf16)
    for d in range(1, NX):
        flag_x_copy(d).start()
    put_low = both_halves(match[:, :LOW]).T.astype(bf16)

    ring_turn(2)
    start_queries(1)
    pairs_came(1)
    place_pairs(1)
    forward(0, 2)
    one_back(0)
    for d in range(1, NX):
        flag_x_copy(d, True).wait_recv()
    flag_z[z] = jnp.max(flag_x[...].astype(f32), axis=0).astype(bf16)
    for d in range(1, NZ):
        flag_z_copy(d).start()
    ring_turn(3)
    start_queries(2)
    one_back(1)
    two_back(0)
    forward(1, 2)
    forward(0, 1)
    two_back(1)
    ring_turn(4)
    start_queries(3)
    forward(0, 0)
    forward(1, 1)
    forward(1, 0)
    for d in range(1, NZ):
        flag_z_copy(d, True).wait_recv()
    flag_ref[0, 0] = jnp.max(flag_z[...].astype(f32)).astype(jnp.int32)
    for n in range(NY):
        sibling_came(n)

    tags_in = over[:, :, HK * HALF_WIDE :].astype(f32)
    mine = (me + 1).astype(f32)
    match_over = ((tags_in[:, :OVER] == column[:, :OVER]) & (tags_in[:, OVER:] == mine)).astype(f32)
    put_over = both_halves(match_over).T.astype(bf16)

    def store(j):
        cols = pl.ds(pl.multiple_of(j * WIDE, WIDE), WIDE)
        return pltpu.make_async_copy(out_buf.at[:, cols], out_hbm.at[0, :, cols], out_sem.at[j])

    ones = jnp.ones((SPAN, HD), bf16)

    def window_came(n):
        each_x(n, 2, came_x, (2,))

        @pl.when(has_last)
        def _():
            each_x(n, 1, came_x, (2,))

        @pl.when(zz >= 2)
        def _():
            each_x(n, 0, came_x, (2,))

    @pl.loop(0, HK)
    def _(j):
        pl.when(j == 0)(functools.partial(window_came, 0))
        pl.when(j == HK // 2)(functools.partial(window_came, 1))

        @pl.loop(1, GROUPS)
        def _(d):
            q_copy(j, d).wait_recv()

        cols = pl.ds(pl.multiple_of(j * HALF_WIDE, HALF_WIDE), HALF_WIDE)
        rows = contract(put_low, q_recv[j].reshape(SLOTS, HALF_WIDE), ((1,), (0,)))
        rows = rows + contract(put_over, over[:, :, cols].reshape(SLOTS, HALF_WIDE), ((1,), (0,)))
        rows = rows.astype(bf16)
        for h in range(HQ // HK):
            half, at = h // (HQ // HK // 2), h % (HQ // HK // 2)
            placed[h] = rows[half * TOK : (half + 1) * TOK, at * HD : (at + 1) * HD]
        key_cols = pl.ds(pl.multiple_of(j % 2 * HD, HD), HD)
        value_cols = pl.ds(pl.multiple_of(PIECE // 2 + j % 2 * HD, HD), HD)
        for h in range(HQ // HK):
            keys = window[j // 2, pl.ds(x, BACK + 1), :, key_cols].reshape(SPAN, HD)
            values = window[j // 2, pl.ds(x, BACK + 1), :, value_cols].reshape(SPAN, HD)
            scores = contract(placed[h], keys, ((1,), (1,))) + mask[...]
            top = jnp.max(scores, axis=1, keepdims=True)
            weights = jnp.exp2((scores - top) * FACTOR).astype(bf16)
            summed = contract(weights, jnp.concatenate([values, ones], axis=1), ((1,), (0,)))
            head_cols = pl.ds(pl.multiple_of((j * (HQ // HK) + h) * HD, HD), HD)
            out_buf[:, head_cols] = (summed[:, :HD] / summed[:, HD:]).astype(bf16)

        store(j).start()

    for j in range(HK):
        store(j).wait()

    @pl.loop(1, GROUPS)
    def _(d):
        for n in range(2):
            kv_copy(n, d).wait_send()
        for j in range(HK):
            q_copy(j, d).wait_send()

    for n in range(2):
        each_x(n, 2, sent_x, beside)
        each_pass(n, 2, lambda copy: copy.wait_send())

        @pl.when(has_next)
        def _(n=n):
            z_copy(n, 2).wait_send()

        @pl.when(has_last)
        def _(n=n):
            each_x(n, 1, sent_x, beside)
            each_pass(n, 1, lambda copy: copy.wait_send())

            @pl.when(has_next)
            def _():
                z_copy(n, 1).wait_send()

        @pl.when(zz >= 2)
        def _(n=n):
            each_x(n, 0, sent_x, beside)
            each_pass(n, 0, lambda copy: copy.wait_send())

    for step in range(1, NY // 2 + 1):
        ring(step, 0).wait_send()
        if step < NY // 2:
            ring(step, 1).wait_send()
    for n in range(NY):
        sibling(n).wait_send()
    for d in range(1, NX):
        flag_x_copy(d).wait_send()
    for d in range(1, NZ):
        flag_z_copy(d).wait_send()


def compact(*operands):
    bf16 = jnp.bfloat16
    dma = pltpu.SemaphoreType.DMA
    vmem = pltpu.VMEM
    return pl.pallas_call(
        compact_kernel,
        out_shape=(
            jax.ShapeDtypeStruct((1, TOK, HQ * HD), bf16),
            jax.ShapeDtypeStruct((1, 1), jnp.int32),
        ),
        in_specs=[pl.BlockSpec(memory_space=pltpu.HBM)] * 5,
        out_specs=(pl.BlockSpec(memory_space=pl.ANY), pl.BlockSpec(memory_space=pltpu.SMEM)),
        scratch_shapes=[
            vmem((2 * HK, TOK, HALF_WIDE), bf16),
            vmem((1, TOK, PAIR), bf16),
            vmem((1, TOK), jnp.int32),
            vmem((1, TOK), jnp.int32),
            pltpu.SMEM((1, 2, 3), jnp.int32),
            vmem((HK, GROUPS, CAP, HALF_WIDE), bf16),
            vmem((HK, GROUPS, CAP, HALF_WIDE), bf16),
            vmem((GROUPS, CAP, PIECE + TOK), bf16),
            vmem((GROUPS, CAP, PIECE + TOK), bf16),
            vmem((GROUPS, CAP, PIECE), bf16),
            vmem((GROUPS, CAP, PIECE), bf16),
            vmem((GROUPS, CAP, HK * HALF_WIDE + TOK), bf16),
            vmem((2, 3 * NX, TOK, PIECE), bf16),
            vmem((TOK, SPAN), jnp.float32),
            vmem((HQ // HK, TOK, HD), bf16),
            vmem((TOK, HQ * HD), bf16),
            vmem((NX, CAP, TOK), bf16),
            vmem((NZ, CAP, TOK), bf16),
            dma((2 * HK + 4,)),
            dma((HK,)),
            dma((HK, GROUPS)),
            dma((HK, GROUPS)),
            dma((2, GROUPS)),
            dma((2, GROUPS)),
            dma((2, NY // 2 + 1)),
            dma((2, NY // 2 + 1)),
            dma((NY,)),
            dma((NY,)),
            dma((2, 3)),
            dma((2, 3)),
            dma((2, 3, NX)),
            dma((2, 3, NX)),
            dma((NX,)),
            dma((NX,)),
            dma((NZ,)),
            dma((NZ,)),
        ],
        compiler_params=pltpu.CompilerParams(
            collective_id=1, has_side_effects=True, vmem_limit_bytes=64 << 20
        ),
    )(*operands)


def local(*operands):
    result, crowded = compact(*operands)
    return lax.switch(crowded[0, 0], [lambda: result, lambda: padded(*operands)])


def solution(mesh):
    return jax.shard_map(
        local,
        mesh=mesh,
        in_specs=(
            P("grp", "seq", None),
            P("grp", "seq", None),
            P("grp", "seq"),
            P("grp", "seq"),
            P("grp", None, None),
        ),
        out_specs=P("grp", "seq", None),
        check_vma=False,
    )
```

```python
import functools
import math

import jax
import jax.numpy as jnp
from jax import lax
from jax.experimental import pallas as pl
from jax.experimental.pallas import tpu as pltpu
from jax.sharding import PartitionSpec as P

HQ = 32
HK = 4
HD = 128
TOK = 128
GROUPS = 16
CAP = 16
SLOTS = GROUPS * CAP
WIDE = HQ // HK * HD
PAIR = 2 * HK * HD
BACK = 8
SPAN = (BACK + 1) * TOK
NX = 4
HALF_ROWS = 4
NEGATIVE = -1e30
MESH = pl.DeviceIdType.MESH
FACTOR = HD ** (-0.5) * math.log2(math.e)


def remote(src, dst, send, recv, device):
    return pltpu.make_async_remote_copy(
        src_ref=src,
        dst_ref=dst,
        send_sem=send,
        recv_sem=recv,
        device_id=device,
        device_id_type=MESH,
    )


def contract(a, b, dims):
    return lax.dot_general(a, b, (dims, ((), ())), preferred_element_type=jnp.float32)


def padded_kernel(
    q_hbm,
    kv_hbm,
    group_hbm,
    slot_hbm,
    length_hbm,
    out_hbm,
    q_in,
    kv_ref,
    group_ref,
    slot_ref,
    length_ref,
    q_send,
    q_recv,
    kv_send,
    kv_recv,
    window,
    mask,
    placed,
    out_buf,
    in_sem,
    out_sem,
    q_ss,
    q_rs,
    kv_ss,
    kv_rs,
    z_ss,
    z_rs,
    x_ss,
    x_rs,
):
    me = lax.axis_index("grp")
    seq = lax.axis_index("seq")
    z = seq // NX
    x = seq % NX
    zz = z % HALF_ROWS
    has_next = zz < HALF_ROWS - 1
    has_last = zz > 0

    def load(j):
        cols = pl.ds(j * WIDE, WIDE)
        return pltpu.make_async_copy(q_hbm.at[0, :, cols], q_in.at[:, cols], in_sem.at[j])

    small = [
        pltpu.make_async_copy(source, target, in_sem.at[HK + n])
        for n, (source, target) in enumerate(
            [
                (group_hbm, group_ref),
                (slot_hbm, slot_ref),
                (kv_hbm, kv_ref),
                (length_hbm, length_ref),
            ]
        )
    ]
    for copy in small:
        copy.start()
    for j in range(HK):
        load(j).start()

    barrier = pltpu.get_barrier_semaphore()

    def greet(group, place):
        pl.semaphore_signal(barrier, inc=1, device_id=(group, place), device_id_type=MESH)

    for d in range(1, GROUPS):
        greet((me + d) % GROUPS, seq)
    for d in range(1, NX):
        greet(me, z * NX + (x + d) % NX)

    @pl.when(has_next)
    def _():
        greet(me, seq + NX)

    @pl.when(has_last)
    def _():
        greet(me, seq - NX)

    for copy in small:
        copy.wait()
    targets = group_ref[...]
    lane = lax.broadcasted_iota(jnp.int32, (TOK, TOK), 1)
    sub = lax.broadcasted_iota(jnp.int32, (TOK, TOK), 0)
    hits = lax.broadcasted_iota(jnp.int32, (GROUPS, TOK), 0) == targets
    before = (sub < lane).astype(jnp.float32).astype(jnp.bfloat16)
    hits_f = hits.astype(jnp.float32)
    ranks = contract(hits_f.astype(jnp.bfloat16), before, ((1,), (0,)))
    ranks = jnp.where(hits, ranks, -1.0)
    level = lax.broadcasted_iota(jnp.int32, (GROUPS, CAP, TOK), 1).astype(jnp.float32)
    pick_f = (ranks[:, None, :] == level).astype(jnp.float32).reshape(SLOTS, TOK)
    pick = pick_f.astype(jnp.bfloat16)
    marks = (pick_f * (slot_ref[...] + 1).astype(jnp.float32)).astype(jnp.bfloat16)
    slots = contract(marks, jnp.ones((TOK, TOK), jnp.bfloat16), ((1,), (0,)))
    kv_send[:, :, PAIR:] = slots.astype(jnp.bfloat16).reshape(GROUPS, CAP, TOK)
    kv_send[:, :, :PAIR] = (
        contract(pick, kv_ref[0], ((1,), (0,))).astype(jnp.bfloat16).reshape(GROUPS, CAP, PAIR)
    )

    pl.semaphore_wait(
        barrier, GROUPS - 1 + NX - 1 + has_next.astype(jnp.int32) + has_last.astype(jnp.int32)
    )

    def kv_copy(d):
        target = (me + d) % GROUPS
        return remote(
            kv_send.at[target], kv_recv.at[me], kv_ss.at[d], kv_rs.at[d], (target, seq)
        )

    @pl.loop(1, GROUPS)
    def _(d):
        kv_copy(d).start()

    kv_recv[me] = kv_send[me]

    def q_copy(j, d):
        target = (me + d) % GROUPS
        return remote(
            q_send.at[j, target], q_recv.at[j, me], q_ss.at[j, d], q_rs.at[j, d], (target, seq)
        )

    for j in range(HK):
        load(j).wait()
        q_send[j] = (
            contract(pick, q_in[:, j * WIDE : (j + 1) * WIDE], ((1,), (0,)))
            .astype(jnp.bfloat16)
            .reshape(GROUPS, CAP, WIDE)
        )

        @pl.loop(1, GROUPS)
        def _(d, j=j):
            q_copy(j, d).start()

        q_recv[j, me] = q_send[j, me]

    query = seq * TOK + lax.broadcasted_iota(jnp.int32, (TOK, SPAN), 0)
    key = (seq - BACK) * TOK + lax.broadcasted_iota(jnp.int32, (TOK, SPAN), 1)
    begin = jnp.zeros((TOK, SPAN), jnp.int32)
    bound = jnp.int32(0)
    for half in range(2):
        for n in range(3):
            bound = bound + length_ref[0, half, n]
            begin = jnp.where(query >= bound, bound, begin)
    mask[...] = jnp.where((key >= begin) & (key <= query), 0.0, NEGATIVE)

    @pl.when(zz == 0)
    def _():
        window[pl.ds(0, 2 * NX)] = jnp.zeros((2 * NX, TOK, PAIR), jnp.bfloat16)

    @pl.when(zz == 1)
    def _():
        window[pl.ds(0, NX)] = jnp.zeros((NX, TOK, PAIR), jnp.bfloat16)

    @pl.loop(1, GROUPS)
    def _(d):
        kv_copy(d).wait_recv()

    marks_in = kv_recv[:, :, PAIR:].reshape(SLOTS, TOK).astype(jnp.float32)
    column = lax.broadcasted_iota(jnp.int32, (SLOTS, TOK), 1).astype(jnp.float32) + 1.0
    put = (marks_in == column).astype(jnp.float32).T.astype(jnp.bfloat16)
    window[2 * NX + x] = contract(
        put, kv_recv[:, :, :PAIR].reshape(SLOTS, PAIR), ((1,), (0,))
    ).astype(jnp.bfloat16)

    def z_copy(plane):
        return remote(
            window.at[plane * NX + x],
            window.at[(plane - 1) * NX + x],
            z_ss.at[plane],
            z_rs.at[plane],
            (me, (seq + NX) % (NX * 8)),
        )

    def x_copy(plane, d):
        return remote(
            window.at[plane * NX + x],
            window.at[plane * NX + x],
            x_ss.at[plane, d],
            x_rs.at[plane, d],
            (me, z * NX + (x + d) % NX),
        )

    def x_wait(plane, d):
        source = (x + NX - d) % NX
        return remote(
            window.at[plane * NX + source],
            window.at[plane * NX + source],
            x_ss.at[plane, d],
            x_rs.at[plane, d],
            (me, z * NX + (x + d) % NX),
        )

    def each_x(plane, act, sending):
        for d in range(1, NX):
            wraps = x + d >= NX if sending else x - d < 0
            if plane == 1:
                act(plane, d)
            else:
                pl.when(wraps if plane == 0 else jnp.logical_not(wraps))(
                    functools.partial(act, plane, d)
                )

    def start_x(plane, d):
        x_copy(plane, d).start()

    def sent_x(plane, d):
        x_copy(plane, d).wait_send()

    def came_x(plane, d):
        x_wait(plane, d).wait_recv()

    @pl.when(has_next)
    def _():
        z_copy(2).start()

    each_x(2, start_x, True)

    @pl.when(has_last)
    def _():
        z_copy(2).wait_recv()

        @pl.when(has_next)
        def _():
            z_copy(1).start()

        each_x(1, start_x, True)

    @pl.when(zz >= 2)
    def _():
        z_copy(1).wait_recv()
        each_x(0, start_x, True)

    each_x(2, came_x, False)

    @pl.when(has_last)
    def _():
        each_x(1, came_x, False)

    @pl.when(zz >= 2)
    def _():
        each_x(0, came_x, False)

    def store(j):
        cols = pl.ds(pl.multiple_of(j * WIDE, WIDE), WIDE)
        return pltpu.make_async_copy(out_buf.at[:, cols], out_hbm.at[0, :, cols], out_sem.at[j])

    ones = jnp.ones((SPAN, HD), jnp.bfloat16)

    @pl.loop(0, HK)
    def _(j):
        @pl.loop(1, GROUPS)
        def _(d):
            q_copy(j, d).wait_recv()

        rows = contract(put, q_recv[j].reshape(SLOTS, WIDE), ((1,), (0,))).astype(jnp.bfloat16)
        for h in range(HQ // HK):
            placed[h] = rows[:, h * HD : (h + 1) * HD]
        key_cols = pl.ds(pl.multiple_of(j * HD, HD), HD)
        value_cols = pl.ds(pl.multiple_of((HK + j) * HD, HD), HD)

        for h in range(HQ // HK):
            keys = window[pl.ds(x, BACK + 1), :, key_cols].reshape(SPAN, HD)
            values = window[pl.ds(x, BACK + 1), :, value_cols].reshape(SPAN, HD)
            scores = contract(placed[h], keys, ((1,), (1,))) + mask[...]
            top = jnp.max(scores, axis=1, keepdims=True)
            weights = jnp.exp2((scores - top) * FACTOR).astype(jnp.bfloat16)
            summed = contract(weights, jnp.concatenate([values, ones], axis=1), ((1,), (0,)))
            cols = pl.ds(pl.multiple_of((j * (HQ // HK) + h) * HD, HD), HD)
            out_buf[:, cols] = (summed[:, :HD] / summed[:, HD:]).astype(jnp.bfloat16)

        store(j).start()

    for j in range(HK):
        store(j).wait()

    @pl.loop(1, GROUPS)
    def _(d):
        kv_copy(d).wait_send()
        for j in range(HK):
            q_copy(j, d).wait_send()

    each_x(2, sent_x, True)

    @pl.when(has_next)
    def _():
        z_copy(2).wait_send()

    @pl.when(has_last)
    def _():
        each_x(1, sent_x, True)

        @pl.when(has_next)
        def _():
            z_copy(1).wait_send()

    @pl.when(zz >= 2)
    def _():
        each_x(0, sent_x, True)


def padded(queries, keys_values, route_group, route_slot, doc_lengths):
    bf16 = jnp.bfloat16
    dma = pltpu.SemaphoreType.DMA
    return pl.pallas_call(
        padded_kernel,
        out_shape=jax.ShapeDtypeStruct((1, TOK, HQ * HD), bf16),
        in_specs=[
            pl.BlockSpec(memory_space=pltpu.HBM),
            pl.BlockSpec(memory_space=pltpu.HBM),
            pl.BlockSpec(memory_space=pltpu.HBM),
            pl.BlockSpec(memory_space=pltpu.HBM),
            pl.BlockSpec(memory_space=pltpu.HBM),
        ],
        out_specs=pl.BlockSpec(memory_space=pl.ANY),
        scratch_shapes=[
            pltpu.VMEM((TOK, HQ * HD), bf16),
            pltpu.VMEM((1, TOK, PAIR), bf16),
            pltpu.VMEM((1, TOK), jnp.int32),
            pltpu.VMEM((1, TOK), jnp.int32),
            pltpu.SMEM((1, 2, 3), jnp.int32),
            pltpu.VMEM((HK, GROUPS, CAP, WIDE), bf16),
            pltpu.VMEM((HK, GROUPS, CAP, WIDE), bf16),
            pltpu.VMEM((GROUPS, CAP, PAIR + TOK), bf16),
            pltpu.VMEM((GROUPS, CAP, PAIR + TOK), bf16),
            pltpu.VMEM((3 * NX, TOK, PAIR), bf16),
            pltpu.VMEM((TOK, SPAN), jnp.float32),
            pltpu.VMEM((HQ // HK, TOK, HD), bf16),
            pltpu.VMEM((TOK, HQ * HD), bf16),
            dma((HK + 4,)),
            dma((HK,)),
            dma((HK, GROUPS)),
            dma((HK, GROUPS)),
            dma((GROUPS,)),
            dma((GROUPS,)),
            dma((3,)),
            dma((3,)),
            dma((3, NX)),
            dma((3, NX)),
        ],
        compiler_params=pltpu.CompilerParams(
            collective_id=0, has_side_effects=True, vmem_limit_bytes=64 << 20
        ),
    )(queries, keys_values, route_group, route_slot, doc_lengths)


LOW = 8
OVER = 8
HALF_WIDE = WIDE // 2
PIECE = PAIR // 2
NY = GROUPS // 2
NZ = 2 * HALF_ROWS


def both_halves(one):
    none = jnp.zeros_like(one)
    left = jnp.concatenate([one, none], axis=1)
    right = jnp.concatenate([none, one], axis=1)
    lanes = one.shape[2]
    return jnp.concatenate([left.reshape(-1, lanes), right.reshape(-1, lanes)], axis=1)


def compact_kernel(
    q_hbm,
    kv_hbm,
    group_hbm,
    slot_hbm,
    length_hbm,
    out_hbm,
    flag_ref,
    q_in,
    kv_ref,
    group_ref,
    slot_ref,
    length_ref,
    q_send,
    q_recv,
    kva_send,
    kva_recv,
    kvb_send,
    kvb_recv,
    over,
    window,
    mask,
    placed,
    out_buf,
    flag_x,
    flag_z,
    in_sem,
    out_sem,
    q_ss,
    q_rs,
    kv_ss,
    kv_rs,
    ring_ss,
    ring_rs,
    sib_ss,
    sib_rs,
    z_ss,
    z_rs,
    x_ss,
    x_rs,
    fx_ss,
    fx_rs,
    fz_ss,
    fz_rs,
):
    bf16 = jnp.bfloat16
    f32 = jnp.float32
    me = lax.axis_index("grp")
    seq = lax.axis_index("seq")
    z = seq // NX
    x = seq % NX
    zz = z % HALF_ROWS
    y = me // 2
    core = me % 2
    has_next = zz < HALF_ROWS - 1
    has_last = zz > 0

    small = [
        pltpu.make_async_copy(source, target, in_sem.at[2 * HK + n])
        for n, (source, target) in enumerate(
            [
                (group_hbm, group_ref),
                (slot_hbm, slot_ref),
                (kv_hbm, kv_ref),
                (length_hbm, length_ref),
            ]
        )
    ]
    loads = [
        pltpu.make_async_copy(
            q_hbm.at[0, :, pl.ds(n * HALF_WIDE, HALF_WIDE)], q_in.at[n], in_sem.at[n]
        )
        for n in range(2 * HK)
    ]
    for copy in small + loads:
        copy.start()

    barrier = pltpu.get_barrier_semaphore()

    def greet(group, place):
        pl.semaphore_signal(barrier, inc=1, device_id=(group, place), device_id_type=MESH)

    for d in range(1, GROUPS):
        greet((me + d) % GROUPS, seq)
    for d in range(1, NX):
        greet(me, z * NX + (x + d) % NX)
    for d in range(1, NZ):
        greet(me, (z + d) % NZ * NX + x)

    for copy in small:
        copy.wait()
    targets = group_ref[...]
    lane = lax.broadcasted_iota(jnp.int32, (TOK, TOK), 1)
    sub = lax.broadcasted_iota(jnp.int32, (TOK, TOK), 0)
    hits = lax.broadcasted_iota(jnp.int32, (GROUPS, TOK), 0) == targets
    before = (sub < lane).astype(f32).astype(bf16)
    all_ones = jnp.ones((TOK, TOK), bf16)
    ranks = contract(hits.astype(f32).astype(bf16), before, ((1,), (0,)))
    ranks = jnp.where(hits, ranks, -1.0)
    level = lax.broadcasted_iota(jnp.int32, (GROUPS, CAP, TOK), 1).astype(f32)
    pick_three = (ranks[:, None, :] == level).astype(f32)
    pick_f = pick_three.reshape(SLOTS, TOK)
    pick = pick_f.astype(bf16)
    places = (slot_ref[...] + 1).astype(f32)
    beyond = jnp.sum((ranks >= LOW).astype(f32), axis=0, keepdims=True)
    order = contract(jnp.broadcast_to(beyond, (OVER, TOK)).astype(bf16), before, ((1,), (0,)))
    row = lax.broadcasted_iota(jnp.int32, (OVER, TOK), 0).astype(f32)
    extra = jnp.where((order == row) & (beyond > 0.0), 1.0, 0.0)
    crowded = jnp.sum(beyond, axis=1, keepdims=True) > OVER
    marks = contract((pick_f * places).astype(bf16), all_ones, ((1,), (0,)))
    marks = jnp.where(crowded, -1.0, marks)
    kva_send[:, :, PIECE:] = marks.astype(bf16).reshape(GROUPS, CAP, TOK)

    sends = [kva_send, kvb_send]
    recvs = [kva_recv, kvb_recv]

    def pack_pairs(n):
        for part in range(2):
            cols = kv_ref[0, :, part * PIECE + n * PIECE // 2 : part * PIECE + (n + 1) * PIECE // 2]
            sends[n][:, :, part * PIECE // 2 : (part + 1) * PIECE // 2] = (
                contract(pick, cols, ((1,), (0,))).astype(bf16).reshape(GROUPS, CAP, PIECE // 2)
            )

    def partner(d):
        return (y + d // 2) % NY * 2 + (core + d % 2) % 2

    def far_first(act):
        @pl.loop(0, NY - 1)
        def _(i):
            away = NY // 2 + i // 2 * (1 - i % 2) - (i + 1) // 2 * (i % 2)
            act(2 * away)
            act(2 * away + 1)

        act(1)

    def kv_copy(n, d):
        target = partner(d)
        return remote(
            sends[n].at[target], recvs[n].at[me], kv_ss.at[n, d], kv_rs.at[n, d], (target, seq)
        )

    def start_pairs(n):
        far_first(lambda d: kv_copy(n, d).start())
        recvs[n][me] = sends[n][me]

    pack_pairs(0)

    high = both_halves(extra[None]).astype(bf16)
    for j in range(HK):
        loads[2 * j].wait()
        loads[2 * j + 1].wait()
        halves = q_in[2 * j : 2 * j + 2].reshape(2 * TOK, HALF_WIDE)
        over[me, :, j * HALF_WIDE : (j + 1) * HALF_WIDE] = contract(
            high, halves, ((1,), (0,))
        ).astype(bf16)
    tags = jnp.concatenate([extra * places, extra * (targets + 1).astype(f32)], axis=0)
    over[me, :, HK * HALF_WIDE :] = contract(tags.astype(bf16), all_ones, ((1,), (0,))).astype(bf16)
    turn = 1 - 2 * core

    def on_ring(at):
        return (at + 2 * NY) % NY * 2 + core

    def on_sibling(at):
        return (at + 2 * NY) % NY * 2 + 1 - core

    def ring(step, way):
        sign = turn if way == 0 else -turn
        block = on_ring(y - sign * (step - 1))
        return remote(
            over.at[block],
            over.at[block],
            ring_ss.at[way, step],
            ring_rs.at[way, step],
            (on_ring(y + sign), seq),
        )

    def ring_came(step, way):
        sign = turn if way == 0 else -turn
        block = on_ring(y - sign * step)
        remote(
            over.at[block],
            over.at[block],
            ring_ss.at[way, step],
            ring_rs.at[way, step],
            (on_ring(y + sign), seq),
        ).wait_recv()

    def sibling(n):
        block = on_ring(y - turn * n if n <= NY // 2 else y + turn * (n - NY // 2))
        return remote(
            over.at[block], over.at[block], sib_ss.at[n], sib_rs.at[n], (on_sibling(y), seq)
        )

    def sibling_came(n):
        block = on_sibling(y + turn * n if n <= NY // 2 else y - turn * (n - NY // 2))
        remote(
            over.at[block], over.at[block], sib_ss.at[n], sib_rs.at[n], (on_sibling(y), seq)
        ).wait_recv()

    def ring_turn(step):
        ring_came(step, 0)
        if step < NY // 2:
            ring(step + 1, 0).start()
            ring_came(step, 1)
            if step + 1 < NY // 2:
                ring(step + 1, 1).start()
            sibling(NY // 2 + step).start()
        sibling(step).start()

    pl.semaphore_wait(barrier, GROUPS - 1 + NX - 1 + NZ - 1)
    ring(1, 0).start()
    ring(1, 1).start()
    start_pairs(0)
    sibling(0).start()
    pack_pairs(1)

    ring_turn(1)
    start_pairs(1)

    low = both_halves(pick_three[:, :LOW]).astype(bf16)
    for j in range(HK):
        halves = q_in[2 * j : 2 * j + 2].reshape(2 * TOK, HALF_WIDE)
        q_send[j] = (
            contract(low, halves, ((1,), (0,))).astype(bf16).reshape(GROUPS, CAP, HALF_WIDE)
        )

    def q_copy(j, d):
        target = partner(d)
        return remote(
            q_send.at[j, target], q_recv.at[j, me], q_ss.at[j, d], q_rs.at[j, d], (target, seq)
        )

    def start_queries(j):
        far_first(lambda d: q_copy(j, d).start())
        q_recv[j, me] = q_send[j, me]

    query = seq * TOK + lax.broadcasted_iota(jnp.int32, (TOK, SPAN), 0)
    key = (seq - BACK) * TOK + lax.broadcasted_iota(jnp.int32, (TOK, SPAN), 1)
    begin = jnp.zeros((TOK, SPAN), jnp.int32)
    bound = jnp.int32(0)
    for half in range(2):
        for n in range(3):
            bound = bound + length_ref[0, half, n]
            begin = jnp.where(query >= bound, bound, begin)
    mask[...] = jnp.where((key >= begin) & (key <= query), 0.0, NEGATIVE)

    @pl.when(zz == 0)
    def _():
        window[:, pl.ds(0, 2 * NX)] = jnp.zeros((2, 2 * NX, TOK, PIECE), bf16)

    @pl.when(zz == 1)
    def _():
        window[:, pl.ds(0, NX)] = jnp.zeros((2, NX, TOK, PIECE), bf16)

    def z_copy(n, plane):
        return remote(
            window.at[n, plane * NX + x],
            window.at[n, (plane - 1) * NX + x],
            z_ss.at[n, plane],
            z_rs.at[n, plane],
            (me, (seq + NX) % (NX * NZ)),
        )

    def x_copy(n, plane, d, came=False):
        at = plane * NX + ((x + NX - d) % NX if came else x)
        return remote(
            window.at[n, at],
            window.at[n, at],
            x_ss.at[n, plane, d],
            x_rs.at[n, plane, d],
            (me, z * NX + (x + d) % NX),
        )

    def start_x(n, plane, d):
        x_copy(n, plane, d).start()

    def sent_x(n, plane, d):
        x_copy(n, plane, d).wait_send()

    def came_x(n, plane, d):
        x_copy(n, plane, d, True).wait_recv()

    def each_x(n, plane, act, steps):
        for d in steps:
            wraps = x - d < 0 if act is came_x else x + d >= NX
            if plane == 1:
                act(n, plane, d)
            else:
                pl.when(wraps if plane == 0 else jnp.logical_not(wraps))(
                    functools.partial(act, n, plane, d)
                )

    beside = (1, NX - 1)
    inner = (x == 1) | (x == 2)

    def pass_on(n, plane, way, slot):
        at = plane * NX + (x + NX - way) % NX
        return remote(
            window.at[n, at],
            window.at[n, at],
            x_ss.at[n, plane, slot],
            x_rs.at[n, plane, 2],
            (me, z * NX + (x + NX + way) % NX),
        )

    def each_pass(n, plane, act):
        if plane == 1:

            @pl.when(jnp.logical_not(inner))
            def _():
                act(pass_on(n, plane, 1, 0))
                act(pass_on(n, plane, -1, 2))

        else:

            @pl.when(inner)
            def _():
                act(pass_on(n, plane, 1 if plane == 2 else -1, 2))

    def forward(n, plane):
        def go():
            each_x(n, plane, came_x, beside)
            each_pass(n, plane, lambda copy: copy.start())

        if plane == 2:
            go()
        else:
            pl.when(has_last if plane == 1 else zz >= 2)(go)

    def place_pairs(n):
        window[n, 2 * NX + x] = contract(
            put, recvs[n][:, :, :PIECE].reshape(SLOTS, PIECE), ((1,), (0,))
        ).astype(bf16)

        @pl.when(has_next)
        def _():
            z_copy(n, 2).start()

        each_x(n, 2, start_x, beside)

    def one_back(n):
        @pl.when(has_last)
        def _():
            z_copy(n, 2).wait_recv()

            @pl.when(has_next)
            def _():
                z_copy(n, 1).start()

            each_x(n, 1, start_x, beside)

    def two_back(n):
        @pl.when(zz >= 2)
        def _():
            z_copy(n, 1).wait_recv()
            each_x(n, 0, start_x, beside)

    def flag_x_copy(d, came=False):
        at = (x + NX - d) % NX if came else x
        return remote(
            flag_x.at[at],
            flag_x.at[at],
            fx_ss.at[d],
            fx_rs.at[d],
            (me, z * NX + (x + d) % NX),
        )

    def flag_z_copy(d, came=False):
        at = (z + NZ - d) % NZ if came else z
        return remote(
            flag_z.at[at],
            flag_z.at[at],
            fz_ss.at[d],
            fz_rs.at[d],
            (me, (z + d) % NZ * NX + x),
        )

    def pairs_came(n):
        @pl.loop(1, GROUPS)
        def _(d):
            kv_copy(n, d).wait_recv()

    pairs_came(0)
    marks_in = kva_recv[:, :, PIECE:].astype(f32)
    column = lax.broadcasted_iota(jnp.int32, (GROUPS, CAP, TOK), 2).astype(f32) + 1.0
    match = (marks_in == column).astype(f32)
    put = match.reshape(SLOTS, TOK).T.astype(bf16)
    place_pairs(0)
    worst = jnp.max((marks_in < 0.0).astype(f32).reshape(SLOTS, TOK), axis=0, keepdims=True)
    flag_x[x] = jnp.broadcast_to(worst, (CAP, TOK)).astype(bf16)
    for d in range(1, NX):
        flag_x_copy(d).start()
    put_low = both_halves(match[:, :LOW]).T.astype(bf16)

    ring_turn(2)
    start_queries(0)
    forward(0, 2)
    one_back(0)
    ring_turn(3)
    start_queries(1)
    pairs_came(1)
    place_pairs(1)
    for d in range(1, NX):
        flag_x_copy(d, True).wait_recv()
    flag_z[z] = jnp.max(flag_x[...].astype(f32), axis=0).astype(bf16)
    for d in range(1, NZ):
        flag_z_copy(d).start()
    forward(0, 1)
    two_back(0)
    ring_turn(4)
    start_queries(2)
    one_back(1)
    forward(1, 2)
    forward(0, 0)
    start_queries(3)
    two_back(1)
    for d in range(1, NZ):
        flag_z_copy(d, True).wait_recv()
    flag_ref[0, 0] = jnp.max(flag_z[...].astype(f32)).astype(jnp.int32)
    for n in range(NY):
        sibling_came(n)

    tags_in = over[:, :, HK * HALF_WIDE :].astype(f32)
    mine = (me + 1).astype(f32)
    match_over = ((tags_in[:, :OVER] == column[:, :OVER]) & (tags_in[:, OVER:] == mine)).astype(f32)
    put_over = both_halves(match_over).T.astype(bf16)

    def store(j):
        cols = pl.ds(pl.multiple_of(j * WIDE, WIDE), WIDE)
        return pltpu.make_async_copy(out_buf.at[:, cols], out_hbm.at[0, :, cols], out_sem.at[j])

    ones = jnp.ones((SPAN, HD), bf16)

    def window_came(n):
        each_x(n, 2, came_x, (2,))

        @pl.when(has_last)
        def _():
            each_x(n, 1, came_x, (2,))

        @pl.when(zz >= 2)
        def _():
            each_x(n, 0, came_x, (2,))

    @pl.loop(0, HK)
    def _(j):
        @pl.when(j == 0)
        def _():
            window_came(0)

        @pl.when(j == 1)
        def _():
            forward(1, 1)
            forward(1, 0)

        @pl.when(j == 2)
        def _():
            window_came(1)

        @pl.loop(1, GROUPS)
        def _(d):
            q_copy(j, d).wait_recv()

        cols = pl.ds(pl.multiple_of(j * HALF_WIDE, HALF_WIDE), HALF_WIDE)
        rows = contract(put_low, q_recv[j].reshape(SLOTS, HALF_WIDE), ((1,), (0,)))
        rows = rows + contract(put_over, over[:, :, cols].reshape(SLOTS, HALF_WIDE), ((1,), (0,)))
        rows = rows.astype(bf16)
        for h in range(HQ // HK):
            half, at = h // (HQ // HK // 2), h % (HQ // HK // 2)
            placed[h] = rows[half * TOK : (half + 1) * TOK, at * HD : (at + 1) * HD]
        key_cols = pl.ds(pl.multiple_of(j % 2 * HD, HD), HD)
        value_cols = pl.ds(pl.multiple_of(PIECE // 2 + j % 2 * HD, HD), HD)
        for h in range(HQ // HK):
            keys = window[j // 2, pl.ds(x, BACK + 1), :, key_cols].reshape(SPAN, HD)
            values = window[j // 2, pl.ds(x, BACK + 1), :, value_cols].reshape(SPAN, HD)
            scores = contract(placed[h], keys, ((1,), (1,))) + mask[...]
            top = jnp.max(scores, axis=1, keepdims=True)
            weights = jnp.exp2((scores - top) * FACTOR).astype(bf16)
            summed = contract(weights, jnp.concatenate([values, ones], axis=1), ((1,), (0,)))
            head_cols = pl.ds(pl.multiple_of((j * (HQ // HK) + h) * HD, HD), HD)
            out_buf[:, head_cols] = (summed[:, :HD] / summed[:, HD:]).astype(bf16)

        store(j).start()

    for j in range(HK):
        store(j).wait()

    @pl.loop(1, GROUPS)
    def _(d):
        for n in range(2):
            kv_copy(n, d).wait_send()
        for j in range(HK):
            q_copy(j, d).wait_send()

    for n in range(2):
        each_x(n, 2, sent_x, beside)
        each_pass(n, 2, lambda copy: copy.wait_send())

        @pl.when(has_next)
        def _(n=n):
            z_copy(n, 2).wait_send()

        @pl.when(has_last)
        def _(n=n):
            each_x(n, 1, sent_x, beside)
            each_pass(n, 1, lambda copy: copy.wait_send())

            @pl.when(has_next)
            def _():
                z_copy(n, 1).wait_send()

        @pl.when(zz >= 2)
        def _(n=n):
            each_x(n, 0, sent_x, beside)
            each_pass(n, 0, lambda copy: copy.wait_send())

    for step in range(1, NY // 2 + 1):
        ring(step, 0).wait_send()
        if step < NY // 2:
            ring(step, 1).wait_send()
    for n in range(NY):
        sibling(n).wait_send()
    for d in range(1, NX):
        flag_x_copy(d).wait_send()
    for d in range(1, NZ):
        flag_z_copy(d).wait_send()


def compact(*operands):
    bf16 = jnp.bfloat16
    dma = pltpu.SemaphoreType.DMA
    vmem = pltpu.VMEM
    return pl.pallas_call(
        compact_kernel,
        out_shape=(
            jax.ShapeDtypeStruct((1, TOK, HQ * HD), bf16),
            jax.ShapeDtypeStruct((1, 1), jnp.int32),
        ),
        in_specs=[pl.BlockSpec(memory_space=pltpu.HBM)] * 5,
        out_specs=(pl.BlockSpec(memory_space=pl.ANY), pl.BlockSpec(memory_space=pltpu.SMEM)),
        scratch_shapes=[
            vmem((2 * HK, TOK, HALF_WIDE), bf16),
            vmem((1, TOK, PAIR), bf16),
            vmem((1, TOK), jnp.int32),
            vmem((1, TOK), jnp.int32),
            pltpu.SMEM((1, 2, 3), jnp.int32),
            vmem((HK, GROUPS, CAP, HALF_WIDE), bf16),
            vmem((HK, GROUPS, CAP, HALF_WIDE), bf16),
            vmem((GROUPS, CAP, PIECE + TOK), bf16),
            vmem((GROUPS, CAP, PIECE + TOK), bf16),
            vmem((GROUPS, CAP, PIECE), bf16),
            vmem((GROUPS, CAP, PIECE), bf16),
            vmem((GROUPS, CAP, HK * HALF_WIDE + TOK), bf16),
            vmem((2, 3 * NX, TOK, PIECE), bf16),
            vmem((TOK, SPAN), jnp.float32),
            vmem((HQ // HK, TOK, HD), bf16),
            vmem((TOK, HQ * HD), bf16),
            vmem((NX, CAP, TOK), bf16),
            vmem((NZ, CAP, TOK), bf16),
            dma((2 * HK + 4,)),
            dma((HK,)),
            dma((HK, GROUPS)),
            dma((HK, GROUPS)),
            dma((2, GROUPS)),
            dma((2, GROUPS)),
            dma((2, NY // 2 + 1)),
            dma((2, NY // 2 + 1)),
            dma((NY,)),
            dma((NY,)),
            dma((2, 3)),
            dma((2, 3)),
            dma((2, 3, NX)),
            dma((2, 3, NX)),
            dma((NX,)),
            dma((NX,)),
            dma((NZ,)),
            dma((NZ,)),
        ],
        compiler_params=pltpu.CompilerParams(
            collective_id=1, has_side_effects=True, vmem_limit_bytes=64 << 20
        ),
    )(*operands)


def local(*operands):
    result, crowded = compact(*operands)
    return lax.switch(crowded[0, 0], [lambda: result, lambda: padded(*operands)])


def solution(mesh):
    return jax.shard_map(
        local,
        mesh=mesh,
        in_specs=(
            P("grp", "seq", None),
            P("grp", "seq", None),
            P("grp", "seq"),
            P("grp", "seq"),
            P("grp", None, None),
        ),
        out_specs=P("grp", "seq", None),
        check_vma=False,
    )
```

```python
import functools
import math

import jax
import jax.numpy as jnp
from jax import lax
from jax.experimental import pallas as pl
from jax.experimental.pallas import tpu as pltpu
from jax.sharding import PartitionSpec as P

HQ = 32
HK = 4
HD = 128
TOK = 128
GROUPS = 16
CAP = 16
SLOTS = GROUPS * CAP
WIDE = HQ // HK * HD
PAIR = 2 * HK * HD
BACK = 8
SPAN = (BACK + 1) * TOK
NX = 4
HALF_ROWS = 4
NEGATIVE = -1e30
MESH = pl.DeviceIdType.MESH
FACTOR = HD ** (-0.5) * math.log2(math.e)


def remote(src, dst, send, recv, device):
    return pltpu.make_async_remote_copy(
        src_ref=src,
        dst_ref=dst,
        send_sem=send,
        recv_sem=recv,
        device_id=device,
        device_id_type=MESH,
    )


def contract(a, b, dims):
    return lax.dot_general(a, b, (dims, ((), ())), preferred_element_type=jnp.float32)


def padded_kernel(
    q_hbm,
    kv_hbm,
    group_hbm,
    slot_hbm,
    length_hbm,
    out_hbm,
    q_in,
    kv_ref,
    group_ref,
    slot_ref,
    length_ref,
    q_send,
    q_recv,
    kv_send,
    kv_recv,
    window,
    mask,
    placed,
    out_buf,
    in_sem,
    out_sem,
    q_ss,
    q_rs,
    kv_ss,
    kv_rs,
    z_ss,
    z_rs,
    x_ss,
    x_rs,
):
    me = lax.axis_index("grp")
    seq = lax.axis_index("seq")
    z = seq // NX
    x = seq % NX
    zz = z % HALF_ROWS
    has_next = zz < HALF_ROWS - 1
    has_last = zz > 0

    def load(j):
        cols = pl.ds(j * WIDE, WIDE)
        return pltpu.make_async_copy(q_hbm.at[0, :, cols], q_in.at[:, cols], in_sem.at[j])

    small = [
        pltpu.make_async_copy(source, target, in_sem.at[HK + n])
        for n, (source, target) in enumerate(
            [
                (group_hbm, group_ref),
                (slot_hbm, slot_ref),
                (kv_hbm, kv_ref),
                (length_hbm, length_ref),
            ]
        )
    ]
    for copy in small:
        copy.start()
    for j in range(HK):
        load(j).start()

    barrier = pltpu.get_barrier_semaphore()

    def greet(group, place):
        pl.semaphore_signal(barrier, inc=1, device_id=(group, place), device_id_type=MESH)

    for d in range(1, GROUPS):
        greet((me + d) % GROUPS, seq)
    for d in range(1, NX):
        greet(me, z * NX + (x + d) % NX)

    @pl.when(has_next)
    def _():
        greet(me, seq + NX)

    @pl.when(has_last)
    def _():
        greet(me, seq - NX)

    for copy in small:
        copy.wait()
    targets = group_ref[...]
    lane = lax.broadcasted_iota(jnp.int32, (TOK, TOK), 1)
    sub = lax.broadcasted_iota(jnp.int32, (TOK, TOK), 0)
    hits = lax.broadcasted_iota(jnp.int32, (GROUPS, TOK), 0) == targets
    before = (sub < lane).astype(jnp.float32).astype(jnp.bfloat16)
    hits_f = hits.astype(jnp.float32)
    ranks = contract(hits_f.astype(jnp.bfloat16), before, ((1,), (0,)))
    ranks = jnp.where(hits, ranks, -1.0)
    level = lax.broadcasted_iota(jnp.int32, (GROUPS, CAP, TOK), 1).astype(jnp.float32)
    pick_f = (ranks[:, None, :] == level).astype(jnp.float32).reshape(SLOTS, TOK)
    pick = pick_f.astype(jnp.bfloat16)
    marks = (pick_f * (slot_ref[...] + 1).astype(jnp.float32)).astype(jnp.bfloat16)
    slots = contract(marks, jnp.ones((TOK, TOK), jnp.bfloat16), ((1,), (0,)))
    kv_send[:, :, PAIR:] = slots.astype(jnp.bfloat16).reshape(GROUPS, CAP, TOK)
    kv_send[:, :, :PAIR] = (
        contract(pick, kv_ref[0], ((1,), (0,))).astype(jnp.bfloat16).reshape(GROUPS, CAP, PAIR)
    )

    pl.semaphore_wait(
        barrier, GROUPS - 1 + NX - 1 + has_next.astype(jnp.int32) + has_last.astype(jnp.int32)
    )

    def kv_copy(d):
        target = (me + d) % GROUPS
        return remote(
            kv_send.at[target], kv_recv.at[me], kv_ss.at[d], kv_rs.at[d], (target, seq)
        )

    @pl.loop(1, GROUPS)
    def _(d):
        kv_copy(d).start()

    kv_recv[me] = kv_send[me]

    def q_copy(j, d):
        target = (me + d) % GROUPS
        return remote(
            q_send.at[j, target], q_recv.at[j, me], q_ss.at[j, d], q_rs.at[j, d], (target, seq)
        )

    for j in range(HK):
        load(j).wait()
        q_send[j] = (
            contract(pick, q_in[:, j * WIDE : (j + 1) * WIDE], ((1,), (0,)))
            .astype(jnp.bfloat16)
            .reshape(GROUPS, CAP, WIDE)
        )

        @pl.loop(1, GROUPS)
        def _(d, j=j):
            q_copy(j, d).start()

        q_recv[j, me] = q_send[j, me]

    query = seq * TOK + lax.broadcasted_iota(jnp.int32, (TOK, SPAN), 0)
    key = (seq - BACK) * TOK + lax.broadcasted_iota(jnp.int32, (TOK, SPAN), 1)
    begin = jnp.zeros((TOK, SPAN), jnp.int32)
    bound = jnp.int32(0)
    for half in range(2):
        for n in range(3):
            bound = bound + length_ref[0, half, n]
            begin = jnp.where(query >= bound, bound, begin)
    mask[...] = jnp.where((key >= begin) & (key <= query), 0.0, NEGATIVE)

    @pl.when(zz == 0)
    def _():
        window[pl.ds(0, 2 * NX)] = jnp.zeros((2 * NX, TOK, PAIR), jnp.bfloat16)

    @pl.when(zz == 1)
    def _():
        window[pl.ds(0, NX)] = jnp.zeros((NX, TOK, PAIR), jnp.bfloat16)

    @pl.loop(1, GROUPS)
    def _(d):
        kv_copy(d).wait_recv()

    marks_in = kv_recv[:, :, PAIR:].reshape(SLOTS, TOK).astype(jnp.float32)
    column = lax.broadcasted_iota(jnp.int32, (SLOTS, TOK), 1).astype(jnp.float32) + 1.0
    put = (marks_in == column).astype(jnp.float32).T.astype(jnp.bfloat16)
    window[2 * NX + x] = contract(
        put, kv_recv[:, :, :PAIR].reshape(SLOTS, PAIR), ((1,), (0,))
    ).astype(jnp.bfloat16)

    def z_copy(plane):
        return remote(
            window.at[plane * NX + x],
            window.at[(plane - 1) * NX + x],
            z_ss.at[plane],
            z_rs.at[plane],
            (me, (seq + NX) % (NX * 8)),
        )

    def x_copy(plane, d):
        return remote(
            window.at[plane * NX + x],
            window.at[plane * NX + x],
            x_ss.at[plane, d],
            x_rs.at[plane, d],
            (me, z * NX + (x + d) % NX),
        )

    def x_wait(plane, d):
        source = (x + NX - d) % NX
        return remote(
            window.at[plane * NX + source],
            window.at[plane * NX + source],
            x_ss.at[plane, d],
            x_rs.at[plane, d],
            (me, z * NX + (x + d) % NX),
        )

    def each_x(plane, act, sending):
        for d in range(1, NX):
            wraps = x + d >= NX if sending else x - d < 0
            if plane == 1:
                act(plane, d)
            else:
                pl.when(wraps if plane == 0 else jnp.logical_not(wraps))(
                    functools.partial(act, plane, d)
                )

    def start_x(plane, d):
        x_copy(plane, d).start()

    def sent_x(plane, d):
        x_copy(plane, d).wait_send()

    def came_x(plane, d):
        x_wait(plane, d).wait_recv()

    @pl.when(has_next)
    def _():
        z_copy(2).start()

    each_x(2, start_x, True)

    @pl.when(has_last)
    def _():
        z_copy(2).wait_recv()

        @pl.when(has_next)
        def _():
            z_copy(1).start()

        each_x(1, start_x, True)

    @pl.when(zz >= 2)
    def _():
        z_copy(1).wait_recv()
        each_x(0, start_x, True)

    each_x(2, came_x, False)

    @pl.when(has_last)
    def _():
        each_x(1, came_x, False)

    @pl.when(zz >= 2)
    def _():
        each_x(0, came_x, False)

    def store(j):
        cols = pl.ds(pl.multiple_of(j * WIDE, WIDE), WIDE)
        return pltpu.make_async_copy(out_buf.at[:, cols], out_hbm.at[0, :, cols], out_sem.at[j])

    ones = jnp.ones((SPAN, HD), jnp.bfloat16)

    @pl.loop(0, HK)
    def _(j):
        @pl.loop(1, GROUPS)
        def _(d):
            q_copy(j, d).wait_recv()

        rows = contract(put, q_recv[j].reshape(SLOTS, WIDE), ((1,), (0,))).astype(jnp.bfloat16)
        for h in range(HQ // HK):
            placed[h] = rows[:, h * HD : (h + 1) * HD]
        key_cols = pl.ds(pl.multiple_of(j * HD, HD), HD)
        value_cols = pl.ds(pl.multiple_of((HK + j) * HD, HD), HD)

        for h in range(HQ // HK):
            keys = window[pl.ds(x, BACK + 1), :, key_cols].reshape(SPAN, HD)
            values = window[pl.ds(x, BACK + 1), :, value_cols].reshape(SPAN, HD)
            scores = contract(placed[h], keys, ((1,), (1,))) + mask[...]
            top = jnp.max(scores, axis=1, keepdims=True)
            weights = jnp.exp2((scores - top) * FACTOR).astype(jnp.bfloat16)
            summed = contract(weights, jnp.concatenate([values, ones], axis=1), ((1,), (0,)))
            cols = pl.ds(pl.multiple_of((j * (HQ // HK) + h) * HD, HD), HD)
            out_buf[:, cols] = (summed[:, :HD] / summed[:, HD:]).astype(jnp.bfloat16)

        store(j).start()

    for j in range(HK):
        store(j).wait()

    @pl.loop(1, GROUPS)
    def _(d):
        kv_copy(d).wait_send()
        for j in range(HK):
            q_copy(j, d).wait_send()

    each_x(2, sent_x, True)

    @pl.when(has_next)
    def _():
        z_copy(2).wait_send()

    @pl.when(has_last)
    def _():
        each_x(1, sent_x, True)

        @pl.when(has_next)
        def _():
            z_copy(1).wait_send()

    @pl.when(zz >= 2)
    def _():
        each_x(0, sent_x, True)


def padded(queries, keys_values, route_group, route_slot, doc_lengths):
    bf16 = jnp.bfloat16
    dma = pltpu.SemaphoreType.DMA
    return pl.pallas_call(
        padded_kernel,
        out_shape=jax.ShapeDtypeStruct((1, TOK, HQ * HD), bf16),
        in_specs=[
            pl.BlockSpec(memory_space=pltpu.HBM),
            pl.BlockSpec(memory_space=pltpu.HBM),
            pl.BlockSpec(memory_space=pltpu.HBM),
            pl.BlockSpec(memory_space=pltpu.HBM),
            pl.BlockSpec(memory_space=pltpu.HBM),
        ],
        out_specs=pl.BlockSpec(memory_space=pl.ANY),
        scratch_shapes=[
            pltpu.VMEM((TOK, HQ * HD), bf16),
            pltpu.VMEM((1, TOK, PAIR), bf16),
            pltpu.VMEM((1, TOK), jnp.int32),
            pltpu.VMEM((1, TOK), jnp.int32),
            pltpu.SMEM((1, 2, 3), jnp.int32),
            pltpu.VMEM((HK, GROUPS, CAP, WIDE), bf16),
            pltpu.VMEM((HK, GROUPS, CAP, WIDE), bf16),
            pltpu.VMEM((GROUPS, CAP, PAIR + TOK), bf16),
            pltpu.VMEM((GROUPS, CAP, PAIR + TOK), bf16),
            pltpu.VMEM((3 * NX, TOK, PAIR), bf16),
            pltpu.VMEM((TOK, SPAN), jnp.float32),
            pltpu.VMEM((HQ // HK, TOK, HD), bf16),
            pltpu.VMEM((TOK, HQ * HD), bf16),
            dma((HK + 4,)),
            dma((HK,)),
            dma((HK, GROUPS)),
            dma((HK, GROUPS)),
            dma((GROUPS,)),
            dma((GROUPS,)),
            dma((3,)),
            dma((3,)),
            dma((3, NX)),
            dma((3, NX)),
        ],
        compiler_params=pltpu.CompilerParams(
            collective_id=0, has_side_effects=True, vmem_limit_bytes=48 << 20
        ),
    )(queries, keys_values, route_group, route_slot, doc_lengths)


LOW = 8
OVER = 8
HALF_WIDE = WIDE // 2
PIECE = PAIR // 2
NY = GROUPS // 2
NZ = 2 * HALF_ROWS


def both_halves(one):
    none = jnp.zeros_like(one)
    left = jnp.concatenate([one, none], axis=1)
    right = jnp.concatenate([none, one], axis=1)
    lanes = one.shape[2]
    return jnp.concatenate([left.reshape(-1, lanes), right.reshape(-1, lanes)], axis=1)


def compact_kernel(
    q_hbm,
    kv_hbm,
    group_hbm,
    slot_hbm,
    length_hbm,
    out_ref,
    flag_ref,
    q_in,
    kv_ref,
    group_ref,
    slot_ref,
    length_ref,
    q_send,
    q_recv,
    kva_send,
    kva_recv,
    kvb_send,
    kvb_recv,
    over,
    window,
    mask,
    placed,
    flag_x,
    flag_z,
    in_sem,
    q_ss,
    q_rs,
    kv_ss,
    kv_rs,
    ring_ss,
    ring_rs,
    sib_ss,
    sib_rs,
    z_ss,
    z_rs,
    x_ss,
    x_rs,
    fx_ss,
    fx_rs,
    fz_ss,
    fz_rs,
):
    bf16 = jnp.bfloat16
    f32 = jnp.float32
    me = lax.axis_index("grp")
    seq = lax.axis_index("seq")
    z = seq // NX
    x = seq % NX
    zz = z % HALF_ROWS
    y = me // 2
    core = me % 2
    has_next = zz < HALF_ROWS - 1
    has_last = zz > 0

    small = [
        pltpu.make_async_copy(source, target, in_sem.at[2 * HK + n])
        for n, (source, target) in enumerate(
            [
                (group_hbm, group_ref),
                (slot_hbm, slot_ref),
                (kv_hbm, kv_ref),
                (length_hbm, length_ref),
            ]
        )
    ]
    loads = [
        pltpu.make_async_copy(
            q_hbm.at[0, :, pl.ds(n * HALF_WIDE, HALF_WIDE)], q_in.at[n], in_sem.at[n]
        )
        for n in range(2 * HK)
    ]
    for copy in small + loads:
        copy.start()

    barrier = pltpu.get_barrier_semaphore()

    def greet(group, place):
        pl.semaphore_signal(barrier, inc=1, device_id=(group, place), device_id_type=MESH)

    for d in range(1, GROUPS):
        greet((me + d) % GROUPS, seq)
    for d in range(1, NX):
        greet(me, z * NX + (x + d) % NX)
    for d in range(1, NZ):
        greet(me, (z + d) % NZ * NX + x)

    for copy in small:
        copy.wait()
    targets = group_ref[...]
    lane = lax.broadcasted_iota(jnp.int32, (TOK, TOK), 1)
    sub = lax.broadcasted_iota(jnp.int32, (TOK, TOK), 0)
    hits = lax.broadcasted_iota(jnp.int32, (GROUPS, TOK), 0) == targets
    before = (sub < lane).astype(f32).astype(bf16)
    all_ones = jnp.ones((TOK, TOK), bf16)
    ranks = contract(hits.astype(f32).astype(bf16), before, ((1,), (0,)))
    ranks = jnp.where(hits, ranks, -1.0)
    level = lax.broadcasted_iota(jnp.int32, (GROUPS, CAP, TOK), 1).astype(f32)
    pick_three = (ranks[:, None, :] == level).astype(f32)
    pick_f = pick_three.reshape(SLOTS, TOK)
    pick = pick_f.astype(bf16)
    places = (slot_ref[...] + 1).astype(f32)
    beyond = jnp.sum((ranks >= LOW).astype(f32), axis=0, keepdims=True)
    order = contract(jnp.broadcast_to(beyond, (OVER, TOK)).astype(bf16), before, ((1,), (0,)))
    row = lax.broadcasted_iota(jnp.int32, (OVER, TOK), 0).astype(f32)
    extra = jnp.where((order == row) & (beyond > 0.0), 1.0, 0.0)
    crowded = jnp.sum(beyond, axis=1, keepdims=True) > OVER
    marks = contract((pick_f * places).astype(bf16), all_ones, ((1,), (0,)))
    marks = jnp.where(crowded, -1.0, marks)
    kva_send[:, :, PIECE:] = marks.astype(bf16).reshape(GROUPS, CAP, TOK)

    sends = [kva_send, kvb_send]
    recvs = [kva_recv, kvb_recv]

    def pack_pairs(n):
        for part in range(2):
            cols = kv_ref[0, :, part * PIECE + n * PIECE // 2 : part * PIECE + (n + 1) * PIECE // 2]
            sends[n][:, :, part * PIECE // 2 : (part + 1) * PIECE // 2] = (
                contract(pick, cols, ((1,), (0,))).astype(bf16).reshape(GROUPS, CAP, PIECE // 2)
            )

    def partner(d):
        return (y + d // 2) % NY * 2 + (core + d % 2) % 2

    def far_first(act):
        @pl.loop(0, NY - 1)
        def _(i):
            away = NY // 2 + i // 2 * (1 - i % 2) - (i + 1) // 2 * (i % 2)
            act(2 * away)
            act(2 * away + 1)

        act(1)

    def kv_copy(n, d):
        target = partner(d)
        return remote(
            sends[n].at[target], recvs[n].at[me], kv_ss.at[n, d], kv_rs.at[n, d], (target, seq)
        )

    def start_pairs(n):
        far_first(lambda d: kv_copy(n, d).start())
        recvs[n][me] = sends[n][me]

    pack_pairs(0)

    high = both_halves(extra[None]).astype(bf16)
    for j in range(HK):
        loads[2 * j].wait()
        loads[2 * j + 1].wait()
        halves = q_in[2 * j : 2 * j + 2].reshape(2 * TOK, HALF_WIDE)
        over[me, :, j * HALF_WIDE : (j + 1) * HALF_WIDE] = contract(
            high, halves, ((1,), (0,))
        ).astype(bf16)
    tags = jnp.concatenate([extra * places, extra * (targets + 1).astype(f32)], axis=0)
    over[me, :, HK * HALF_WIDE :] = contract(tags.astype(bf16), all_ones, ((1,), (0,))).astype(bf16)
    turn = 1 - 2 * core

    def on_ring(at):
        return (at + 2 * NY) % NY * 2 + core

    def on_sibling(at):
        return (at + 2 * NY) % NY * 2 + 1 - core

    def ring(step, way):
        sign = turn if way == 0 else -turn
        block = on_ring(y - sign * (step - 1))
        return remote(
            over.at[block],
            over.at[block],
            ring_ss.at[way, step],
            ring_rs.at[way, step],
            (on_ring(y + sign), seq),
        )

    def ring_came(step, way):
        sign = turn if way == 0 else -turn
        block = on_ring(y - sign * step)
        remote(
            over.at[block],
            over.at[block],
            ring_ss.at[way, step],
            ring_rs.at[way, step],
            (on_ring(y + sign), seq),
        ).wait_recv()

    def sibling(n):
        block = on_ring(y - turn * n if n <= NY // 2 else y + turn * (n - NY // 2))
        return remote(
            over.at[block], over.at[block], sib_ss.at[n], sib_rs.at[n], (on_sibling(y), seq)
        )

    def sibling_came(n):
        block = on_sibling(y + turn * n if n <= NY // 2 else y - turn * (n - NY // 2))
        remote(
            over.at[block], over.at[block], sib_ss.at[n], sib_rs.at[n], (on_sibling(y), seq)
        ).wait_recv()

    def ring_turn(step):
        ring_came(step, 0)
        if step < NY // 2:
            ring(step + 1, 0).start()
            ring_came(step, 1)
            if step + 1 < NY // 2:
                ring(step + 1, 1).start()
            sibling(NY // 2 + step).start()
        sibling(step).start()

    pl.semaphore_wait(barrier, GROUPS - 1 + NX - 1 + NZ - 1)
    ring(1, 0).start()
    ring(1, 1).start()
    start_pairs(0)
    sibling(0).start()
    pack_pairs(1)

    ring_turn(1)
    start_pairs(1)

    low = both_halves(pick_three[:, :LOW]).astype(bf16)
    for j in range(HK):
        halves = q_in[2 * j : 2 * j + 2].reshape(2 * TOK, HALF_WIDE)
        q_send[j] = (
            contract(low, halves, ((1,), (0,))).astype(bf16).reshape(GROUPS, CAP, HALF_WIDE)
        )

    def q_copy(j, d):
        target = partner(d)
        return remote(
            q_send.at[j, target], q_recv.at[j, me], q_ss.at[j, d], q_rs.at[j, d], (target, seq)
        )

    def start_queries(j):
        far_first(lambda d: q_copy(j, d).start())
        q_recv[j, me] = q_send[j, me]

    query = seq * TOK + lax.broadcasted_iota(jnp.int32, (TOK, SPAN), 0)
    key = (seq - BACK) * TOK + lax.broadcasted_iota(jnp.int32, (TOK, SPAN), 1)
    begin = jnp.zeros((TOK, SPAN), jnp.int32)
    bound = jnp.int32(0)
    for half in range(2):
        for n in range(3):
            bound = bound + length_ref[0, half, n]
            begin = jnp.where(query >= bound, bound, begin)
    mask[...] = jnp.where((key >= begin) & (key <= query), 0.0, NEGATIVE)

    @pl.when(zz == 0)
    def _():
        window[:, pl.ds(0, 2 * NX)] = jnp.zeros((2, 2 * NX, TOK, PIECE), bf16)

    @pl.when(zz == 1)
    def _():
        window[:, pl.ds(0, NX)] = jnp.zeros((2, NX, TOK, PIECE), bf16)

    def z_copy(n, plane):
        return remote(
            window.at[n, plane * NX + x],
            window.at[n, (plane - 1) * NX + x],
            z_ss.at[n, plane],
            z_rs.at[n, plane],
            (me, (seq + NX) % (NX * NZ)),
        )

    def x_copy(n, plane, d, came=False):
        at = plane * NX + ((x + NX - d) % NX if came else x)
        return remote(
            window.at[n, at],
            window.at[n, at],
            x_ss.at[n, plane, d],
            x_rs.at[n, plane, d],
            (me, z * NX + (x + d) % NX),
        )

    def start_x(n, plane, d):
        x_copy(n, plane, d).start()

    def sent_x(n, plane, d):
        x_copy(n, plane, d).wait_send()

    def came_x(n, plane, d):
        x_copy(n, plane, d, True).wait_recv()

    def each_x(n, plane, act, steps):
        for d in steps:
            wraps = x - d < 0 if act is came_x else x + d >= NX
            if plane == 1:
                act(n, plane, d)
            else:
                pl.when(wraps if plane == 0 else jnp.logical_not(wraps))(
                    functools.partial(act, n, plane, d)
                )

    beside = (1, NX - 1)
    inner = (x == 1) | (x == 2)

    def pass_on(n, plane, way, slot):
        at = plane * NX + (x + NX - way) % NX
        return remote(
            window.at[n, at],
            window.at[n, at],
            x_ss.at[n, plane, slot],
            x_rs.at[n, plane, 2],
            (me, z * NX + (x + NX + way) % NX),
        )

    def each_pass(n, plane, act):
        if plane == 1:

            @pl.when(jnp.logical_not(inner))
            def _():
                act(pass_on(n, plane, 1, 0))
                act(pass_on(n, plane, -1, 2))

        else:

            @pl.when(inner)
            def _():
                act(pass_on(n, plane, 1 if plane == 2 else -1, 2))

    def forward(n, plane):
        def go():
            each_x(n, plane, came_x, beside)
            each_pass(n, plane, lambda copy: copy.start())

        if plane == 2:
            go()
        else:
            pl.when(has_last if plane == 1 else zz >= 2)(go)

    def place_pairs(n):
        window[n, 2 * NX + x] = contract(
            put, recvs[n][:, :, :PIECE].reshape(SLOTS, PIECE), ((1,), (0,))
        ).astype(bf16)

        @pl.when(has_next)
        def _():
            z_copy(n, 2).start()

        each_x(n, 2, start_x, beside)

    def one_back(n):
        @pl.when(has_last)
        def _():
            z_copy(n, 2).wait_recv()

            @pl.when(has_next)
            def _():
                z_copy(n, 1).start()

            each_x(n, 1, start_x, beside)

    def two_back(n):
        @pl.when(zz >= 2)
        def _():
            z_copy(n, 1).wait_recv()
            each_x(n, 0, start_x, beside)

    def flag_x_copy(d, came=False):
        at = (x + NX - d) % NX if came else x
        return remote(
            flag_x.at[at],
            flag_x.at[at],
            fx_ss.at[d],
            fx_rs.at[d],
            (me, z * NX + (x + d) % NX),
        )

    def flag_z_copy(d, came=False):
        at = (z + NZ - d) % NZ if came else z
        return remote(
            flag_z.at[at],
            flag_z.at[at],
            fz_ss.at[d],
            fz_rs.at[d],
            (me, (z + d) % NZ * NX + x),
        )

    def pairs_came(n):
        @pl.loop(1, GROUPS)
        def _(d):
            kv_copy(n, d).wait_recv()

    pairs_came(0)
    marks_in = kva_recv[:, :, PIECE:].astype(f32)
    column = lax.broadcasted_iota(jnp.int32, (GROUPS, CAP, TOK), 2).astype(f32) + 1.0
    match = (marks_in == column).astype(f32)
    put = match.reshape(SLOTS, TOK).T.astype(bf16)
    place_pairs(0)
    worst = jnp.max((marks_in < 0.0).astype(f32).reshape(SLOTS, TOK), axis=0, keepdims=True)
    flag_x[x] = jnp.broadcast_to(worst, (CAP, TOK)).astype(bf16)
    for d in range(1, NX):
        flag_x_copy(d).start()
    put_low = both_halves(match[:, :LOW]).T.astype(bf16)

    ring_turn(2)
    start_queries(0)
    forward(0, 2)
    one_back(0)
    ring_turn(3)
    start_queries(1)
    pairs_came(1)
    place_pairs(1)
    for d in range(1, NX):
        flag_x_copy(d, True).wait_recv()
    flag_z[z] = jnp.max(flag_x[...].astype(f32), axis=0).astype(bf16)
    for d in range(1, NZ):
        flag_z_copy(d).start()
    two_back(0)
    start_queries(2)
    forward(0, 1)
    one_back(1)
    forward(1, 2)
    start_queries(3)
    ring_turn(4)
    two_back(1)
    forward(0, 0)
    for d in range(1, NZ):
        flag_z_copy(d, True).wait_recv()
    flag_ref[0, 0] = jnp.max(flag_z[...].astype(f32)).astype(jnp.int32)
    for n in range(NY):
        sibling_came(n)

    tags_in = over[:, :, HK * HALF_WIDE :].astype(f32)
    mine = (me + 1).astype(f32)
    match_over = ((tags_in[:, :OVER] == column[:, :OVER]) & (tags_in[:, OVER:] == mine)).astype(f32)
    put_over = both_halves(match_over).T.astype(bf16)

    ones = jnp.ones((SPAN, HD), bf16)

    def window_came(n):
        each_x(n, 2, came_x, (2,))

        @pl.when(has_last)
        def _():
            each_x(n, 1, came_x, (2,))

        @pl.when(zz >= 2)
        def _():
            each_x(n, 0, came_x, (2,))

    @pl.loop(0, HK)
    def _(j):
        @pl.when(j == 0)
        def _():
            window_came(0)

        @pl.when(j == 1)
        def _():
            forward(1, 1)
            forward(1, 0)

        @pl.when(j == 2)
        def _():
            window_came(1)

        @pl.loop(1, GROUPS)
        def _(d):
            q_copy(j, d).wait_recv()

        cols = pl.ds(pl.multiple_of(j * HALF_WIDE, HALF_WIDE), HALF_WIDE)
        rows = contract(put_low, q_recv[j].reshape(SLOTS, HALF_WIDE), ((1,), (0,)))
        rows = rows + contract(put_over, over[:, :, cols].reshape(SLOTS, HALF_WIDE), ((1,), (0,)))
        rows = rows.astype(bf16)
        for h in range(HQ // HK):
            half, at = h // (HQ // HK // 2), h % (HQ // HK // 2)
            placed[h] = rows[half * TOK : (half + 1) * TOK, at * HD : (at + 1) * HD]
        key_cols = pl.ds(pl.multiple_of(j % 2 * HD, HD), HD)
        value_cols = pl.ds(pl.multiple_of(PIECE // 2 + j % 2 * HD, HD), HD)
        for h in range(HQ // HK):
            keys = window[j // 2, pl.ds(x, BACK + 1), :, key_cols].reshape(SPAN, HD)
            values = window[j // 2, pl.ds(x, BACK + 1), :, value_cols].reshape(SPAN, HD)
            scores = contract(placed[h], keys, ((1,), (1,))) + mask[...]
            top = jnp.max(scores, axis=1, keepdims=True)
            weights = jnp.exp2((scores - top) * FACTOR).astype(bf16)
            summed = contract(weights, jnp.concatenate([values, ones], axis=1), ((1,), (0,)))
            head_cols = pl.ds(pl.multiple_of((j * (HQ // HK) + h) * HD, HD), HD)
            out_ref[0, :, head_cols] = (summed[:, :HD] / summed[:, HD:]).astype(bf16)


    @pl.loop(1, GROUPS)
    def _(d):
        for n in range(2):
            kv_copy(n, d).wait_send()
        for j in range(HK):
            q_copy(j, d).wait_send()

    for n in range(2):
        each_x(n, 2, sent_x, beside)
        each_pass(n, 2, lambda copy: copy.wait_send())

        @pl.when(has_next)
        def _(n=n):
            z_copy(n, 2).wait_send()

        @pl.when(has_last)
        def _(n=n):
            each_x(n, 1, sent_x, beside)
            each_pass(n, 1, lambda copy: copy.wait_send())

            @pl.when(has_next)
            def _():
                z_copy(n, 1).wait_send()

        @pl.when(zz >= 2)
        def _(n=n):
            each_x(n, 0, sent_x, beside)
            each_pass(n, 0, lambda copy: copy.wait_send())

    for step in range(1, NY // 2 + 1):
        ring(step, 0).wait_send()
        if step < NY // 2:
            ring(step, 1).wait_send()
    for n in range(NY):
        sibling(n).wait_send()
    for d in range(1, NX):
        flag_x_copy(d).wait_send()
    for d in range(1, NZ):
        flag_z_copy(d).wait_send()


def compact(*operands):
    bf16 = jnp.bfloat16
    dma = pltpu.SemaphoreType.DMA
    vmem = pltpu.VMEM
    return pl.pallas_call(
        compact_kernel,
        out_shape=(
            pltpu.VMEM((1, TOK, HQ * HD), bf16),
            jax.ShapeDtypeStruct((1, 1), jnp.int32),
        ),
        in_specs=[pl.BlockSpec(memory_space=pltpu.HBM)] * 5,
        out_specs=(pl.BlockSpec(memory_space=pltpu.VMEM), pl.BlockSpec(memory_space=pltpu.SMEM)),
        scratch_shapes=[
            vmem((2 * HK, TOK, HALF_WIDE), bf16),
            vmem((1, TOK, PAIR), bf16),
            vmem((1, TOK), jnp.int32),
            vmem((1, TOK), jnp.int32),
            pltpu.SMEM((1, 2, 3), jnp.int32),
            vmem((HK, GROUPS, CAP, HALF_WIDE), bf16),
            vmem((HK, GROUPS, CAP, HALF_WIDE), bf16),
            vmem((GROUPS, CAP, PIECE + TOK), bf16),
            vmem((GROUPS, CAP, PIECE + TOK), bf16),
            vmem((GROUPS, CAP, PIECE), bf16),
            vmem((GROUPS, CAP, PIECE), bf16),
            vmem((GROUPS, CAP, HK * HALF_WIDE + TOK), bf16),
            vmem((2, 3 * NX, TOK, PIECE), bf16),
            vmem((TOK, SPAN), jnp.float32),
            vmem((HQ // HK, TOK, HD), bf16),
            vmem((NX, CAP, TOK), bf16),
            vmem((NZ, CAP, TOK), bf16),
            dma((2 * HK + 4,)),
            dma((HK, GROUPS)),
            dma((HK, GROUPS)),
            dma((2, GROUPS)),
            dma((2, GROUPS)),
            dma((2, NY // 2 + 1)),
            dma((2, NY // 2 + 1)),
            dma((NY,)),
            dma((NY,)),
            dma((2, 3)),
            dma((2, 3)),
            dma((2, 3, NX)),
            dma((2, 3, NX)),
            dma((NX,)),
            dma((NX,)),
            dma((NZ,)),
            dma((NZ,)),
        ],
        compiler_params=pltpu.CompilerParams(
            collective_id=1, has_side_effects=True, vmem_limit_bytes=48 << 20
        ),
    )(*operands)


def local(*operands):
    operands = [pltpu.with_memory_space_constraint(one, pltpu.HBM) for one in operands]
    result, crowded = compact(*operands)
    return lax.switch(crowded[0, 0], [lambda: result, lambda: padded(*operands)])


def solution(mesh):
    return jax.shard_map(
        local,
        mesh=mesh,
        in_specs=(
            P("grp", "seq", None),
            P("grp", "seq", None),
            P("grp", "seq"),
            P("grp", "seq"),
            P("grp", None, None),
        ),
        out_specs=P("grp", "seq", None),
        check_vma=False,
    )
```

```python
import functools
import math

import jax
import jax.numpy as jnp
from jax import lax
from jax.experimental import pallas as pl
from jax.experimental.pallas import tpu as pltpu
from jax.sharding import PartitionSpec as P

HQ = 32
HK = 4
HD = 128
TOK = 128
GROUPS = 16
CAP = 16
SLOTS = GROUPS * CAP
WIDE = HQ // HK * HD
PAIR = 2 * HK * HD
BACK = 8
SPAN = (BACK + 1) * TOK
NX = 4
HALF_ROWS = 4
NEGATIVE = -1e30
MESH = pl.DeviceIdType.MESH
FACTOR = HD ** (-0.5) * math.log2(math.e)


def remote(src, dst, send, recv, device):
    return pltpu.make_async_remote_copy(
        src_ref=src,
        dst_ref=dst,
        send_sem=send,
        recv_sem=recv,
        device_id=device,
        device_id_type=MESH,
    )


def contract(a, b, dims):
    return lax.dot_general(a, b, (dims, ((), ())), preferred_element_type=jnp.float32)


def padded_kernel(
    q_hbm,
    kv_hbm,
    group_hbm,
    slot_hbm,
    length_hbm,
    out_hbm,
    q_in,
    kv_ref,
    group_ref,
    slot_ref,
    length_ref,
    q_send,
    q_recv,
    kv_send,
    kv_recv,
    window,
    mask,
    placed,
    out_buf,
    in_sem,
    out_sem,
    q_ss,
    q_rs,
    kv_ss,
    kv_rs,
    z_ss,
    z_rs,
    x_ss,
    x_rs,
):
    me = lax.axis_index("grp")
    seq = lax.axis_index("seq")
    z = seq // NX
    x = seq % NX
    zz = z % HALF_ROWS
    has_next = zz < HALF_ROWS - 1
    has_last = zz > 0

    def load(j):
        cols = pl.ds(j * WIDE, WIDE)
        return pltpu.make_async_copy(q_hbm.at[0, :, cols], q_in.at[:, cols], in_sem.at[j])

    small = [
        pltpu.make_async_copy(source, target, in_sem.at[HK + n])
        for n, (source, target) in enumerate(
            [
                (group_hbm, group_ref),
                (slot_hbm, slot_ref),
                (kv_hbm, kv_ref),
                (length_hbm, length_ref),
            ]
        )
    ]
    for copy in small:
        copy.start()
    for j in range(HK):
        load(j).start()

    barrier = pltpu.get_barrier_semaphore()

    def greet(group, place):
        pl.semaphore_signal(barrier, inc=1, device_id=(group, place), device_id_type=MESH)

    for d in range(1, GROUPS):
        greet((me + d) % GROUPS, seq)
    for d in range(1, NX):
        greet(me, z * NX + (x + d) % NX)

    @pl.when(has_next)
    def _():
        greet(me, seq + NX)

    @pl.when(has_last)
    def _():
        greet(me, seq - NX)

    for copy in small:
        copy.wait()
    targets = group_ref[...]
    lane = lax.broadcasted_iota(jnp.int32, (TOK, TOK), 1)
    sub = lax.broadcasted_iota(jnp.int32, (TOK, TOK), 0)
    hits = lax.broadcasted_iota(jnp.int32, (GROUPS, TOK), 0) == targets
    before = (sub < lane).astype(jnp.float32).astype(jnp.bfloat16)
    hits_f = hits.astype(jnp.float32)
    ranks = contract(hits_f.astype(jnp.bfloat16), before, ((1,), (0,)))
    ranks = jnp.where(hits, ranks, -1.0)
    level = lax.broadcasted_iota(jnp.int32, (GROUPS, CAP, TOK), 1).astype(jnp.float32)
    pick_f = (ranks[:, None, :] == level).astype(jnp.float32).reshape(SLOTS, TOK)
    pick = pick_f.astype(jnp.bfloat16)
    marks = (pick_f * (slot_ref[...] + 1).astype(jnp.float32)).astype(jnp.bfloat16)
    slots = contract(marks, jnp.ones((TOK, TOK), jnp.bfloat16), ((1,), (0,)))
    kv_send[:, :, PAIR:] = slots.astype(jnp.bfloat16).reshape(GROUPS, CAP, TOK)
    kv_send[:, :, :PAIR] = (
        contract(pick, kv_ref[0], ((1,), (0,))).astype(jnp.bfloat16).reshape(GROUPS, CAP, PAIR)
    )

    pl.semaphore_wait(
        barrier, GROUPS - 1 + NX - 1 + has_next.astype(jnp.int32) + has_last.astype(jnp.int32)
    )

    def kv_copy(d):
        target = (me + d) % GROUPS
        return remote(
            kv_send.at[target], kv_recv.at[me], kv_ss.at[d], kv_rs.at[d], (target, seq)
        )

    @pl.loop(1, GROUPS)
    def _(d):
        kv_copy(d).start()

    kv_recv[me] = kv_send[me]

    def q_copy(j, d):
        target = (me + d) % GROUPS
        return remote(
            q_send.at[j, target], q_recv.at[j, me], q_ss.at[j, d], q_rs.at[j, d], (target, seq)
        )

    for j in range(HK):
        load(j).wait()
        q_send[j] = (
            contract(pick, q_in[:, j * WIDE : (j + 1) * WIDE], ((1,), (0,)))
            .astype(jnp.bfloat16)
            .reshape(GROUPS, CAP, WIDE)
        )

        @pl.loop(1, GROUPS)
        def _(d, j=j):
            q_copy(j, d).start()

        q_recv[j, me] = q_send[j, me]

    query = seq * TOK + lax.broadcasted_iota(jnp.int32, (TOK, SPAN), 0)
    key = (seq - BACK) * TOK + lax.broadcasted_iota(jnp.int32, (TOK, SPAN), 1)
    begin = jnp.zeros((TOK, SPAN), jnp.int32)
    bound = jnp.int32(0)
    for half in range(2):
        for n in range(3):
            bound = bound + length_ref[0, half, n]
            begin = jnp.where(query >= bound, bound, begin)
    mask[...] = jnp.where((key >= begin) & (key <= query), 0.0, NEGATIVE)

    @pl.when(zz == 0)
    def _():
        window[pl.ds(0, 2 * NX)] = jnp.zeros((2 * NX, TOK, PAIR), jnp.bfloat16)

    @pl.when(zz == 1)
    def _():
        window[pl.ds(0, NX)] = jnp.zeros((NX, TOK, PAIR), jnp.bfloat16)

    @pl.loop(1, GROUPS)
    def _(d):
        kv_copy(d).wait_recv()

    marks_in = kv_recv[:, :, PAIR:].reshape(SLOTS, TOK).astype(jnp.float32)
    column = lax.broadcasted_iota(jnp.int32, (SLOTS, TOK), 1).astype(jnp.float32) + 1.0
    put = (marks_in == column).astype(jnp.float32).T.astype(jnp.bfloat16)
    window[2 * NX + x] = contract(
        put, kv_recv[:, :, :PAIR].reshape(SLOTS, PAIR), ((1,), (0,))
    ).astype(jnp.bfloat16)

    def z_copy(plane):
        return remote(
            window.at[plane * NX + x],
            window.at[(plane - 1) * NX + x],
            z_ss.at[plane],
            z_rs.at[plane],
            (me, (seq + NX) % (NX * 8)),
        )

    def x_copy(plane, d):
        return remote(
            window.at[plane * NX + x],
            window.at[plane * NX + x],
            x_ss.at[plane, d],
            x_rs.at[plane, d],
            (me, z * NX + (x + d) % NX),
        )

    def x_wait(plane, d):
        source = (x + NX - d) % NX
        return remote(
            window.at[plane * NX + source],
            window.at[plane * NX + source],
            x_ss.at[plane, d],
            x_rs.at[plane, d],
            (me, z * NX + (x + d) % NX),
        )

    def each_x(plane, act, sending):
        for d in range(1, NX):
            wraps = x + d >= NX if sending else x - d < 0
            if plane == 1:
                act(plane, d)
            else:
                pl.when(wraps if plane == 0 else jnp.logical_not(wraps))(
                    functools.partial(act, plane, d)
                )

    def start_x(plane, d):
        x_copy(plane, d).start()

    def sent_x(plane, d):
        x_copy(plane, d).wait_send()

    def came_x(plane, d):
        x_wait(plane, d).wait_recv()

    @pl.when(has_next)
    def _():
        z_copy(2).start()

    each_x(2, start_x, True)

    @pl.when(has_last)
    def _():
        z_copy(2).wait_recv()

        @pl.when(has_next)
        def _():
            z_copy(1).start()

        each_x(1, start_x, True)

    @pl.when(zz >= 2)
    def _():
        z_copy(1).wait_recv()
        each_x(0, start_x, True)

    each_x(2, came_x, False)

    @pl.when(has_last)
    def _():
        each_x(1, came_x, False)

    @pl.when(zz >= 2)
    def _():
        each_x(0, came_x, False)

    def store(j):
        cols = pl.ds(pl.multiple_of(j * WIDE, WIDE), WIDE)
        return pltpu.make_async_copy(out_buf.at[:, cols], out_hbm.at[0, :, cols], out_sem.at[j])

    ones = jnp.ones((SPAN, HD), jnp.bfloat16)

    @pl.loop(0, HK)
    def _(j):
        @pl.loop(1, GROUPS)
        def _(d):
            q_copy(j, d).wait_recv()

        rows = contract(put, q_recv[j].reshape(SLOTS, WIDE), ((1,), (0,))).astype(jnp.bfloat16)
        for h in range(HQ // HK):
            placed[h] = rows[:, h * HD : (h + 1) * HD]
        key_cols = pl.ds(pl.multiple_of(j * HD, HD), HD)
        value_cols = pl.ds(pl.multiple_of((HK + j) * HD, HD), HD)

        for h in range(HQ // HK):
            keys = window[pl.ds(x, BACK + 1), :, key_cols].reshape(SPAN, HD)
            values = window[pl.ds(x, BACK + 1), :, value_cols].reshape(SPAN, HD)
            scores = contract(placed[h], keys, ((1,), (1,))) + mask[...]
            top = jnp.max(scores, axis=1, keepdims=True)
            weights = jnp.exp2((scores - top) * FACTOR).astype(jnp.bfloat16)
            summed = contract(weights, jnp.concatenate([values, ones], axis=1), ((1,), (0,)))
            cols = pl.ds(pl.multiple_of((j * (HQ // HK) + h) * HD, HD), HD)
            out_buf[:, cols] = (summed[:, :HD] / summed[:, HD:]).astype(jnp.bfloat16)

        store(j).start()

    for j in range(HK):
        store(j).wait()

    @pl.loop(1, GROUPS)
    def _(d):
        kv_copy(d).wait_send()
        for j in range(HK):
            q_copy(j, d).wait_send()

    each_x(2, sent_x, True)

    @pl.when(has_next)
    def _():
        z_copy(2).wait_send()

    @pl.when(has_last)
    def _():
        each_x(1, sent_x, True)

        @pl.when(has_next)
        def _():
            z_copy(1).wait_send()

    @pl.when(zz >= 2)
    def _():
        each_x(0, sent_x, True)


def padded(queries, keys_values, route_group, route_slot, doc_lengths):
    bf16 = jnp.bfloat16
    dma = pltpu.SemaphoreType.DMA
    return pl.pallas_call(
        padded_kernel,
        out_shape=jax.ShapeDtypeStruct((1, TOK, HQ * HD), bf16),
        in_specs=[
            pl.BlockSpec(memory_space=pltpu.HBM),
            pl.BlockSpec(memory_space=pltpu.HBM),
            pl.BlockSpec(memory_space=pltpu.HBM),
            pl.BlockSpec(memory_space=pltpu.HBM),
            pl.BlockSpec(memory_space=pltpu.HBM),
        ],
        out_specs=pl.BlockSpec(memory_space=pl.ANY),
        scratch_shapes=[
            pltpu.VMEM((TOK, HQ * HD), bf16),
            pltpu.VMEM((1, TOK, PAIR), bf16),
            pltpu.VMEM((1, TOK), jnp.int32),
            pltpu.VMEM((1, TOK), jnp.int32),
            pltpu.SMEM((1, 2, 3), jnp.int32),
            pltpu.VMEM((HK, GROUPS, CAP, WIDE), bf16),
            pltpu.VMEM((HK, GROUPS, CAP, WIDE), bf16),
            pltpu.VMEM((GROUPS, CAP, PAIR + TOK), bf16),
            pltpu.VMEM((GROUPS, CAP, PAIR + TOK), bf16),
            pltpu.VMEM((3 * NX, TOK, PAIR), bf16),
            pltpu.VMEM((TOK, SPAN), jnp.float32),
            pltpu.VMEM((HQ // HK, TOK, HD), bf16),
            pltpu.VMEM((TOK, HQ * HD), bf16),
            dma((HK + 4,)),
            dma((HK,)),
            dma((HK, GROUPS)),
            dma((HK, GROUPS)),
            dma((GROUPS,)),
            dma((GROUPS,)),
            dma((3,)),
            dma((3,)),
            dma((3, NX)),
            dma((3, NX)),
        ],
        compiler_params=pltpu.CompilerParams(
            collective_id=0, has_side_effects=True, vmem_limit_bytes=48 << 20
        ),
    )(queries, keys_values, route_group, route_slot, doc_lengths)


LOW = 8
OVER = 8
HALF_WIDE = WIDE // 2
PIECE = PAIR // 2
NY = GROUPS // 2
NZ = 2 * HALF_ROWS


def both_halves(one):
    none = jnp.zeros_like(one)
    left = jnp.concatenate([one, none], axis=1)
    right = jnp.concatenate([none, one], axis=1)
    lanes = one.shape[2]
    return jnp.concatenate([left.reshape(-1, lanes), right.reshape(-1, lanes)], axis=1)


def compact_kernel(
    q_hbm,
    kv_hbm,
    group_hbm,
    slot_hbm,
    length_hbm,
    out_ref,
    flag_ref,
    q_in,
    kv_ref,
    group_ref,
    slot_ref,
    length_ref,
    q_send,
    q_recv,
    kva_send,
    kva_recv,
    kvb_send,
    kvb_recv,
    over,
    window,
    mask,
    placed,
    flag_x,
    flag_z,
    in_sem,
    q_ss,
    q_rs,
    kv_ss,
    kv_rs,
    ring_ss,
    ring_rs,
    sib_ss,
    sib_rs,
    z_ss,
    z_rs,
    x_ss,
    x_rs,
    fx_ss,
    fx_rs,
    fz_ss,
    fz_rs,
):
    bf16 = jnp.bfloat16
    f32 = jnp.float32
    me = lax.axis_index("grp")
    seq = lax.axis_index("seq")
    z = seq // NX
    x = seq % NX
    zz = z % HALF_ROWS
    y = me // 2
    core = me % 2
    has_next = zz < HALF_ROWS - 1
    has_last = zz > 0

    small = [
        pltpu.make_async_copy(source, target, in_sem.at[2 * HK + n])
        for n, (source, target) in enumerate(
            [
                (group_hbm, group_ref),
                (slot_hbm, slot_ref),
                (kv_hbm, kv_ref),
                (length_hbm, length_ref),
            ]
        )
    ]
    loads = [
        pltpu.make_async_copy(
            q_hbm.at[0, :, pl.ds(n * HALF_WIDE, HALF_WIDE)], q_in.at[n], in_sem.at[n]
        )
        for n in range(2 * HK)
    ]
    for copy in small + loads:
        copy.start()

    barrier = pltpu.get_barrier_semaphore()

    def greet(group, place):
        pl.semaphore_signal(barrier, inc=1, device_id=(group, place), device_id_type=MESH)

    for d in range(1, GROUPS):
        greet((me + d) % GROUPS, seq)
    for d in range(1, NX):
        greet(me, z * NX + (x + d) % NX)
    for d in range(1, NZ):
        greet(me, (z + d) % NZ * NX + x)

    for copy in small:
        copy.wait()
    targets = group_ref[...]
    lane = lax.broadcasted_iota(jnp.int32, (TOK, TOK), 1)
    sub = lax.broadcasted_iota(jnp.int32, (TOK, TOK), 0)
    hits = lax.broadcasted_iota(jnp.int32, (GROUPS, TOK), 0) == targets
    before = (sub < lane).astype(f32).astype(bf16)
    all_ones = jnp.ones((TOK, TOK), bf16)
    ranks = contract(hits.astype(f32).astype(bf16), before, ((1,), (0,)))
    ranks = jnp.where(hits, ranks, -1.0)
    level = lax.broadcasted_iota(jnp.int32, (GROUPS, CAP, TOK), 1).astype(f32)
    pick_three = (ranks[:, None, :] == level).astype(f32)
    pick_f = pick_three.reshape(SLOTS, TOK)
    pick = pick_f.astype(bf16)
    places = (slot_ref[...] + 1).astype(f32)
    beyond = jnp.sum((ranks >= LOW).astype(f32), axis=0, keepdims=True)
    order = contract(jnp.broadcast_to(beyond, (OVER, TOK)).astype(bf16), before, ((1,), (0,)))
    row = lax.broadcasted_iota(jnp.int32, (OVER, TOK), 0).astype(f32)
    extra = jnp.where((order == row) & (beyond > 0.0), 1.0, 0.0)
    crowded = jnp.sum(beyond, axis=1, keepdims=True) > OVER
    marks = contract((pick_f * places).astype(bf16), all_ones, ((1,), (0,)))
    marks = jnp.where(crowded, -1.0, marks)
    kva_send[:, :, PIECE:] = marks.astype(bf16).reshape(GROUPS, CAP, TOK)

    sends = [kva_send, kvb_send]
    recvs = [kva_recv, kvb_recv]

    def pack_pairs(n):
        for part in range(2):
            cols = kv_ref[0, :, part * PIECE + n * PIECE // 2 : part * PIECE + (n + 1) * PIECE // 2]
            sends[n][:, :, part * PIECE // 2 : (part + 1) * PIECE // 2] = (
                contract(pick, cols, ((1,), (0,))).astype(bf16).reshape(GROUPS, CAP, PIECE // 2)
            )

    def partner(d):
        return (y + d // 2) % NY * 2 + (core + d % 2) % 2

    def far_first(act):
        @pl.loop(0, NY - 1)
        def _(i):
            away = NY // 2 + i // 2 * (1 - i % 2) - (i + 1) // 2 * (i % 2)
            act(2 * away)
            act(2 * away + 1)

        act(1)

    def kv_copy(n, d):
        target = partner(d)
        return remote(
            sends[n].at[target], recvs[n].at[me], kv_ss.at[n, d], kv_rs.at[n, d], (target, seq)
        )

    def start_pairs(n):
        far_first(lambda d: kv_copy(n, d).start())
        recvs[n][me] = sends[n][me]

    pack_pairs(0)

    high = both_halves(extra[None]).astype(bf16)
    for j in range(HK):
        loads[2 * j].wait()
        loads[2 * j + 1].wait()
        halves = q_in[2 * j : 2 * j + 2].reshape(2 * TOK, HALF_WIDE)
        over[me, :, j * HALF_WIDE : (j + 1) * HALF_WIDE] = contract(
            high, halves, ((1,), (0,))
        ).astype(bf16)
    tags = jnp.concatenate([extra * places, extra * (targets + 1).astype(f32)], axis=0)
    over[me, :, HK * HALF_WIDE :] = contract(tags.astype(bf16), all_ones, ((1,), (0,))).astype(bf16)
    turn = 1 - 2 * core

    def on_ring(at):
        return (at + 2 * NY) % NY * 2 + core

    def on_sibling(at):
        return (at + 2 * NY) % NY * 2 + 1 - core

    def ring(step, way):
        sign = turn if way == 0 else -turn
        block = on_ring(y - sign * (step - 1))
        return remote(
            over.at[block],
            over.at[block],
            ring_ss.at[way, step],
            ring_rs.at[way, step],
            (on_ring(y + sign), seq),
        )

    def ring_came(step, way):
        sign = turn if way == 0 else -turn
        block = on_ring(y - sign * step)
        remote(
            over.at[block],
            over.at[block],
            ring_ss.at[way, step],
            ring_rs.at[way, step],
            (on_ring(y + sign), seq),
        ).wait_recv()

    def sibling(n):
        block = on_ring(y - turn * n if n <= NY // 2 else y + turn * (n - NY // 2))
        return remote(
            over.at[block], over.at[block], sib_ss.at[n], sib_rs.at[n], (on_sibling(y), seq)
        )

    def sibling_came(n):
        block = on_sibling(y + turn * n if n <= NY // 2 else y - turn * (n - NY // 2))
        remote(
            over.at[block], over.at[block], sib_ss.at[n], sib_rs.at[n], (on_sibling(y), seq)
        ).wait_recv()

    def ring_turn(step):
        ring_came(step, 0)
        if step < NY // 2:
            ring(step + 1, 0).start()
            ring_came(step, 1)
            if step + 1 < NY // 2:
                ring(step + 1, 1).start()
            sibling(NY // 2 + step).start()
        sibling(step).start()

    pl.semaphore_wait(barrier, GROUPS - 1 + NX - 1 + NZ - 1)
    ring(1, 0).start()
    ring(1, 1).start()
    start_pairs(0)
    sibling(0).start()
    pack_pairs(1)

    ring_turn(1)
    start_pairs(1)

    low = both_halves(pick_three[:, :LOW]).astype(bf16)
    for j in range(HK):
        halves = q_in[2 * j : 2 * j + 2].reshape(2 * TOK, HALF_WIDE)
        q_send[j] = (
            contract(low, halves, ((1,), (0,))).astype(bf16).reshape(GROUPS, CAP, HALF_WIDE)
        )

    def q_copy(j, d, part=None):
        target = partner(d)
        source, goal, sem = q_send.at[j, target], q_recv.at[j, me], j
        if part is not None:
            cols = pl.ds(part * (HALF_WIDE // 2), HALF_WIDE // 2)
            source, goal, sem = source.at[:, cols], goal.at[:, cols], j + part
        return remote(source, goal, q_ss.at[sem, d], q_rs.at[sem, d], (target, seq))

    def start_queries(j):
        if j < HK - 1:
            far_first(lambda d: q_copy(j, d).start())
        else:
            for part in range(2):
                far_first(lambda d, part=part: q_copy(j, d, part).start())
        q_recv[j, me] = q_send[j, me]

    query = seq * TOK + lax.broadcasted_iota(jnp.int32, (TOK, SPAN), 0)
    key = (seq - BACK) * TOK + lax.broadcasted_iota(jnp.int32, (TOK, SPAN), 1)
    begin = jnp.zeros((TOK, SPAN), jnp.int32)
    bound = jnp.int32(0)
    for half in range(2):
        for n in range(3):
            bound = bound + length_ref[0, half, n]
            begin = jnp.where(query >= bound, bound, begin)
    mask[...] = jnp.where((key >= begin) & (key <= query), 0.0, NEGATIVE)

    @pl.when(zz == 0)
    def _():
        window[:, pl.ds(0, 2 * NX)] = jnp.zeros((2, 2 * NX, TOK, PIECE), bf16)

    @pl.when(zz == 1)
    def _():
        window[:, pl.ds(0, NX)] = jnp.zeros((2, NX, TOK, PIECE), bf16)

    def z_copy(n, plane):
        return remote(
            window.at[n, plane * NX + x],
            window.at[n, (plane - 1) * NX + x],
            z_ss.at[n, plane],
            z_rs.at[n, plane],
            (me, (seq + NX) % (NX * NZ)),
        )

    def x_copy(n, plane, d, came=False):
        at = plane * NX + ((x + NX - d) % NX if came else x)
        return remote(
            window.at[n, at],
            window.at[n, at],
            x_ss.at[n, plane, d],
            x_rs.at[n, plane, d],
            (me, z * NX + (x + d) % NX),
        )

    def start_x(n, plane, d):
        x_copy(n, plane, d).start()

    def sent_x(n, plane, d):
        x_copy(n, plane, d).wait_send()

    def came_x(n, plane, d):
        x_copy(n, plane, d, True).wait_recv()

    def each_x(n, plane, act, steps):
        for d in steps:
            wraps = x - d < 0 if act is came_x else x + d >= NX
            if plane == 1:
                act(n, plane, d)
            else:
                pl.when(wraps if plane == 0 else jnp.logical_not(wraps))(
                    functools.partial(act, n, plane, d)
                )

    beside = (1, NX - 1)
    inner = (x == 1) | (x == 2)

    def pass_on(n, plane, way, slot):
        at = plane * NX + (x + NX - way) % NX
        return remote(
            window.at[n, at],
            window.at[n, at],
            x_ss.at[n, plane, slot],
            x_rs.at[n, plane, 2],
            (me, z * NX + (x + NX + way) % NX),
        )

    def each_pass(n, plane, act):
        if plane == 1:

            @pl.when(jnp.logical_not(inner))
            def _():
                act(pass_on(n, plane, 1, 0))
                act(pass_on(n, plane, -1, 2))

        else:

            @pl.when(inner)
            def _():
                act(pass_on(n, plane, 1 if plane == 2 else -1, 2))

    def forward(n, plane):
        def go():
            each_x(n, plane, came_x, beside)
            each_pass(n, plane, lambda copy: copy.start())

        if plane == 2:
            go()
        else:
            pl.when(has_last if plane == 1 else zz >= 2)(go)

    def place_pairs(n):
        window[n, 2 * NX + x] = contract(
            put, recvs[n][:, :, :PIECE].reshape(SLOTS, PIECE), ((1,), (0,))
        ).astype(bf16)

        @pl.when(has_next)
        def _():
            z_copy(n, 2).start()

        each_x(n, 2, start_x, beside)

    def one_back(n):
        @pl.when(has_last)
        def _():
            z_copy(n, 2).wait_recv()

            @pl.when(has_next)
            def _():
                z_copy(n, 1).start()

            each_x(n, 1, start_x, beside)

    def two_back(n):
        @pl.when(zz >= 2)
        def _():
            z_copy(n, 1).wait_recv()
            each_x(n, 0, start_x, beside)

    def flag_x_copy(d, came=False):
        at = (x + NX - d) % NX if came else x
        return remote(
            flag_x.at[at],
            flag_x.at[at],
            fx_ss.at[d],
            fx_rs.at[d],
            (me, z * NX + (x + d) % NX),
        )

    def flag_z_copy(d, came=False):
        at = (z + NZ - d) % NZ if came else z
        return remote(
            flag_z.at[at],
            flag_z.at[at],
            fz_ss.at[d],
            fz_rs.at[d],
            (me, (z + d) % NZ * NX + x),
        )

    def pairs_came(n):
        @pl.loop(1, GROUPS)
        def _(d):
            kv_copy(n, d).wait_recv()

    ring_turn(2)
    start_queries(0)
    pairs_came(0)
    marks_in = kva_recv[:, :, PIECE:].astype(f32)
    column = lax.broadcasted_iota(jnp.int32, (GROUPS, CAP, TOK), 2).astype(f32) + 1.0
    match = (marks_in == column).astype(f32)
    put = match.reshape(SLOTS, TOK).T.astype(bf16)
    place_pairs(0)
    worst = jnp.max((marks_in < 0.0).astype(f32).reshape(SLOTS, TOK), axis=0, keepdims=True)
    flag_x[x] = jnp.broadcast_to(worst, (CAP, TOK)).astype(bf16)
    for d in range(1, NX):
        flag_x_copy(d).start()
    put_low = both_halves(match[:, :LOW]).T.astype(bf16)

    forward(0, 2)
    one_back(0)
    ring_turn(3)
    start_queries(1)
    pairs_came(1)
    place_pairs(1)
    for d in range(1, NX):
        flag_x_copy(d, True).wait_recv()
    flag_z[z] = jnp.max(flag_x[...].astype(f32), axis=0).astype(bf16)
    for d in range(1, NZ):
        flag_z_copy(d).start()
    two_back(0)
    start_queries(2)
    forward(0, 1)
    one_back(1)
    forward(1, 2)
    start_queries(3)
    ring_turn(4)
    two_back(1)
    forward(0, 0)
    for d in range(1, NZ):
        flag_z_copy(d, True).wait_recv()
    flag_ref[0, 0] = jnp.max(flag_z[...].astype(f32)).astype(jnp.int32)
    for n in range(NY):
        sibling_came(n)

    tags_in = over[:, :, HK * HALF_WIDE :].astype(f32)
    mine = (me + 1).astype(f32)
    match_over = ((tags_in[:, :OVER] == column[:, :OVER]) & (tags_in[:, OVER:] == mine)).astype(f32)
    put_over = both_halves(match_over).T.astype(bf16)

    ones = jnp.ones((SPAN, HD), bf16)

    def window_came(n):
        each_x(n, 2, came_x, (2,))

        @pl.when(has_last)
        def _():
            each_x(n, 1, came_x, (2,))

        @pl.when(zz >= 2)
        def _():
            each_x(n, 0, came_x, (2,))

    def place_queries(j, cols, over_cols):
        rows = contract(put_low, q_recv[j, :, :, cols].reshape(SLOTS, -1), ((1,), (0,)))
        rows = rows + contract(put_over, over[:, :, over_cols].reshape(SLOTS, -1), ((1,), (0,)))
        rows = rows.astype(bf16)
        count = rows.shape[1] // HD
        for n in range(2 * count):
            half, at = n // count, n % count
            placed[n] = rows[half * TOK : (half + 1) * TOK, at * HD : (at + 1) * HD]

    def attend(j, heads):
        key_cols = pl.ds(pl.multiple_of(j % 2 * HD, HD), HD)
        value_cols = pl.ds(pl.multiple_of(PIECE // 2 + j % 2 * HD, HD), HD)
        for n, h in enumerate(heads):
            keys = window[j // 2, pl.ds(x, BACK + 1), :, key_cols].reshape(SPAN, HD)
            values = window[j // 2, pl.ds(x, BACK + 1), :, value_cols].reshape(SPAN, HD)
            scores = contract(placed[n], keys, ((1,), (1,))) + mask[...]
            top = jnp.max(scores, axis=1, keepdims=True)
            weights = jnp.exp2((scores - top) * FACTOR).astype(bf16)
            summed = contract(weights, jnp.concatenate([values, ones], axis=1), ((1,), (0,)))
            head_cols = pl.ds(pl.multiple_of((j * (HQ // HK) + h) * HD, HD), HD)
            out_ref[0, :, head_cols] = (summed[:, :HD] / summed[:, HD:]).astype(bf16)

    @pl.loop(0, HK - 1)
    def _(j):
        @pl.when(j == 0)
        def _():
            window_came(0)

        @pl.when(j == 1)
        def _():
            forward(1, 1)
            forward(1, 0)

        @pl.when(j == 2)
        def _():
            window_came(1)

        @pl.loop(1, GROUPS)
        def _(d):
            q_copy(j, d).wait_recv()

        cols = pl.ds(pl.multiple_of(j * HALF_WIDE, HALF_WIDE), HALF_WIDE)
        place_queries(j, slice(None), cols)
        attend(j, range(HQ // HK))

    @pl.loop(1, GROUPS)
    def _(d):
        for n in range(2):
            kv_copy(n, d).wait_send()
        for j in range(HK - 1):
            q_copy(j, d).wait_send()

    for n in range(2):
        each_x(n, 2, sent_x, beside)
        each_pass(n, 2, lambda copy: copy.wait_send())

        @pl.when(has_next)
        def _(n=n):
            z_copy(n, 2).wait_send()

        @pl.when(has_last)
        def _(n=n):
            each_x(n, 1, sent_x, beside)
            each_pass(n, 1, lambda copy: copy.wait_send())

            @pl.when(has_next)
            def _():
                z_copy(n, 1).wait_send()

        @pl.when(zz >= 2)
        def _(n=n):
            each_x(n, 0, sent_x, beside)
            each_pass(n, 0, lambda copy: copy.wait_send())

    for step in range(1, NY // 2 + 1):
        ring(step, 0).wait_send()
        if step < NY // 2:
            ring(step, 1).wait_send()
    for n in range(NY):
        sibling(n).wait_send()
    for d in range(1, NX):
        flag_x_copy(d).wait_send()
    for d in range(1, NZ):
        flag_z_copy(d).wait_send()

    last = HK - 1
    quarter = HQ // HK // 4
    for part in range(2):

        @pl.loop(1, GROUPS)
        def _(d, part=part):
            q_copy(last, d, part).wait()

        at = part * HALF_WIDE // 2
        start = last * HALF_WIDE + at
        place_queries(last, slice(at, at + HALF_WIDE // 2), slice(start, start + HALF_WIDE // 2))
        attend(last, [2 * quarter * half + part * quarter + n for half in range(2) for n in range(quarter)])


def compact(*operands):
    bf16 = jnp.bfloat16
    dma = pltpu.SemaphoreType.DMA
    vmem = pltpu.VMEM
    return pl.pallas_call(
        compact_kernel,
        out_shape=(
            pltpu.VMEM((1, TOK, HQ * HD), bf16),
            jax.ShapeDtypeStruct((1, 1), jnp.int32),
        ),
        in_specs=[pl.BlockSpec(memory_space=pltpu.HBM)] * 5,
        out_specs=(pl.BlockSpec(memory_space=pltpu.VMEM), pl.BlockSpec(memory_space=pltpu.SMEM)),
        scratch_shapes=[
            vmem((2 * HK, TOK, HALF_WIDE), bf16),
            vmem((1, TOK, PAIR), bf16),
            vmem((1, TOK), jnp.int32),
            vmem((1, TOK), jnp.int32),
            pltpu.SMEM((1, 2, 3), jnp.int32),
            vmem((HK, GROUPS, CAP, HALF_WIDE), bf16),
            vmem((HK, GROUPS, CAP, HALF_WIDE), bf16),
            vmem((GROUPS, CAP, PIECE + TOK), bf16),
            vmem((GROUPS, CAP, PIECE + TOK), bf16),
            vmem((GROUPS, CAP, PIECE), bf16),
            vmem((GROUPS, CAP, PIECE), bf16),
            vmem((GROUPS, CAP, HK * HALF_WIDE + TOK), bf16),
            vmem((2, 3 * NX, TOK, PIECE), bf16),
            vmem((TOK, SPAN), jnp.float32),
            vmem((HQ // HK, TOK, HD), bf16),
            vmem((NX, CAP, TOK), bf16),
            vmem((NZ, CAP, TOK), bf16),
            dma((2 * HK + 4,)),
            dma((HK + 1, GROUPS)),
            dma((HK + 1, GROUPS)),
            dma((2, GROUPS)),
            dma((2, GROUPS)),
            dma((2, NY // 2 + 1)),
            dma((2, NY // 2 + 1)),
            dma((NY,)),
            dma((NY,)),
            dma((2, 3)),
            dma((2, 3)),
            dma((2, 3, NX)),
            dma((2, 3, NX)),
            dma((NX,)),
            dma((NX,)),
            dma((NZ,)),
            dma((NZ,)),
        ],
        compiler_params=pltpu.CompilerParams(
            collective_id=1, has_side_effects=True, vmem_limit_bytes=48 << 20
        ),
    )(*operands)


def local(*operands):
    operands = [pltpu.with_memory_space_constraint(one, pltpu.HBM) for one in operands]
    result, crowded = compact(*operands)
    return lax.switch(crowded[0, 0], [lambda: result, lambda: padded(*operands)])


def solution(mesh):
    return jax.shard_map(
        local,
        mesh=mesh,
        in_specs=(
            P("grp", "seq", None),
            P("grp", "seq", None),
            P("grp", "seq"),
            P("grp", "seq"),
            P("grp", None, None),
        ),
        out_specs=P("grp", "seq", None),
        check_vma=False,
    )
```

```python
import functools
import math

import jax
import jax.numpy as jnp
from jax import lax
from jax.experimental import pallas as pl
from jax.experimental.pallas import tpu as pltpu
from jax.sharding import PartitionSpec as P

HQ = 32
HK = 4
HD = 128
TOK = 128
GROUPS = 16
CAP = 16
SLOTS = GROUPS * CAP
WIDE = HQ // HK * HD
PAIR = 2 * HK * HD
BACK = 8
SPAN = (BACK + 1) * TOK
NX = 4
HALF_ROWS = 4
NEGATIVE = -1e30
MESH = pl.DeviceIdType.MESH
FACTOR = HD ** (-0.5) * math.log2(math.e)


def remote(src, dst, send, recv, device):
    return pltpu.make_async_remote_copy(
        src_ref=src,
        dst_ref=dst,
        send_sem=send,
        recv_sem=recv,
        device_id=device,
        device_id_type=MESH,
    )


def contract(a, b, dims):
    return lax.dot_general(a, b, (dims, ((), ())), preferred_element_type=jnp.float32)


def padded_kernel(
    q_hbm,
    kv_hbm,
    group_hbm,
    slot_hbm,
    length_hbm,
    out_hbm,
    q_in,
    kv_ref,
    group_ref,
    slot_ref,
    length_ref,
    q_send,
    q_recv,
    kv_send,
    kv_recv,
    window,
    mask,
    placed,
    out_buf,
    in_sem,
    out_sem,
    q_ss,
    q_rs,
    kv_ss,
    kv_rs,
    z_ss,
    z_rs,
    x_ss,
    x_rs,
):
    me = lax.axis_index("grp")
    seq = lax.axis_index("seq")
    z = seq // NX
    x = seq % NX
    zz = z % HALF_ROWS
    has_next = zz < HALF_ROWS - 1
    has_last = zz > 0

    def load(j):
        cols = pl.ds(j * WIDE, WIDE)
        return pltpu.make_async_copy(q_hbm.at[0, :, cols], q_in.at[:, cols], in_sem.at[j])

    small = [
        pltpu.make_async_copy(source, target, in_sem.at[HK + n])
        for n, (source, target) in enumerate(
            [
                (group_hbm, group_ref),
                (slot_hbm, slot_ref),
                (kv_hbm, kv_ref),
                (length_hbm, length_ref),
            ]
        )
    ]
    for copy in small:
        copy.start()
    for j in range(HK):
        load(j).start()

    barrier = pltpu.get_barrier_semaphore()

    def greet(group, place):
        pl.semaphore_signal(barrier, inc=1, device_id=(group, place), device_id_type=MESH)

    for d in range(1, GROUPS):
        greet((me + d) % GROUPS, seq)
    for d in range(1, NX):
        greet(me, z * NX + (x + d) % NX)

    @pl.when(has_next)
    def _():
        greet(me, seq + NX)

    @pl.when(has_last)
    def _():
        greet(me, seq - NX)

    for copy in small:
        copy.wait()
    targets = group_ref[...]
    lane = lax.broadcasted_iota(jnp.int32, (TOK, TOK), 1)
    sub = lax.broadcasted_iota(jnp.int32, (TOK, TOK), 0)
    hits = lax.broadcasted_iota(jnp.int32, (GROUPS, TOK), 0) == targets
    before = (sub < lane).astype(jnp.float32).astype(jnp.bfloat16)
    hits_f = hits.astype(jnp.float32)
    ranks = contract(hits_f.astype(jnp.bfloat16), before, ((1,), (0,)))
    ranks = jnp.where(hits, ranks, -1.0)
    level = lax.broadcasted_iota(jnp.int32, (GROUPS, CAP, TOK), 1).astype(jnp.float32)
    pick_f = (ranks[:, None, :] == level).astype(jnp.float32).reshape(SLOTS, TOK)
    pick = pick_f.astype(jnp.bfloat16)
    marks = (pick_f * (slot_ref[...] + 1).astype(jnp.float32)).astype(jnp.bfloat16)
    slots = contract(marks, jnp.ones((TOK, TOK), jnp.bfloat16), ((1,), (0,)))
    kv_send[:, :, PAIR:] = slots.astype(jnp.bfloat16).reshape(GROUPS, CAP, TOK)
    kv_send[:, :, :PAIR] = (
        contract(pick, kv_ref[0], ((1,), (0,))).astype(jnp.bfloat16).reshape(GROUPS, CAP, PAIR)
    )

    pl.semaphore_wait(
        barrier, GROUPS - 1 + NX - 1 + has_next.astype(jnp.int32) + has_last.astype(jnp.int32)
    )

    def kv_copy(d):
        target = (me + d) % GROUPS
        return remote(
            kv_send.at[target], kv_recv.at[me], kv_ss.at[d], kv_rs.at[d], (target, seq)
        )

    @pl.loop(1, GROUPS)
    def _(d):
        kv_copy(d).start()

    kv_recv[me] = kv_send[me]

    def q_copy(j, d):
        target = (me + d) % GROUPS
        return remote(
            q_send.at[j, target], q_recv.at[j, me], q_ss.at[j, d], q_rs.at[j, d], (target, seq)
        )

    for j in range(HK):
        load(j).wait()
        q_send[j] = (
            contract(pick, q_in[:, j * WIDE : (j + 1) * WIDE], ((1,), (0,)))
            .astype(jnp.bfloat16)
            .reshape(GROUPS, CAP, WIDE)
        )

        @pl.loop(1, GROUPS)
        def _(d, j=j):
            q_copy(j, d).start()

        q_recv[j, me] = q_send[j, me]

    query = seq * TOK + lax.broadcasted_iota(jnp.int32, (TOK, SPAN), 0)
    key = (seq - BACK) * TOK + lax.broadcasted_iota(jnp.int32, (TOK, SPAN), 1)
    begin = jnp.zeros((TOK, SPAN), jnp.int32)
    bound = jnp.int32(0)
    for half in range(2):
        for n in range(3):
            bound = bound + length_ref[0, half, n]
            begin = jnp.where(query >= bound, bound, begin)
    mask[...] = jnp.where((key >= begin) & (key <= query), 0.0, NEGATIVE)

    @pl.when(zz == 0)
    def _():
        window[pl.ds(0, 2 * NX)] = jnp.zeros((2 * NX, TOK, PAIR), jnp.bfloat16)

    @pl.when(zz == 1)
    def _():
        window[pl.ds(0, NX)] = jnp.zeros((NX, TOK, PAIR), jnp.bfloat16)

    @pl.loop(1, GROUPS)
    def _(d):
        kv_copy(d).wait_recv()

    marks_in = kv_recv[:, :, PAIR:].reshape(SLOTS, TOK).astype(jnp.float32)
    column = lax.broadcasted_iota(jnp.int32, (SLOTS, TOK), 1).astype(jnp.float32) + 1.0
    put = (marks_in == column).astype(jnp.float32).T.astype(jnp.bfloat16)
    window[2 * NX + x] = contract(
        put, kv_recv[:, :, :PAIR].reshape(SLOTS, PAIR), ((1,), (0,))
    ).astype(jnp.bfloat16)

    def z_copy(plane):
        return remote(
            window.at[plane * NX + x],
            window.at[(plane - 1) * NX + x],
            z_ss.at[plane],
            z_rs.at[plane],
            (me, (seq + NX) % (NX * 8)),
        )

    def x_copy(plane, d):
        return remote(
            window.at[plane * NX + x],
            window.at[plane * NX + x],
            x_ss.at[plane, d],
            x_rs.at[plane, d],
            (me, z * NX + (x + d) % NX),
        )

    def x_wait(plane, d):
        source = (x + NX - d) % NX
        return remote(
            window.at[plane * NX + source],
            window.at[plane * NX + source],
            x_ss.at[plane, d],
            x_rs.at[plane, d],
            (me, z * NX + (x + d) % NX),
        )

    def each_x(plane, act, sending):
        for d in range(1, NX):
            wraps = x + d >= NX if sending else x - d < 0
            if plane == 1:
                act(plane, d)
            else:
                pl.when(wraps if plane == 0 else jnp.logical_not(wraps))(
                    functools.partial(act, plane, d)
                )

    def start_x(plane, d):
        x_copy(plane, d).start()

    def sent_x(plane, d):
        x_copy(plane, d).wait_send()

    def came_x(plane, d):
        x_wait(plane, d).wait_recv()

    @pl.when(has_next)
    def _():
        z_copy(2).start()

    each_x(2, start_x, True)

    @pl.when(has_last)
    def _():
        z_copy(2).wait_recv()

        @pl.when(has_next)
        def _():
            z_copy(1).start()

        each_x(1, start_x, True)

    @pl.when(zz >= 2)
    def _():
        z_copy(1).wait_recv()
        each_x(0, start_x, True)

    each_x(2, came_x, False)

    @pl.when(has_last)
    def _():
        each_x(1, came_x, False)

    @pl.when(zz >= 2)
    def _():
        each_x(0, came_x, False)

    def store(j):
        cols = pl.ds(pl.multiple_of(j * WIDE, WIDE), WIDE)
        return pltpu.make_async_copy(out_buf.at[:, cols], out_hbm.at[0, :, cols], out_sem.at[j])

    ones = jnp.ones((SPAN, HD), jnp.bfloat16)

    @pl.loop(0, HK)
    def _(j):
        @pl.loop(1, GROUPS)
        def _(d):
            q_copy(j, d).wait_recv()

        rows = contract(put, q_recv[j].reshape(SLOTS, WIDE), ((1,), (0,))).astype(jnp.bfloat16)
        for h in range(HQ // HK):
            placed[h] = rows[:, h * HD : (h + 1) * HD]
        key_cols = pl.ds(pl.multiple_of(j * HD, HD), HD)
        value_cols = pl.ds(pl.multiple_of((HK + j) * HD, HD), HD)

        for h in range(HQ // HK):
            keys = window[pl.ds(x, BACK + 1), :, key_cols].reshape(SPAN, HD)
            values = window[pl.ds(x, BACK + 1), :, value_cols].reshape(SPAN, HD)
            scores = contract(placed[h], keys, ((1,), (1,))) + mask[...]
            top = jnp.max(scores, axis=1, keepdims=True)
            weights = jnp.exp2((scores - top) * FACTOR).astype(jnp.bfloat16)
            summed = contract(weights, jnp.concatenate([values, ones], axis=1), ((1,), (0,)))
            cols = pl.ds(pl.multiple_of((j * (HQ // HK) + h) * HD, HD), HD)
            out_buf[:, cols] = (summed[:, :HD] / summed[:, HD:]).astype(jnp.bfloat16)

        store(j).start()

    for j in range(HK):
        store(j).wait()

    @pl.loop(1, GROUPS)
    def _(d):
        kv_copy(d).wait_send()
        for j in range(HK):
            q_copy(j, d).wait_send()

    each_x(2, sent_x, True)

    @pl.when(has_next)
    def _():
        z_copy(2).wait_send()

    @pl.when(has_last)
    def _():
        each_x(1, sent_x, True)

        @pl.when(has_next)
        def _():
            z_copy(1).wait_send()

    @pl.when(zz >= 2)
    def _():
        each_x(0, sent_x, True)


def padded(queries, keys_values, route_group, route_slot, doc_lengths):
    bf16 = jnp.bfloat16
    dma = pltpu.SemaphoreType.DMA
    return pl.pallas_call(
        padded_kernel,
        out_shape=jax.ShapeDtypeStruct((1, TOK, HQ * HD), bf16),
        in_specs=[
            pl.BlockSpec(memory_space=pltpu.HBM),
            pl.BlockSpec(memory_space=pltpu.HBM),
            pl.BlockSpec(memory_space=pltpu.HBM),
            pl.BlockSpec(memory_space=pltpu.HBM),
            pl.BlockSpec(memory_space=pltpu.HBM),
        ],
        out_specs=pl.BlockSpec(memory_space=pl.ANY),
        scratch_shapes=[
            pltpu.VMEM((TOK, HQ * HD), bf16),
            pltpu.VMEM((1, TOK, PAIR), bf16),
            pltpu.VMEM((1, TOK), jnp.int32),
            pltpu.VMEM((1, TOK), jnp.int32),
            pltpu.SMEM((1, 2, 3), jnp.int32),
            pltpu.VMEM((HK, GROUPS, CAP, WIDE), bf16),
            pltpu.VMEM((HK, GROUPS, CAP, WIDE), bf16),
            pltpu.VMEM((GROUPS, CAP, PAIR + TOK), bf16),
            pltpu.VMEM((GROUPS, CAP, PAIR + TOK), bf16),
            pltpu.VMEM((3 * NX, TOK, PAIR), bf16),
            pltpu.VMEM((TOK, SPAN), jnp.float32),
            pltpu.VMEM((HQ // HK, TOK, HD), bf16),
            pltpu.VMEM((TOK, HQ * HD), bf16),
            dma((HK + 4,)),
            dma((HK,)),
            dma((HK, GROUPS)),
            dma((HK, GROUPS)),
            dma((GROUPS,)),
            dma((GROUPS,)),
            dma((3,)),
            dma((3,)),
            dma((3, NX)),
            dma((3, NX)),
        ],
        compiler_params=pltpu.CompilerParams(
            collective_id=0, has_side_effects=True, vmem_limit_bytes=48 << 20
        ),
    )(queries, keys_values, route_group, route_slot, doc_lengths)


LOW = 8
OVER = 8
HALF_WIDE = WIDE // 2
PIECE = PAIR // 2
NY = GROUPS // 2
NZ = 2 * HALF_ROWS


def both_halves(one):
    none = jnp.zeros_like(one)
    left = jnp.concatenate([one, none], axis=1)
    right = jnp.concatenate([none, one], axis=1)
    lanes = one.shape[2]
    return jnp.concatenate([left.reshape(-1, lanes), right.reshape(-1, lanes)], axis=1)


def compact_kernel(
    q_hbm,
    kv_hbm,
    group_hbm,
    slot_hbm,
    length_hbm,
    out_ref,
    flag_ref,
    q_in,
    kv_ref,
    group_ref,
    slot_ref,
    length_ref,
    q_send,
    q_recv,
    kva_send,
    kva_recv,
    kvb_send,
    kvb_recv,
    over,
    window,
    mask,
    placed,
    flag_x,
    flag_z,
    in_sem,
    q_ss,
    q_rs,
    kv_ss,
    kv_rs,
    ring_ss,
    ring_rs,
    sib_ss,
    sib_rs,
    z_ss,
    z_rs,
    x_ss,
    x_rs,
    fx_ss,
    fx_rs,
    fz_ss,
    fz_rs,
):
    bf16 = jnp.bfloat16
    f32 = jnp.float32
    me = lax.axis_index("grp")
    seq = lax.axis_index("seq")
    z = seq // NX
    x = seq % NX
    zz = z % HALF_ROWS
    y = me // 2
    core = me % 2
    has_next = zz < HALF_ROWS - 1
    has_last = zz > 0

    small = [
        pltpu.make_async_copy(source, target, in_sem.at[2 * HK + n])
        for n, (source, target) in enumerate(
            [
                (group_hbm, group_ref),
                (slot_hbm, slot_ref),
                (kv_hbm, kv_ref),
                (length_hbm, length_ref),
            ]
        )
    ]
    loads = [
        pltpu.make_async_copy(
            q_hbm.at[0, :, pl.ds(n * HALF_WIDE, HALF_WIDE)], q_in.at[n], in_sem.at[n]
        )
        for n in range(2 * HK)
    ]
    for copy in small + loads:
        copy.start()

    barrier = pltpu.get_barrier_semaphore()

    def greet(group, place):
        pl.semaphore_signal(barrier, inc=1, device_id=(group, place), device_id_type=MESH)

    for d in range(1, GROUPS):
        greet((me + d) % GROUPS, seq)
    for d in range(1, NX):
        greet(me, z * NX + (x + d) % NX)
    for d in range(1, NZ):
        greet(me, (z + d) % NZ * NX + x)

    for copy in small:
        copy.wait()
    targets = group_ref[...]
    lane = lax.broadcasted_iota(jnp.int32, (TOK, TOK), 1)
    sub = lax.broadcasted_iota(jnp.int32, (TOK, TOK), 0)
    hits = lax.broadcasted_iota(jnp.int32, (GROUPS, TOK), 0) == targets
    before = (sub < lane).astype(f32).astype(bf16)
    all_ones = jnp.ones((TOK, TOK), bf16)
    ranks = contract(hits.astype(f32).astype(bf16), before, ((1,), (0,)))
    ranks = jnp.where(hits, ranks, -1.0)
    level = lax.broadcasted_iota(jnp.int32, (GROUPS, CAP, TOK), 1).astype(f32)
    pick_three = (ranks[:, None, :] == level).astype(f32)
    pick_f = pick_three.reshape(SLOTS, TOK)
    pick = pick_f.astype(bf16)
    places = (slot_ref[...] + 1).astype(f32)
    beyond = jnp.sum((ranks >= LOW).astype(f32), axis=0, keepdims=True)
    order = contract(jnp.broadcast_to(beyond, (OVER, TOK)).astype(bf16), before, ((1,), (0,)))
    row = lax.broadcasted_iota(jnp.int32, (OVER, TOK), 0).astype(f32)
    extra = jnp.where((order == row) & (beyond > 0.0), 1.0, 0.0)
    crowded = jnp.sum(beyond, axis=1, keepdims=True) > OVER
    marks = contract((pick_f * places).astype(bf16), all_ones, ((1,), (0,)))
    marks = jnp.where(crowded, -1.0, marks)
    kva_send[:, :, PIECE:] = marks.astype(bf16).reshape(GROUPS, CAP, TOK)

    sends = [kva_send, kvb_send]
    recvs = [kva_recv, kvb_recv]

    def pack_pairs(n):
        for part in range(2):
            cols = kv_ref[0, :, part * PIECE + n * PIECE // 2 : part * PIECE + (n + 1) * PIECE // 2]
            sends[n][:, :, part * PIECE // 2 : (part + 1) * PIECE // 2] = (
                contract(pick, cols, ((1,), (0,))).astype(bf16).reshape(GROUPS, CAP, PIECE // 2)
            )

    def partner(d):
        return (y + d // 2) % NY * 2 + (core + d % 2) % 2

    def far_first(act):
        @pl.loop(0, NY - 1)
        def _(i):
            away = NY // 2 + i // 2 * (1 - i % 2) - (i + 1) // 2 * (i % 2)
            act(2 * away)
            act(2 * away + 1)

        act(1)

    def kv_copy(n, d):
        target = partner(d)
        return remote(
            sends[n].at[target], recvs[n].at[me], kv_ss.at[n, d], kv_rs.at[n, d], (target, seq)
        )

    def start_pairs(n):
        far_first(lambda d: kv_copy(n, d).start())
        recvs[n][me] = sends[n][me]

    pack_pairs(0)

    turn = 1 - 2 * core

    def on_ring(at):
        return (at + 2 * NY) % NY * 2 + core

    def on_sibling(at):
        return (at + 2 * NY) % NY * 2 + 1 - core

    def ring(step, way):
        sign = turn if way == 0 else -turn
        block = on_ring(y - sign * (step - 1))
        return remote(
            over.at[block],
            over.at[block],
            ring_ss.at[way, step],
            ring_rs.at[way, step],
            (on_ring(y + sign), seq),
        )

    def ring_came(step, way):
        sign = turn if way == 0 else -turn
        block = on_ring(y - sign * step)
        remote(
            over.at[block],
            over.at[block],
            ring_ss.at[way, step],
            ring_rs.at[way, step],
            (on_ring(y + sign), seq),
        ).wait_recv()

    def sibling(n):
        block = on_ring(y - turn * n if n <= NY // 2 else y + turn * (n - NY // 2))
        return remote(
            over.at[block], over.at[block], sib_ss.at[n], sib_rs.at[n], (on_sibling(y), seq)
        )

    def sibling_came(n):
        block = on_sibling(y + turn * n if n <= NY // 2 else y - turn * (n - NY // 2))
        remote(
            over.at[block], over.at[block], sib_ss.at[n], sib_rs.at[n], (on_sibling(y), seq)
        ).wait_recv()

    def ring_turn(step):
        ring_came(step, 0)
        if step < NY // 2:
            ring(step + 1, 0).start()
            ring_came(step, 1)
            if step + 1 < NY // 2:
                ring(step + 1, 1).start()
            sibling(NY // 2 + step).start()
        sibling(step).start()

    pl.semaphore_wait(barrier, GROUPS - 1 + NX - 1 + NZ - 1)
    start_pairs(0)

    high = both_halves(extra[None]).astype(bf16)
    for j in range(HK):
        loads[2 * j].wait()
        loads[2 * j + 1].wait()
        halves = q_in[2 * j : 2 * j + 2].reshape(2 * TOK, HALF_WIDE)
        over[me, :, j * HALF_WIDE : (j + 1) * HALF_WIDE] = contract(
            high, halves, ((1,), (0,))
        ).astype(bf16)
    tags = jnp.concatenate([extra * places, extra * (targets + 1).astype(f32)], axis=0)
    over[me, :, HK * HALF_WIDE :] = contract(tags.astype(bf16), all_ones, ((1,), (0,))).astype(bf16)
    ring(1, 0).start()
    ring(1, 1).start()
    pack_pairs(1)
    start_pairs(1)
    sibling(0).start()

    low = both_halves(pick_three[:, :LOW]).astype(bf16)
    for j in range(HK):
        halves = q_in[2 * j : 2 * j + 2].reshape(2 * TOK, HALF_WIDE)
        q_send[j] = (
            contract(low, halves, ((1,), (0,))).astype(bf16).reshape(GROUPS, CAP, HALF_WIDE)
        )

    def q_copy(j, d, part=None):
        target = partner(d)
        source, goal, sem = q_send.at[j, target], q_recv.at[j, me], j
        if part is not None:
            cols = pl.ds(part * (HALF_WIDE // 2), HALF_WIDE // 2)
            source, goal, sem = source.at[:, cols], goal.at[:, cols], j + part
        return remote(source, goal, q_ss.at[sem, d], q_rs.at[sem, d], (target, seq))

    def start_queries(j):
        if j < HK - 1:
            far_first(lambda d: q_copy(j, d).start())
        else:
            for part in range(2):
                far_first(lambda d, part=part: q_copy(j, d, part).start())
        q_recv[j, me] = q_send[j, me]

    query = seq * TOK + lax.broadcasted_iota(jnp.int32, (TOK, SPAN), 0)
    key = (seq - BACK) * TOK + lax.broadcasted_iota(jnp.int32, (TOK, SPAN), 1)
    begin = jnp.zeros((TOK, SPAN), jnp.int32)
    bound = jnp.int32(0)
    for half in range(2):
        for n in range(3):
            bound = bound + length_ref[0, half, n]
            begin = jnp.where(query >= bound, bound, begin)
    mask[...] = jnp.where((key >= begin) & (key <= query), 0.0, NEGATIVE)

    @pl.when(zz == 0)
    def _():
        window[:, pl.ds(0, 2 * NX)] = jnp.zeros((2, 2 * NX, TOK, PIECE), bf16)

    @pl.when(zz == 1)
    def _():
        window[:, pl.ds(0, NX)] = jnp.zeros((2, NX, TOK, PIECE), bf16)

    def z_copy(n, plane):
        return remote(
            window.at[n, plane * NX + x],
            window.at[n, (plane - 1) * NX + x],
            z_ss.at[n, plane],
            z_rs.at[n, plane],
            (me, (seq + NX) % (NX * NZ)),
        )

    def x_copy(n, plane, d, came=False):
        at = plane * NX + ((x + NX - d) % NX if came else x)
        return remote(
            window.at[n, at],
            window.at[n, at],
            x_ss.at[n, plane, d],
            x_rs.at[n, plane, d],
            (me, z * NX + (x + d) % NX),
        )

    def start_x(n, plane, d):
        x_copy(n, plane, d).start()

    def sent_x(n, plane, d):
        x_copy(n, plane, d).wait_send()

    def came_x(n, plane, d):
        x_copy(n, plane, d, True).wait_recv()

    def each_x(n, plane, act, steps):
        for d in steps:
            wraps = x - d < 0 if act is came_x else x + d >= NX
            if plane == 1:
                act(n, plane, d)
            else:
                pl.when(wraps if plane == 0 else jnp.logical_not(wraps))(
                    functools.partial(act, n, plane, d)
                )

    beside = (1, NX - 1)
    inner = (x == 1) | (x == 2)

    def pass_on(n, plane, way, slot):
        at = plane * NX + (x + NX - way) % NX
        return remote(
            window.at[n, at],
            window.at[n, at],
            x_ss.at[n, plane, slot],
            x_rs.at[n, plane, 2],
            (me, z * NX + (x + NX + way) % NX),
        )

    def each_pass(n, plane, act):
        if plane == 1:

            @pl.when(jnp.logical_not(inner))
            def _():
                act(pass_on(n, plane, 1, 0))
                act(pass_on(n, plane, -1, 2))

        else:

            @pl.when(inner)
            def _():
                act(pass_on(n, plane, 1 if plane == 2 else -1, 2))

    def forward(n, plane):
        def go():
            each_x(n, plane, came_x, beside)
            each_pass(n, plane, lambda copy: copy.start())

        if plane == 2:
            go()
        else:
            pl.when(has_last if plane == 1 else zz >= 2)(go)

    def place_pairs(n):
        window[n, 2 * NX + x] = contract(
            put, recvs[n][:, :, :PIECE].reshape(SLOTS, PIECE), ((1,), (0,))
        ).astype(bf16)

        @pl.when(has_next)
        def _():
            z_copy(n, 2).start()

        each_x(n, 2, start_x, beside)

    def one_back(n):
        @pl.when(has_last)
        def _():
            z_copy(n, 2).wait_recv()

            @pl.when(has_next)
            def _():
                z_copy(n, 1).start()

            each_x(n, 1, start_x, beside)

    def two_back(n):
        @pl.when(zz >= 2)
        def _():
            z_copy(n, 1).wait_recv()
            each_x(n, 0, start_x, beside)

    def flag_x_copy(d, came=False):
        at = (x + NX - d) % NX if came else x
        return remote(
            flag_x.at[at],
            flag_x.at[at],
            fx_ss.at[d],
            fx_rs.at[d],
            (me, z * NX + (x + d) % NX),
        )

    def flag_z_copy(d, came=False):
        at = (z + NZ - d) % NZ if came else z
        return remote(
            flag_z.at[at],
            flag_z.at[at],
            fz_ss.at[d],
            fz_rs.at[d],
            (me, (z + d) % NZ * NX + x),
        )

    def pairs_came(n):
        @pl.loop(1, GROUPS)
        def _(d):
            kv_copy(n, d).wait_recv()

    pairs_came(0)
    marks_in = kva_recv[:, :, PIECE:].astype(f32)
    column = lax.broadcasted_iota(jnp.int32, (GROUPS, CAP, TOK), 2).astype(f32) + 1.0
    match = (marks_in == column).astype(f32)
    put = match.reshape(SLOTS, TOK).T.astype(bf16)
    place_pairs(0)
    worst = jnp.max((marks_in < 0.0).astype(f32).reshape(SLOTS, TOK), axis=0, keepdims=True)
    flag_x[x] = jnp.broadcast_to(worst, (CAP, TOK)).astype(bf16)
    for d in range(1, NX):
        flag_x_copy(d).start()
    put_low = both_halves(match[:, :LOW]).T.astype(bf16)

    ring_turn(1)
    start_queries(0)
    forward(0, 2)
    one_back(0)
    pairs_came(1)
    place_pairs(1)
    ring_turn(2)
    start_queries(1)
    for d in range(1, NX):
        flag_x_copy(d, True).wait_recv()
    flag_z[z] = jnp.max(flag_x[...].astype(f32), axis=0).astype(bf16)
    for d in range(1, NZ):
        flag_z_copy(d).start()
    two_back(0)
    forward(0, 1)
    one_back(1)
    forward(1, 2)
    ring_turn(3)
    start_queries(2)
    start_queries(3)
    two_back(1)
    forward(0, 0)
    ring_turn(4)
    for n in range(NY):
        sibling_came(n)

    tags_in = over[:, :, HK * HALF_WIDE :].astype(f32)
    mine = (me + 1).astype(f32)
    match_over = ((tags_in[:, :OVER] == column[:, :OVER]) & (tags_in[:, OVER:] == mine)).astype(f32)
    put_over = both_halves(match_over).T.astype(bf16)

    ones = jnp.ones((SPAN, HD), bf16)

    def window_came(n):
        each_x(n, 2, came_x, (2,))

        @pl.when(has_last)
        def _():
            each_x(n, 1, came_x, (2,))

        @pl.when(zz >= 2)
        def _():
            each_x(n, 0, came_x, (2,))

    def place_queries(j, cols, over_cols):
        rows = contract(put_low, q_recv[j, :, :, cols].reshape(SLOTS, -1), ((1,), (0,)))
        rows = rows + contract(put_over, over[:, :, over_cols].reshape(SLOTS, -1), ((1,), (0,)))
        rows = rows.astype(bf16)
        count = rows.shape[1] // HD
        for n in range(2 * count):
            half, at = n // count, n % count
            placed[n] = rows[half * TOK : (half + 1) * TOK, at * HD : (at + 1) * HD]

    def attend(j, heads):
        key_cols = pl.ds(pl.multiple_of(j % 2 * HD, HD), HD)
        value_cols = pl.ds(pl.multiple_of(PIECE // 2 + j % 2 * HD, HD), HD)
        for n, h in enumerate(heads):
            keys = window[j // 2, pl.ds(x, BACK + 1), :, key_cols].reshape(SPAN, HD)
            values = window[j // 2, pl.ds(x, BACK + 1), :, value_cols].reshape(SPAN, HD)
            scores = contract(placed[n], keys, ((1,), (1,))) + mask[...]
            top = jnp.max(scores, axis=1, keepdims=True)
            weights = jnp.exp2((scores - top) * FACTOR).astype(bf16)
            summed = contract(weights, jnp.concatenate([values, ones], axis=1), ((1,), (0,)))
            head_cols = pl.ds(pl.multiple_of((j * (HQ // HK) + h) * HD, HD), HD)
            out_ref[0, :, head_cols] = (summed[:, :HD] / summed[:, HD:]).astype(bf16)

    @pl.loop(0, HK - 1)
    def _(j):
        @pl.when(j == 0)
        def _():
            window_came(0)

        @pl.when(j == 1)
        def _():
            forward(1, 1)
            forward(1, 0)

        @pl.when(j == 2)
        def _():
            window_came(1)

        @pl.loop(1, GROUPS)
        def _(d):
            q_copy(j, d).wait_recv()

        cols = pl.ds(pl.multiple_of(j * HALF_WIDE, HALF_WIDE), HALF_WIDE)
        place_queries(j, slice(None), cols)
        attend(j, range(HQ // HK))

    @pl.loop(1, GROUPS)
    def _(d):
        for n in range(2):
            kv_copy(n, d).wait_send()
        for j in range(HK - 1):
            q_copy(j, d).wait_send()

    for n in range(2):
        each_x(n, 2, sent_x, beside)
        each_pass(n, 2, lambda copy: copy.wait_send())

        @pl.when(has_next)
        def _(n=n):
            z_copy(n, 2).wait_send()

        @pl.when(has_last)
        def _(n=n):
            each_x(n, 1, sent_x, beside)
            each_pass(n, 1, lambda copy: copy.wait_send())

            @pl.when(has_next)
            def _():
                z_copy(n, 1).wait_send()

        @pl.when(zz >= 2)
        def _(n=n):
            each_x(n, 0, sent_x, beside)
            each_pass(n, 0, lambda copy: copy.wait_send())

    for step in range(1, NY // 2 + 1):
        ring(step, 0).wait_send()
        if step < NY // 2:
            ring(step, 1).wait_send()
    for n in range(NY):
        sibling(n).wait_send()
    for d in range(1, NX):
        flag_x_copy(d).wait_send()
    for d in range(1, NZ):
        flag_z_copy(d).wait_send()

    for d in range(1, NZ):
        flag_z_copy(d, True).wait_recv()
    flag_ref[0, 0] = jnp.max(flag_z[...].astype(f32)).astype(jnp.int32)

    last = HK - 1
    quarter = HQ // HK // 4
    for part in range(2):

        @pl.loop(1, GROUPS)
        def _(d, part=part):
            q_copy(last, d, part).wait()

        at = part * HALF_WIDE // 2
        start = last * HALF_WIDE + at
        place_queries(last, slice(at, at + HALF_WIDE // 2), slice(start, start + HALF_WIDE // 2))
        attend(last, [2 * quarter * half + part * quarter + n for half in range(2) for n in range(quarter)])


def compact(*operands):
    bf16 = jnp.bfloat16
    dma = pltpu.SemaphoreType.DMA
    vmem = pltpu.VMEM
    return pl.pallas_call(
        compact_kernel,
        out_shape=(
            pltpu.VMEM((1, TOK, HQ * HD), bf16),
            jax.ShapeDtypeStruct((1, 1), jnp.int32),
        ),
        in_specs=[pl.BlockSpec(memory_space=pltpu.HBM)] * 5,
        out_specs=(pl.BlockSpec(memory_space=pltpu.VMEM), pl.BlockSpec(memory_space=pltpu.SMEM)),
        scratch_shapes=[
            vmem((2 * HK, TOK, HALF_WIDE), bf16),
            vmem((1, TOK, PAIR), bf16),
            vmem((1, TOK), jnp.int32),
            vmem((1, TOK), jnp.int32),
            pltpu.SMEM((1, 2, 3), jnp.int32),
            vmem((HK, GROUPS, CAP, HALF_WIDE), bf16),
            vmem((HK, GROUPS, CAP, HALF_WIDE), bf16),
            vmem((GROUPS, CAP, PIECE + TOK), bf16),
            vmem((GROUPS, CAP, PIECE + TOK), bf16),
            vmem((GROUPS, CAP, PIECE), bf16),
            vmem((GROUPS, CAP, PIECE), bf16),
            vmem((GROUPS, CAP, HK * HALF_WIDE + TOK), bf16),
            vmem((2, 3 * NX, TOK, PIECE), bf16),
            vmem((TOK, SPAN), jnp.float32),
            vmem((HQ // HK, TOK, HD), bf16),
            vmem((NX, CAP, TOK), bf16),
            vmem((NZ, CAP, TOK), bf16),
            dma((2 * HK + 4,)),
            dma((HK + 1, GROUPS)),
            dma((HK + 1, GROUPS)),
            dma((2, GROUPS)),
            dma((2, GROUPS)),
            dma((2, NY // 2 + 1)),
            dma((2, NY // 2 + 1)),
            dma((NY,)),
            dma((NY,)),
            dma((2, 3)),
            dma((2, 3)),
            dma((2, 3, NX)),
            dma((2, 3, NX)),
            dma((NX,)),
            dma((NX,)),
            dma((NZ,)),
            dma((NZ,)),
        ],
        compiler_params=pltpu.CompilerParams(
            collective_id=1, has_side_effects=True, vmem_limit_bytes=48 << 20
        ),
    )(*operands)


def local(*operands):
    operands = [pltpu.with_memory_space_constraint(one, pltpu.HBM) for one in operands]
    result, crowded = compact(*operands)
    return lax.switch(crowded[0, 0], [lambda: result, lambda: padded(*operands)])


def solution(mesh):
    return jax.shard_map(
        local,
        mesh=mesh,
        in_specs=(
            P("grp", "seq", None),
            P("grp", "seq", None),
            P("grp", "seq"),
            P("grp", "seq"),
            P("grp", None, None),
        ),
        out_specs=P("grp", "seq", None),
        check_vma=False,
    )
```

```python
import functools
import math

import jax
import jax.numpy as jnp
from jax import lax
from jax.experimental import pallas as pl
from jax.experimental.pallas import tpu as pltpu
from jax.sharding import PartitionSpec as P

HQ = 32
HK = 4
HD = 128
TOK = 128
GROUPS = 16
CAP = 16
SLOTS = GROUPS * CAP
WIDE = HQ // HK * HD
PAIR = 2 * HK * HD
BACK = 8
SPAN = (BACK + 1) * TOK
NX = 4
HALF_ROWS = 4
NEGATIVE = -1e30
MESH = pl.DeviceIdType.MESH
FACTOR = HD ** (-0.5) * math.log2(math.e)


def remote(src, dst, send, recv, device):
    return pltpu.make_async_remote_copy(
        src_ref=src,
        dst_ref=dst,
        send_sem=send,
        recv_sem=recv,
        device_id=device,
        device_id_type=MESH,
    )


def contract(a, b, dims):
    return lax.dot_general(a, b, (dims, ((), ())), preferred_element_type=jnp.float32)


def padded_kernel(
    q_hbm,
    kv_hbm,
    group_hbm,
    slot_hbm,
    length_hbm,
    out_hbm,
    q_in,
    kv_ref,
    group_ref,
    slot_ref,
    length_ref,
    q_send,
    q_recv,
    kv_send,
    kv_recv,
    window,
    mask,
    placed,
    out_buf,
    in_sem,
    out_sem,
    q_ss,
    q_rs,
    kv_ss,
    kv_rs,
    z_ss,
    z_rs,
    x_ss,
    x_rs,
):
    me = lax.axis_index("grp")
    seq = lax.axis_index("seq")
    z = seq // NX
    x = seq % NX
    zz = z % HALF_ROWS
    has_next = zz < HALF_ROWS - 1
    has_last = zz > 0

    def load(j):
        cols = pl.ds(j * WIDE, WIDE)
        return pltpu.make_async_copy(q_hbm.at[0, :, cols], q_in.at[:, cols], in_sem.at[j])

    small = [
        pltpu.make_async_copy(source, target, in_sem.at[HK + n])
        for n, (source, target) in enumerate(
            [
                (group_hbm, group_ref),
                (slot_hbm, slot_ref),
                (kv_hbm, kv_ref),
                (length_hbm, length_ref),
            ]
        )
    ]
    for copy in small:
        copy.start()
    for j in range(HK):
        load(j).start()

    barrier = pltpu.get_barrier_semaphore()

    def greet(group, place):
        pl.semaphore_signal(barrier, inc=1, device_id=(group, place), device_id_type=MESH)

    for d in range(1, GROUPS):
        greet((me + d) % GROUPS, seq)
    for d in range(1, NX):
        greet(me, z * NX + (x + d) % NX)

    @pl.when(has_next)
    def _():
        greet(me, seq + NX)

    @pl.when(has_last)
    def _():
        greet(me, seq - NX)

    for copy in small:
        copy.wait()
    targets = group_ref[...]
    lane = lax.broadcasted_iota(jnp.int32, (TOK, TOK), 1)
    sub = lax.broadcasted_iota(jnp.int32, (TOK, TOK), 0)
    hits = lax.broadcasted_iota(jnp.int32, (GROUPS, TOK), 0) == targets
    before = (sub < lane).astype(jnp.float32).astype(jnp.bfloat16)
    hits_f = hits.astype(jnp.float32)
    ranks = contract(hits_f.astype(jnp.bfloat16), before, ((1,), (0,)))
    ranks = jnp.where(hits, ranks, -1.0)
    level = lax.broadcasted_iota(jnp.int32, (GROUPS, CAP, TOK), 1).astype(jnp.float32)
    pick_f = (ranks[:, None, :] == level).astype(jnp.float32).reshape(SLOTS, TOK)
    pick = pick_f.astype(jnp.bfloat16)
    marks = (pick_f * (slot_ref[...] + 1).astype(jnp.float32)).astype(jnp.bfloat16)
    slots = contract(marks, jnp.ones((TOK, TOK), jnp.bfloat16), ((1,), (0,)))
    kv_send[:, :, PAIR:] = slots.astype(jnp.bfloat16).reshape(GROUPS, CAP, TOK)
    kv_send[:, :, :PAIR] = (
        contract(pick, kv_ref[0], ((1,), (0,))).astype(jnp.bfloat16).reshape(GROUPS, CAP, PAIR)
    )

    pl.semaphore_wait(
        barrier, GROUPS - 1 + NX - 1 + has_next.astype(jnp.int32) + has_last.astype(jnp.int32)
    )

    def kv_copy(d):
        target = (me + d) % GROUPS
        return remote(
            kv_send.at[target], kv_recv.at[me], kv_ss.at[d], kv_rs.at[d], (target, seq)
        )

    @pl.loop(1, GROUPS)
    def _(d):
        kv_copy(d).start()

    kv_recv[me] = kv_send[me]

    def q_copy(j, d):
        target = (me + d) % GROUPS
        return remote(
            q_send.at[j, target], q_recv.at[j, me], q_ss.at[j, d], q_rs.at[j, d], (target, seq)
        )

    for j in range(HK):
        load(j).wait()
        q_send[j] = (
            contract(pick, q_in[:, j * WIDE : (j + 1) * WIDE], ((1,), (0,)))
            .astype(jnp.bfloat16)
            .reshape(GROUPS, CAP, WIDE)
        )

        @pl.loop(1, GROUPS)
        def _(d, j=j):
            q_copy(j, d).start()

        q_recv[j, me] = q_send[j, me]

    query = seq * TOK + lax.broadcasted_iota(jnp.int32, (TOK, SPAN), 0)
    key = (seq - BACK) * TOK + lax.broadcasted_iota(jnp.int32, (TOK, SPAN), 1)
    begin = jnp.zeros((TOK, SPAN), jnp.int32)
    bound = jnp.int32(0)
    for half in range(2):
        for n in range(3):
            bound = bound + length_ref[0, half, n]
            begin = jnp.where(query >= bound, bound, begin)
    mask[...] = jnp.where((key >= begin) & (key <= query), 0.0, NEGATIVE)

    @pl.when(zz == 0)
    def _():
        window[pl.ds(0, 2 * NX)] = jnp.zeros((2 * NX, TOK, PAIR), jnp.bfloat16)

    @pl.when(zz == 1)
    def _():
        window[pl.ds(0, NX)] = jnp.zeros((NX, TOK, PAIR), jnp.bfloat16)

    @pl.loop(1, GROUPS)
    def _(d):
        kv_copy(d).wait_recv()

    marks_in = kv_recv[:, :, PAIR:].reshape(SLOTS, TOK).astype(jnp.float32)
    column = lax.broadcasted_iota(jnp.int32, (SLOTS, TOK), 1).astype(jnp.float32) + 1.0
    put = (marks_in == column).astype(jnp.float32).T.astype(jnp.bfloat16)
    window[2 * NX + x] = contract(
        put, kv_recv[:, :, :PAIR].reshape(SLOTS, PAIR), ((1,), (0,))
    ).astype(jnp.bfloat16)

    def z_copy(plane):
        return remote(
            window.at[plane * NX + x],
            window.at[(plane - 1) * NX + x],
            z_ss.at[plane],
            z_rs.at[plane],
            (me, (seq + NX) % (NX * 8)),
        )

    def x_copy(plane, d):
        return remote(
            window.at[plane * NX + x],
            window.at[plane * NX + x],
            x_ss.at[plane, d],
            x_rs.at[plane, d],
            (me, z * NX + (x + d) % NX),
        )

    def x_wait(plane, d):
        source = (x + NX - d) % NX
        return remote(
            window.at[plane * NX + source],
            window.at[plane * NX + source],
            x_ss.at[plane, d],
            x_rs.at[plane, d],
            (me, z * NX + (x + d) % NX),
        )

    def each_x(plane, act, sending):
        for d in range(1, NX):
            wraps = x + d >= NX if sending else x - d < 0
            if plane == 1:
                act(plane, d)
            else:
                pl.when(wraps if plane == 0 else jnp.logical_not(wraps))(
                    functools.partial(act, plane, d)
                )

    def start_x(plane, d):
        x_copy(plane, d).start()

    def sent_x(plane, d):
        x_copy(plane, d).wait_send()

    def came_x(plane, d):
        x_wait(plane, d).wait_recv()

    @pl.when(has_next)
    def _():
        z_copy(2).start()

    each_x(2, start_x, True)

    @pl.when(has_last)
    def _():
        z_copy(2).wait_recv()

        @pl.when(has_next)
        def _():
            z_copy(1).start()

        each_x(1, start_x, True)

    @pl.when(zz >= 2)
    def _():
        z_copy(1).wait_recv()
        each_x(0, start_x, True)

    each_x(2, came_x, False)

    @pl.when(has_last)
    def _():
        each_x(1, came_x, False)

    @pl.when(zz >= 2)
    def _():
        each_x(0, came_x, False)

    def store(j):
        cols = pl.ds(pl.multiple_of(j * WIDE, WIDE), WIDE)
        return pltpu.make_async_copy(out_buf.at[:, cols], out_hbm.at[0, :, cols], out_sem.at[j])

    ones = jnp.ones((SPAN, HD), jnp.bfloat16)

    @pl.loop(0, HK)
    def _(j):
        @pl.loop(1, GROUPS)
        def _(d):
            q_copy(j, d).wait_recv()

        rows = contract(put, q_recv[j].reshape(SLOTS, WIDE), ((1,), (0,))).astype(jnp.bfloat16)
        for h in range(HQ // HK):
            placed[h] = rows[:, h * HD : (h + 1) * HD]
        key_cols = pl.ds(pl.multiple_of(j * HD, HD), HD)
        value_cols = pl.ds(pl.multiple_of((HK + j) * HD, HD), HD)

        for h in range(HQ // HK):
            keys = window[pl.ds(x, BACK + 1), :, key_cols].reshape(SPAN, HD)
            values = window[pl.ds(x, BACK + 1), :, value_cols].reshape(SPAN, HD)
            scores = contract(placed[h], keys, ((1,), (1,))) + mask[...]
            top = jnp.max(scores, axis=1, keepdims=True)
            weights = jnp.exp2((scores - top) * FACTOR).astype(jnp.bfloat16)
            summed = contract(weights, jnp.concatenate([values, ones], axis=1), ((1,), (0,)))
            cols = pl.ds(pl.multiple_of((j * (HQ // HK) + h) * HD, HD), HD)
            out_buf[:, cols] = (summed[:, :HD] / summed[:, HD:]).astype(jnp.bfloat16)

        store(j).start()

    for j in range(HK):
        store(j).wait()

    @pl.loop(1, GROUPS)
    def _(d):
        kv_copy(d).wait_send()
        for j in range(HK):
            q_copy(j, d).wait_send()

    each_x(2, sent_x, True)

    @pl.when(has_next)
    def _():
        z_copy(2).wait_send()

    @pl.when(has_last)
    def _():
        each_x(1, sent_x, True)

        @pl.when(has_next)
        def _():
            z_copy(1).wait_send()

    @pl.when(zz >= 2)
    def _():
        each_x(0, sent_x, True)


def padded(queries, keys_values, route_group, route_slot, doc_lengths):
    bf16 = jnp.bfloat16
    dma = pltpu.SemaphoreType.DMA
    return pl.pallas_call(
        padded_kernel,
        out_shape=jax.ShapeDtypeStruct((1, TOK, HQ * HD), bf16),
        in_specs=[
            pl.BlockSpec(memory_space=pltpu.HBM),
            pl.BlockSpec(memory_space=pltpu.HBM),
            pl.BlockSpec(memory_space=pltpu.HBM),
            pl.BlockSpec(memory_space=pltpu.HBM),
            pl.BlockSpec(memory_space=pltpu.HBM),
        ],
        out_specs=pl.BlockSpec(memory_space=pl.ANY),
        scratch_shapes=[
            pltpu.VMEM((TOK, HQ * HD), bf16),
            pltpu.VMEM((1, TOK, PAIR), bf16),
            pltpu.VMEM((1, TOK), jnp.int32),
            pltpu.VMEM((1, TOK), jnp.int32),
            pltpu.SMEM((1, 2, 3), jnp.int32),
            pltpu.VMEM((HK, GROUPS, CAP, WIDE), bf16),
            pltpu.VMEM((HK, GROUPS, CAP, WIDE), bf16),
            pltpu.VMEM((GROUPS, CAP, PAIR + TOK), bf16),
            pltpu.VMEM((GROUPS, CAP, PAIR + TOK), bf16),
            pltpu.VMEM((3 * NX, TOK, PAIR), bf16),
            pltpu.VMEM((TOK, SPAN), jnp.float32),
            pltpu.VMEM((HQ // HK, TOK, HD), bf16),
            pltpu.VMEM((TOK, HQ * HD), bf16),
            dma((HK + 4,)),
            dma((HK,)),
            dma((HK, GROUPS)),
            dma((HK, GROUPS)),
            dma((GROUPS,)),
            dma((GROUPS,)),
            dma((3,)),
            dma((3,)),
            dma((3, NX)),
            dma((3, NX)),
        ],
        compiler_params=pltpu.CompilerParams(
            collective_id=0, has_side_effects=True, vmem_limit_bytes=48 << 20
        ),
    )(queries, keys_values, route_group, route_slot, doc_lengths)


LOW = 8
OVER = 8
HALF_WIDE = WIDE // 2
PIECE = PAIR // 2
NY = GROUPS // 2
NZ = 2 * HALF_ROWS


def both_halves(one):
    none = jnp.zeros_like(one)
    left = jnp.concatenate([one, none], axis=1)
    right = jnp.concatenate([none, one], axis=1)
    lanes = one.shape[2]
    return jnp.concatenate([left.reshape(-1, lanes), right.reshape(-1, lanes)], axis=1)


def compact_kernel(
    q_hbm,
    kv_hbm,
    group_hbm,
    slot_hbm,
    length_hbm,
    out_ref,
    flag_ref,
    q_in,
    kv_ref,
    group_ref,
    slot_ref,
    length_ref,
    q_send,
    q_recv,
    kva_send,
    kva_recv,
    kvb_send,
    kvb_recv,
    over,
    window,
    mask,
    placed,
    flag_x,
    flag_z,
    in_sem,
    q_ss,
    q_rs,
    kv_ss,
    kv_rs,
    ring_ss,
    ring_rs,
    sib_ss,
    sib_rs,
    z_ss,
    z_rs,
    x_ss,
    x_rs,
    fx_ss,
    fx_rs,
    fz_ss,
    fz_rs,
):
    bf16 = jnp.bfloat16
    f32 = jnp.float32
    me = lax.axis_index("grp")
    seq = lax.axis_index("seq")
    z = seq // NX
    x = seq % NX
    zz = z % HALF_ROWS
    y = me // 2
    core = me % 2
    has_next = zz < HALF_ROWS - 1
    has_last = zz > 0

    small = [
        pltpu.make_async_copy(source, target, in_sem.at[2 * HK + n])
        for n, (source, target) in enumerate(
            [
                (group_hbm, group_ref),
                (slot_hbm, slot_ref),
                (kv_hbm, kv_ref),
                (length_hbm, length_ref),
            ]
        )
    ]
    loads = [
        pltpu.make_async_copy(
            q_hbm.at[0, :, pl.ds(n * HALF_WIDE, HALF_WIDE)], q_in.at[n], in_sem.at[n]
        )
        for n in range(2 * HK)
    ]
    for copy in small + loads:
        copy.start()

    barrier = pltpu.get_barrier_semaphore()

    def greet(group, place):
        pl.semaphore_signal(barrier, inc=1, device_id=(group, place), device_id_type=MESH)

    for d in range(1, GROUPS):
        greet((me + d) % GROUPS, seq)
    for d in range(1, NX):
        greet(me, z * NX + (x + d) % NX)
    for d in range(1, NZ):
        greet(me, (z + d) % NZ * NX + x)

    for copy in small:
        copy.wait()
    targets = group_ref[...]
    lane = lax.broadcasted_iota(jnp.int32, (TOK, TOK), 1)
    sub = lax.broadcasted_iota(jnp.int32, (TOK, TOK), 0)
    hits = lax.broadcasted_iota(jnp.int32, (GROUPS, TOK), 0) == targets
    before = (sub < lane).astype(f32).astype(bf16)
    all_ones = jnp.ones((TOK, TOK), bf16)
    ranks = contract(hits.astype(f32).astype(bf16), before, ((1,), (0,)))
    ranks = jnp.where(hits, ranks, -1.0)
    level = lax.broadcasted_iota(jnp.int32, (GROUPS, CAP, TOK), 1).astype(f32)
    pick_three = (ranks[:, None, :] == level).astype(f32)
    pick_f = pick_three.reshape(SLOTS, TOK)
    pick = pick_f.astype(bf16)
    places = (slot_ref[...] + 1).astype(f32)
    beyond = jnp.sum((ranks >= LOW).astype(f32), axis=0, keepdims=True)
    order = contract(jnp.broadcast_to(beyond, (OVER, TOK)).astype(bf16), before, ((1,), (0,)))
    row = lax.broadcasted_iota(jnp.int32, (OVER, TOK), 0).astype(f32)
    extra = jnp.where((order == row) & (beyond > 0.0), 1.0, 0.0)
    crowded = jnp.sum(beyond, axis=1, keepdims=True) > OVER
    marks = contract((pick_f * places).astype(bf16), all_ones, ((1,), (0,)))
    marks = jnp.where(crowded, -1.0, marks)
    kva_send[:, :, PIECE:] = marks.astype(bf16).reshape(GROUPS, CAP, TOK)

    sends = [kva_send, kvb_send]
    recvs = [kva_recv, kvb_recv]

    def pack_pairs(n):
        for part in range(2):
            cols = kv_ref[0, :, part * PIECE + n * PIECE // 2 : part * PIECE + (n + 1) * PIECE // 2]
            sends[n][:, :, part * PIECE // 2 : (part + 1) * PIECE // 2] = (
                contract(pick, cols, ((1,), (0,))).astype(bf16).reshape(GROUPS, CAP, PIECE // 2)
            )

    def partner(d):
        return (y + d // 2) % NY * 2 + (core + d % 2) % 2

    def far_first(act):
        @pl.loop(0, NY - 1)
        def _(i):
            away = NY // 2 + i // 2 * (1 - i % 2) - (i + 1) // 2 * (i % 2)
            act(2 * away)
            act(2 * away + 1)

        act(1)

    def kv_copy(n, d):
        target = partner(d)
        return remote(
            sends[n].at[target], recvs[n].at[me], kv_ss.at[n, d], kv_rs.at[n, d], (target, seq)
        )

    def start_pairs(n):
        far_first(lambda d: kv_copy(n, d).start())
        recvs[n][me] = sends[n][me]

    pack_pairs(0)

    high = both_halves(extra[None]).astype(bf16)
    for j in range(HK):
        loads[2 * j].wait()
        loads[2 * j + 1].wait()
        halves = q_in[2 * j : 2 * j + 2].reshape(2 * TOK, HALF_WIDE)
        over[me, :, j * HALF_WIDE : (j + 1) * HALF_WIDE] = contract(
            high, halves, ((1,), (0,))
        ).astype(bf16)
    tags = jnp.concatenate([extra * places, extra * (targets + 1).astype(f32)], axis=0)
    over[me, :, HK * HALF_WIDE :] = contract(tags.astype(bf16), all_ones, ((1,), (0,))).astype(bf16)
    turn = 1 - 2 * core

    def on_ring(at):
        return (at + 2 * NY) % NY * 2 + core

    def on_sibling(at):
        return (at + 2 * NY) % NY * 2 + 1 - core

    def ring(step, way):
        sign = turn if way == 0 else -turn
        block = on_ring(y - sign * (step - 1))
        return remote(
            over.at[block],
            over.at[block],
            ring_ss.at[way, step],
            ring_rs.at[way, step],
            (on_ring(y + sign), seq),
        )

    def ring_came(step, way):
        sign = turn if way == 0 else -turn
        block = on_ring(y - sign * step)
        remote(
            over.at[block],
            over.at[block],
            ring_ss.at[way, step],
            ring_rs.at[way, step],
            (on_ring(y + sign), seq),
        ).wait_recv()

    def sibling(n):
        block = on_ring(y - turn * n if n <= NY // 2 else y + turn * (n - NY // 2))
        return remote(
            over.at[block], over.at[block], sib_ss.at[n], sib_rs.at[n], (on_sibling(y), seq)
        )

    def sibling_came(n):
        block = on_sibling(y + turn * n if n <= NY // 2 else y - turn * (n - NY // 2))
        remote(
            over.at[block], over.at[block], sib_ss.at[n], sib_rs.at[n], (on_sibling(y), seq)
        ).wait_recv()

    def ring_turn(step):
        ring_came(step, 0)
        if step < NY // 2:
            ring(step + 1, 0).start()
            ring_came(step, 1)
            if step + 1 < NY // 2:
                ring(step + 1, 1).start()
            sibling(NY // 2 + step).start()
        sibling(step).start()

    pl.semaphore_wait(barrier, GROUPS - 1 + NX - 1 + NZ - 1)
    ring(1, 0).start()
    ring(1, 1).start()
    start_pairs(0)
    sibling(0).start()
    pack_pairs(1)

    ring_turn(1)
    start_pairs(1)

    low = both_halves(pick_three[:, :LOW]).astype(bf16)
    for j in range(HK):
        halves = q_in[2 * j : 2 * j + 2].reshape(2 * TOK, HALF_WIDE)
        q_send[j] = (
            contract(low, halves, ((1,), (0,))).astype(bf16).reshape(GROUPS, CAP, HALF_WIDE)
        )

    def q_copy(j, d):
        target = partner(d)
        return remote(
            q_send.at[j, target], q_recv.at[j, me], q_ss.at[j, d], q_rs.at[j, d], (target, seq)
        )

    def start_queries(j):
        far_first(lambda d: q_copy(j, d).start())
        q_recv[j, me] = q_send[j, me]

    query = seq * TOK + lax.broadcasted_iota(jnp.int32, (TOK, SPAN), 0)
    key = (seq - BACK) * TOK + lax.broadcasted_iota(jnp.int32, (TOK, SPAN), 1)
    begin = jnp.zeros((TOK, SPAN), jnp.int32)
    bound = jnp.int32(0)
    for half in range(2):
        for n in range(3):
            bound = bound + length_ref[0, half, n]
            begin = jnp.where(query >= bound, bound, begin)
    mask[...] = jnp.where((key >= begin) & (key <= query), 0.0, NEGATIVE)

    @pl.when(zz == 0)
    def _():
        window[:, pl.ds(0, 2 * NX)] = jnp.zeros((2, 2 * NX, TOK, PIECE), bf16)

    @pl.when(zz == 1)
    def _():
        window[:, pl.ds(0, NX)] = jnp.zeros((2, NX, TOK, PIECE), bf16)

    def z_copy(n, plane):
        return remote(
            window.at[n, plane * NX + x],
            window.at[n, (plane - 1) * NX + x],
            z_ss.at[n, plane],
            z_rs.at[n, plane],
            (me, (seq + NX) % (NX * NZ)),
        )

    def x_copy(n, plane, d, came=False):
        at = plane * NX + ((x + NX - d) % NX if came else x)
        return remote(
            window.at[n, at],
            window.at[n, at],
            x_ss.at[n, plane, d],
            x_rs.at[n, plane, d],
            (me, z * NX + (x + d) % NX),
        )

    def start_x(n, plane, d):
        x_copy(n, plane, d).start()

    def sent_x(n, plane, d):
        x_copy(n, plane, d).wait_send()

    def came_x(n, plane, d):
        x_copy(n, plane, d, True).wait_recv()

    def each_x(n, plane, act, steps):
        for d in steps:
            wraps = x - d < 0 if act is came_x else x + d >= NX
            if plane == 1:
                act(n, plane, d)
            else:
                pl.when(wraps if plane == 0 else jnp.logical_not(wraps))(
                    functools.partial(act, n, plane, d)
                )

    beside = (1, NX - 1)
    inner = (x == 1) | (x == 2)

    def pass_on(n, plane, way, slot):
        at = plane * NX + (x + NX - way) % NX
        return remote(
            window.at[n, at],
            window.at[n, at],
            x_ss.at[n, plane, slot],
            x_rs.at[n, plane, 2],
            (me, z * NX + (x + NX + way) % NX),
        )

    def each_pass(n, plane, act):
        if plane == 1:

            @pl.when(jnp.logical_not(inner))
            def _():
                act(pass_on(n, plane, 1, 0))
                act(pass_on(n, plane, -1, 2))

        else:

            @pl.when(inner)
            def _():
                act(pass_on(n, plane, 1 if plane == 2 else -1, 2))

    def forward(n, plane):
        def go():
            each_x(n, plane, came_x, beside)
            each_pass(n, plane, lambda copy: copy.start())

        if plane == 2:
            go()
        else:
            pl.when(has_last if plane == 1 else zz >= 2)(go)

    def place_pairs(n):
        window[n, 2 * NX + x] = contract(
            put, recvs[n][:, :, :PIECE].reshape(SLOTS, PIECE), ((1,), (0,))
        ).astype(bf16)

        @pl.when(has_next)
        def _():
            z_copy(n, 2).start()

        each_x(n, 2, start_x, beside)

    def one_back(n):
        @pl.when(has_last)
        def _():
            z_copy(n, 2).wait_recv()

            @pl.when(has_next)
            def _():
                z_copy(n, 1).start()

            each_x(n, 1, start_x, beside)

    def two_back(n):
        @pl.when(zz >= 2)
        def _():
            z_copy(n, 1).wait_recv()
            each_x(n, 0, start_x, beside)

    def flag_x_copy(d, came=False):
        at = (x + NX - d) % NX if came else x
        return remote(
            flag_x.at[at],
            flag_x.at[at],
            fx_ss.at[d],
            fx_rs.at[d],
            (me, z * NX + (x + d) % NX),
        )

    def flag_z_copy(d, came=False):
        at = (z + NZ - d) % NZ if came else z
        return remote(
            flag_z.at[at],
            flag_z.at[at],
            fz_ss.at[d],
            fz_rs.at[d],
            (me, (z + d) % NZ * NX + x),
        )

    def pairs_came(n):
        @pl.loop(1, GROUPS)
        def _(d):
            kv_copy(n, d).wait_recv()

    pairs_came(0)
    marks_in = kva_recv[:, :, PIECE:].astype(f32)
    column = lax.broadcasted_iota(jnp.int32, (GROUPS, CAP, TOK), 2).astype(f32) + 1.0
    match = (marks_in == column).astype(f32)
    put = match.reshape(SLOTS, TOK).T.astype(bf16)
    place_pairs(0)
    worst = jnp.max((marks_in < 0.0).astype(f32).reshape(SLOTS, TOK), axis=0, keepdims=True)
    flag_x[x] = jnp.broadcast_to(worst, (CAP, TOK)).astype(bf16)
    for d in range(1, NX):
        flag_x_copy(d).start()
    put_low = both_halves(match[:, :LOW]).T.astype(bf16)

    ring_turn(2)
    start_queries(0)
    forward(0, 2)
    one_back(0)
    ring_turn(3)
    start_queries(1)
    pairs_came(1)
    place_pairs(1)
    for d in range(1, NX):
        flag_x_copy(d, True).wait_recv()
    flag_z[z] = jnp.max(flag_x[...].astype(f32), axis=0).astype(bf16)
    for d in range(1, NZ):
        flag_z_copy(d).start()
    two_back(0)
    start_queries(2)
    forward(0, 1)
    one_back(1)
    forward(1, 2)
    start_queries(3)
    ring_turn(4)
    two_back(1)
    forward(0, 0)
    for n in range(NY):
        sibling_came(n)

    tags_in = over[:, :, HK * HALF_WIDE :].astype(f32)
    mine = (me + 1).astype(f32)
    match_over = ((tags_in[:, :OVER] == column[:, :OVER]) & (tags_in[:, OVER:] == mine)).astype(f32)
    put_over = both_halves(match_over).T.astype(bf16)

    ones = jnp.ones((SPAN, HD), bf16)

    def window_came(n):
        each_x(n, 2, came_x, (2,))

        @pl.when(has_last)
        def _():
            each_x(n, 1, came_x, (2,))

        @pl.when(zz >= 2)
        def _():
            each_x(n, 0, came_x, (2,))

    @pl.loop(0, HK)
    def _(j):
        @pl.when(j == 0)
        def _():
            window_came(0)

        @pl.when(j == 1)
        def _():
            forward(1, 1)
            forward(1, 0)

        @pl.when(j == 2)
        def _():
            window_came(1)

        @pl.loop(1, GROUPS)
        def _(d):
            q_copy(j, d).wait_recv()

        cols = pl.ds(pl.multiple_of(j * HALF_WIDE, HALF_WIDE), HALF_WIDE)
        rows = contract(put_low, q_recv[j].reshape(SLOTS, HALF_WIDE), ((1,), (0,)))
        rows = rows + contract(put_over, over[:, :, cols].reshape(SLOTS, HALF_WIDE), ((1,), (0,)))
        rows = rows.astype(bf16)
        for h in range(HQ // HK):
            half, at = h // (HQ // HK // 2), h % (HQ // HK // 2)
            placed[h] = rows[half * TOK : (half + 1) * TOK, at * HD : (at + 1) * HD]
        key_cols = pl.ds(pl.multiple_of(j % 2 * HD, HD), HD)
        value_cols = pl.ds(pl.multiple_of(PIECE // 2 + j % 2 * HD, HD), HD)
        for h in range(HQ // HK):
            keys = window[j // 2, pl.ds(x, BACK + 1), :, key_cols].reshape(SPAN, HD)
            values = window[j // 2, pl.ds(x, BACK + 1), :, value_cols].reshape(SPAN, HD)
            scores = contract(placed[h], keys, ((1,), (1,))) + mask[...]
            top = jnp.max(scores, axis=1, keepdims=True)
            weights = jnp.exp2((scores - top) * FACTOR).astype(bf16)
            summed = contract(weights, jnp.concatenate([values, ones], axis=1), ((1,), (0,)))
            head_cols = pl.ds(pl.multiple_of((j * (HQ // HK) + h) * HD, HD), HD)
            out_ref[0, :, head_cols] = (summed[:, :HD] / summed[:, HD:]).astype(bf16)


    for d in range(1, NZ):
        flag_z_copy(d, True).wait_recv()
    flag_ref[0, 0] = jnp.max(flag_z[...].astype(f32)).astype(jnp.int32)

    @pl.loop(1, GROUPS)
    def _(d):
        for n in range(2):
            kv_copy(n, d).wait_send()
        for j in range(HK):
            q_copy(j, d).wait_send()

    for n in range(2):
        each_x(n, 2, sent_x, beside)
        each_pass(n, 2, lambda copy: copy.wait_send())

        @pl.when(has_next)
        def _(n=n):
            z_copy(n, 2).wait_send()

        @pl.when(has_last)
        def _(n=n):
            each_x(n, 1, sent_x, beside)
            each_pass(n, 1, lambda copy: copy.wait_send())

            @pl.when(has_next)
            def _():
                z_copy(n, 1).wait_send()

        @pl.when(zz >= 2)
        def _(n=n):
            each_x(n, 0, sent_x, beside)
            each_pass(n, 0, lambda copy: copy.wait_send())

    for step in range(1, NY // 2 + 1):
        ring(step, 0).wait_send()
        if step < NY // 2:
            ring(step, 1).wait_send()
    for n in range(NY):
        sibling(n).wait_send()
    for d in range(1, NX):
        flag_x_copy(d).wait_send()
    for d in range(1, NZ):
        flag_z_copy(d).wait_send()


def compact(*operands):
    bf16 = jnp.bfloat16
    dma = pltpu.SemaphoreType.DMA
    vmem = pltpu.VMEM
    return pl.pallas_call(
        compact_kernel,
        out_shape=(
            pltpu.VMEM((1, TOK, HQ * HD), bf16),
            jax.ShapeDtypeStruct((1, 1), jnp.int32),
        ),
        in_specs=[pl.BlockSpec(memory_space=pltpu.HBM)] * 5,
        out_specs=(pl.BlockSpec(memory_space=pltpu.VMEM), pl.BlockSpec(memory_space=pltpu.SMEM)),
        scratch_shapes=[
            vmem((2 * HK, TOK, HALF_WIDE), bf16),
            vmem((1, TOK, PAIR), bf16),
            vmem((1, TOK), jnp.int32),
            vmem((1, TOK), jnp.int32),
            pltpu.SMEM((1, 2, 3), jnp.int32),
            vmem((HK, GROUPS, CAP, HALF_WIDE), bf16),
            vmem((HK, GROUPS, CAP, HALF_WIDE), bf16),
            vmem((GROUPS, CAP, PIECE + TOK), bf16),
            vmem((GROUPS, CAP, PIECE + TOK), bf16),
            vmem((GROUPS, CAP, PIECE), bf16),
            vmem((GROUPS, CAP, PIECE), bf16),
            vmem((GROUPS, CAP, HK * HALF_WIDE + TOK), bf16),
            vmem((2, 3 * NX, TOK, PIECE), bf16),
            vmem((TOK, SPAN), jnp.float32),
            vmem((HQ // HK, TOK, HD), bf16),
            vmem((NX, CAP, TOK), bf16),
            vmem((NZ, CAP, TOK), bf16),
            dma((2 * HK + 4,)),
            dma((HK, GROUPS)),
            dma((HK, GROUPS)),
            dma((2, GROUPS)),
            dma((2, GROUPS)),
            dma((2, NY // 2 + 1)),
            dma((2, NY // 2 + 1)),
            dma((NY,)),
            dma((NY,)),
            dma((2, 3)),
            dma((2, 3)),
            dma((2, 3, NX)),
            dma((2, 3, NX)),
            dma((NX,)),
            dma((NX,)),
            dma((NZ,)),
            dma((NZ,)),
        ],
        compiler_params=pltpu.CompilerParams(
            collective_id=1, has_side_effects=True, vmem_limit_bytes=48 << 20
        ),
    )(*operands)


def local(*operands):
    operands = [pltpu.with_memory_space_constraint(one, pltpu.HBM) for one in operands]
    result, crowded = compact(*operands)
    return lax.switch(crowded[0, 0], [lambda: result, lambda: padded(*operands)])


def solution(mesh):
    return jax.shard_map(
        local,
        mesh=mesh,
        in_specs=(
            P("grp", "seq", None),
            P("grp", "seq", None),
            P("grp", "seq"),
            P("grp", "seq"),
            P("grp", None, None),
        ),
        out_specs=P("grp", "seq", None),
        check_vma=False,
    )
```
